32 devices in a mesh: freq: 4 (over x, core), span: 4 (over z), wall: 2 (over y).
Axes of the slice: x: 2, y: 2, z: 4, core: 2. Of those that a mesh axis runs over, the one named last changes fastest.
Arguments:
- amplitudes: float32 [2, 5, 128, 32768], P(None, None, 'wall', ('freq', 'span')), may hold values from -20 to 20
- upstream: float32 [2, 5, 128, 32768], P(None, None, 'wall', ('freq', 'span')), may hold values from -6 to 6
- harmonic_mask: int32 [32768], P(('freq', 'span')), may hold values 0 or 1
- quadratic_coefficients: float32 [5, 5, 5], replicated, may hold values from -1.25 to 1.25
- slab_inverse: float32 [2, 320, 320], P('wall'), may hold values from -1 to 2
- lower_coupling: float32 [2, 5, 5], P('wall'), may hold values from -2.5 to 2.5
- upper_coupling: float32 [2, 5, 5], P('wall'), may hold values from -2.5 to 2.5
- reduced_lower: float32 [2, 10, 10], P('wall'), may hold values from -1 to 1
- reduced_upper: float32 [2, 10, 10], P('wall'), may hold values from -1 to 1
- reduced_pivot: float32 [2, 10, 10], P('wall'), may hold values from -2 to 3
Outputs:
- new_amplitudes: float32 [2, 5, 128, 32768], P(None, None, 'wall', ('freq', 'span'))
- wavenumber_shift: float32 [2, 32768], P(None, ('freq', 'span'))
The draws below stay inside these ranges and needn't reach their ends.
Inputs may be any that keep to these rules, and one draw needn't show every extreme that they name: `harmonic_mask`: 1 marks a retained mode.
All inputs are finite; a program needn't handle non-finite values. No bound on the sum of `harmonic_mask` on one device may be relied on, other than what follows from the above.
Results may differ from the reference program's by a relative error of at most 0.0001.
Values sent between devices are 32-bit elements; how exact they have to be, the bound alone decides.
No kernel may reach another device: no remote copies, remote signals or barrier semaphores. Data moves between devices by JAX's collectives and lax.ppermute only.
A program may use at most 64 MiB of HBM per device.

```python
import math
import jax
import jax.numpy as jnp
from jax import lax

V = 5
NF = 128
NB = 256
CY = 64
NY = 128
NM = 32768
N_WALL = 2


def draw_amplitudes(key, part):
    key_rough, key_level = jax.random.split(key, 2)
    levels = jnp.exp(jax.random.uniform(key_level, (1, 1, 1, NF * NB), jnp.float32, math.log(0.3), math.log(3.0)))
    height = 0.5 + jnp.arange(NY, dtype=jnp.float32) / NY
    profile = height[None, None, :, None]
    values = jax.random.normal(key_rough, (2, V, NY, NF * NB), jnp.float32)
    return jnp.clip(values * levels * profile, -20.0, 20.0)


def draw_slab_inverse(key, part):
    extent = V * CY
    noise = jax.random.normal(key, (N_WALL, extent, extent), jnp.float32)
    return jnp.clip(jnp.eye(extent, dtype=jnp.float32)[None] + 0.7 * noise / math.sqrt(extent), -1.0, 2.0)


def draw_reduced_pivot(key, part):
    extent = 2 * V
    noise = jax.random.normal(key, (N_WALL, extent, extent), jnp.float32)
    return jnp.clip(jnp.eye(extent, dtype=jnp.float32)[None] + 0.35 * noise / math.sqrt(extent), -2.0, 3.0)


def touch_ends(values, rng, least, high):
    index_at = [jax.random.randint(jax.random.fold_in(rng, axis), (), 0, length) for axis, length in enumerate(values.shape)]
    widest = values.shape.index(max(values.shape))
    beside = index_at[:widest] + [(index_at[widest] + 1) % values.shape[widest]] + index_at[widest + 1:]
    return values.at[tuple(index_at)].set(least).at[tuple(beside)].set(high)


def level_of(rng, dims, shards, least, largest):
    factor_of = 1.0
    for dim, parts in shards:
        draws = jax.random.uniform(jax.random.fold_in(jax.random.fold_in(rng, 6), dim), (parts,), jnp.float32, least / len(shards), largest / len(shards))
        factor_of = factor_of * jnp.repeat(jnp.exp(draws), dims[dim] // parts).reshape((-1,) + (1,) * (len(dims) - 1 - dim))
    return factor_of


def bell_draw(own_key, dims, width, reach, cuts=(), kind=jnp.bfloat16):
    factor_of = level_of(own_key, dims, cuts, -0.22, 0.18) if cuts else 1.0
    result = jax.random.normal(own_key, dims, jnp.float32) * width * factor_of
    return jnp.minimum(jnp.maximum(result, -reach), reach).astype(kind)


def setup_inputs(seed: int = 0) -> dict:
    seeds = jax.random.split(jax.random.key(seed), 11)
    amplitudes = draw_amplitudes(jax.random.fold_in(seeds[10], 71), 0)
    upstream = bell_draw(seeds[1], (2, V, NY, NM), 1.0, 6.0, ((2, 2), (3, 16)), jnp.float32)
    harmonic_mask = touch_ends((jax.random.randint(seeds[2], (NM,), 0, 4) < 3).astype(jnp.int32), jax.random.fold_in(seeds[2], 1), 0, 1)
    quadratic_coefficients = bell_draw(seeds[3], (V, V, V), (V * V) ** -0.5, 1.25, (), jnp.float32)
    slab_inverse = draw_slab_inverse(jax.random.fold_in(seeds[10], 71), 0)
    lower_coupling = bell_draw(seeds[5], (N_WALL, V, V), V ** -0.5, 2.5, ((0, 2),), jnp.float32)
    upper_coupling = bell_draw(seeds[6], (N_WALL, V, V), V ** -0.5, 2.5, ((0, 2),), jnp.float32)
    reduced_lower = bell_draw(seeds[7], (N_WALL, 2 * V, 2 * V), (6 * V) ** -0.5, 1.0, ((0, 2),), jnp.float32)
    reduced_upper = bell_draw(seeds[8], (N_WALL, 2 * V, 2 * V), (6 * V) ** -0.5, 1.0, ((0, 2),), jnp.float32)
    reduced_pivot = draw_reduced_pivot(jax.random.fold_in(seeds[10], 71), 0)
    return dict(amplitudes=amplitudes, upstream=upstream, harmonic_mask=harmonic_mask, quadratic_coefficients=quadratic_coefficients, slab_inverse=slab_inverse, lower_coupling=lower_coupling, upper_coupling=upper_coupling, reduced_lower=reduced_lower, reduced_upper=reduced_upper, reduced_pivot=reduced_pivot)


epsilon = 1e-06

def apply_left(matrix, vectors):
    return jnp.einsum('ij,cjm->cim', matrix, vectors, precision=lax.Precision.HIGHEST)

def quadratic(field, coefficients):
    weights = coefficients * (1.0 - jnp.eye(coefficients.shape[0], dtype=jnp.float32))[None]
    total = jnp.zeros_like(field)
    for source_var in range(field.shape[0]):
        mixed = jnp.einsum('wb,bynt->wynt', weights[:, source_var, :], field, precision=lax.Precision.HIGHEST)
        total = total + field[source_var][None] * mixed
    return total

def reference(amplitudes, upstream, harmonic_mask, quadratic_coefficients, slab_inverse, lower_coupling, upper_coupling, reduced_lower, reduced_upper, reduced_pivot):
    keep = harmonic_mask.astype(jnp.float32)
    kept = amplitudes * keep
    scale = 1.0 / math.sqrt(NF * NB)

    def slab_solve(items):
        block, source, inverse = items
        spectrum = lax.complex(block[0], block[1]).reshape(V, CY, NF, NB)
        field = jnp.real(jnp.fft.ifft2(spectrum, axes=(2, 3))) * (NF * NB * scale)
        forcing = jnp.fft.fft2(quadratic(field, quadratic_coefficients), axes=(2, 3)) * scale
        forcing = forcing.reshape(V, CY, NF * NB)
        right_side = (jnp.stack([jnp.real(forcing), jnp.imag(forcing)]) + source) * keep
        flat = right_side.reshape(2, V * CY, NF * NB)
        solved = jnp.einsum('ij,cjm->cim', inverse, flat, precision=lax.Precision.HIGHEST)
        return solved.reshape(2, V, CY, NF * NB)

    def slabs(array):
        return jnp.moveaxis(array.reshape(2, V, N_WALL, CY, NF * NB), 2, 0)
    solved = lax.map(slab_solve, (slabs(kept), slabs(upstream), slab_inverse))
    bounds = jnp.concatenate([solved[:, :, :, 0], solved[:, :, :, CY - 1]], axis=2)
    zeros = jnp.zeros_like(bounds[0])
    ahead = []
    carried = zeros
    for wall_index in range(N_WALL):
        carried = bounds[wall_index] - apply_left(reduced_lower[wall_index], carried)
        ahead.append(carried)
    interface = [zeros] * N_WALL
    carried = zeros
    for wall_index in range(N_WALL - 1, -1, -1):
        carried = apply_left(reduced_pivot[wall_index], ahead[wall_index] - apply_left(reduced_upper[wall_index], carried))
        interface[wall_index] = carried
    pieces = []
    for wall_index in range(N_WALL):
        below = interface[wall_index - 1][:, V:] if wall_index > 0 else zeros[:, V:]
        above = interface[wall_index + 1][:, :V] if wall_index < N_WALL - 1 else zeros[:, :V]
        columns = slab_inverse[wall_index].reshape(V * CY, V, CY)
        pushed = apply_left(columns[:, :, 0], apply_left(lower_coupling[wall_index], below))
        pushed = pushed + apply_left(columns[:, :, CY - 1], apply_left(upper_coupling[wall_index], above))
        pieces.append(solved[wall_index] - pushed.reshape(2, V, CY, NF * NB))
    new_amplitudes = jnp.concatenate(pieces, axis=2)
    change = new_amplitudes - kept
    real_part = lax.optimization_barrier(jnp.sum(kept[0] * change[0] + kept[1] * change[1], axis=(0, 1)))
    imag_part = lax.optimization_barrier(jnp.sum(kept[0] * change[1] - kept[1] * change[0], axis=(0, 1)))
    weight = lax.optimization_barrier(jnp.sum(kept * kept, axis=(0, 1, 2))) + epsilon
    wavenumber_shift = jnp.stack([imag_part / weight, -real_part / weight])
    return (new_amplitudes, wavenumber_shift)
```

```python
import functools
import math

import jax
import jax.numpy as jnp
import numpy as np
from jax import lax
from jax.experimental import pallas as pl
from jax.experimental.pallas import tpu as pltpu
from jax.sharding import PartitionSpec as P

NF = 128
NB = 256

epsilon = 1e-06

SPLIT = lax.Precision.HIGH
FULL = lax.Precision.HIGHEST
GATHERED_ROWS = 24


def tables():
    def turns(length):
        counter = np.arange(length)
        angles = (counter[:, None] * counter[None, :] % length) * (2.0 * math.pi / length)
        return np.cos(angles), np.sin(angles)

    cos_time, sin_time = turns(NF)
    cos_span, sin_span = turns(NB)
    scale = 1.0 / math.sqrt(NF * NB)
    out = (
        np.block([[cos_time, -sin_time], [sin_time, cos_time]]),
        np.concatenate([cos_span, -sin_span], 0) * scale,
        np.concatenate([cos_span, -sin_span], 1) * scale,
        np.block([[cos_time, sin_time], [-sin_time, cos_time]]),
    )
    return [jnp.asarray(table.astype(np.float32)) for table in out]


def params(megabytes=40):
    return pltpu.CompilerParams(vmem_limit_bytes=megabytes * 1024 * 1024)


def whole(array):
    zeros = (0,) * array.ndim
    return pl.BlockSpec(array.shape, lambda *_: zeros)


def prepare_body(x_ref, mask_ref, out_ref):
    keep = mask_ref[...]
    rows, _, freqs, _ = out_ref.shape
    for part in range(2):
        kept = x_ref[part, 0] * keep
        out_ref[:, 0, :, part * NB : (part + 1) * NB] = kept.reshape(rows, freqs, NB)


def prepare(amplitudes, keep, start, rows):
    _, variables, _, modes = amplitudes.shape
    freqs = modes // NB
    at = start // rows
    return pl.pallas_call(
        prepare_body,
        grid=(variables,),
        in_specs=[
            pl.BlockSpec((2, 1, rows, modes), lambda v: (0, v, at, 0)),
            pl.BlockSpec((1, modes), lambda v: (0, 0)),
        ],
        out_specs=pl.BlockSpec((rows, 1, freqs, 2 * NB), lambda v: (0, v, 0, 0)),
        out_shape=jax.ShapeDtypeStruct((rows, variables, freqs, 2 * NB), jnp.float32),
        compiler_params=params(),
        name="prepare",
    )(amplitudes, keep)


def nonlinear_body(q_ref, in_ref, wi_ref, ei_ref, ef_ref, wf_ref, out_ref, field_ref, force_ref):
    devices, _, variables, freqs, _ = in_ref.shape
    for v in range(variables):
        modes = in_ref[:, 0, v].reshape(NF, 2 * NB)
        stacked = jnp.concatenate([modes[:, :NB], modes[:, NB:]], axis=0)
        turned = jnp.dot(
            wi_ref[...], stacked, precision=SPLIT, preferred_element_type=jnp.float32
        )
        beside = jnp.concatenate([turned[:NF], turned[NF:]], axis=1)
        field_ref[v] = jnp.dot(
            beside, ei_ref[...], precision=SPLIT, preferred_element_type=jnp.float32
        )
    pairs = [(a, b) for a in range(variables) for b in range(a + 1, variables)]
    weights = [
        [q_ref[w * variables + a, b] + q_ref[w * variables + b, a] for a, b in pairs]
        for w in range(variables)
    ]
    step = 8
    for row in range(0, NF, step):
        at = slice(row, row + step)
        values = [field_ref[v, at] for v in range(variables)]
        total = [None] * variables
        for i, (a, b) in enumerate(pairs):
            product = values[a] * values[b]
            for w in range(variables):
                term = weights[w][i] * product
                total[w] = term if total[w] is None else total[w] + term
        for w in range(variables):
            force_ref[w, at] = total[w]
    for w in range(variables):
        spread = jnp.dot(
            force_ref[w], ef_ref[...], precision=SPLIT, preferred_element_type=jnp.float32
        )
        stacked = jnp.concatenate([spread[:, :NB], spread[:, NB:]], axis=0)
        turned = jnp.dot(
            wf_ref[...], stacked, precision=SPLIT, preferred_element_type=jnp.float32
        )
        for part in range(2):
            piece = turned[part * NF : (part + 1) * NF]
            out_ref[:, 0, w, :, part * NB : (part + 1) * NB] = piece.reshape(devices, freqs, NB)


def nonlinear(block, coefficients, transforms):
    devices, points, variables, freqs, lanes = block.shape
    spec = pl.BlockSpec((devices, 1, variables, freqs, lanes), lambda j: (0, j, 0, 0, 0))
    flops = points * variables * 12 * NF * NB * (NF + NB) * 2
    return pl.pallas_call(
        nonlinear_body,
        grid=(points,),
        in_specs=[pl.BlockSpec(memory_space=pltpu.SMEM), spec] + [whole(t) for t in transforms],
        out_specs=spec,
        out_shape=jax.ShapeDtypeStruct(block.shape, jnp.float32),
        scratch_shapes=[pltpu.VMEM((variables, NF, NB), jnp.float32)] * 2,
        compiler_params=params(),
        cost_estimate=pl.CostEstimate(
            flops=flops, bytes_accessed=2 * block.size * 4, transcendentals=0
        ),
        name="nonlinear",
    )(coefficients, block, *transforms)


def adjoint_body(x_ref, mask_ref, inverse_ref, out_ref, edge_ref):
    _, variables, heights, lanes = x_ref.shape
    extent = variables * heights
    keep = mask_ref[...]
    weight = jnp.zeros((1, lanes), jnp.float32)
    for part in range(2):
        kept = x_ref[part].reshape(extent, lanes) * keep
        weight = weight + jnp.sum(kept * kept, axis=0, keepdims=True)
        moved = jnp.dot(
            inverse_ref[...], kept, precision=SPLIT, preferred_element_type=jnp.float32
        )
        out_ref[part] = moved.reshape(variables, heights, lanes)
        for end, point in enumerate((0, heights - 1)):
            for v in range(variables):
                row = part * 2 * variables + end * variables + v
                at = v * heights + point
                edge_ref[row : row + 1] = moved[at : at + 1]
    last = 4 * variables
    edge_ref[last : last + 1] = weight
    edge_ref[last + 1 :] = jnp.zeros((GATHERED_ROWS - last - 1, lanes), jnp.float32)


def adjoint(amplitudes, keep, inverse_t):
    _, variables, heights, modes = amplitudes.shape
    spec = pl.BlockSpec((2, variables, heights, NB), lambda i: (0, 0, 0, i))
    return pl.pallas_call(
        adjoint_body,
        grid=(modes // NB,),
        in_specs=[spec, pl.BlockSpec((1, NB), lambda i: (0, i)), whole(inverse_t)],
        out_specs=[spec, pl.BlockSpec((GATHERED_ROWS, NB), lambda i: (0, i))],
        out_shape=[
            jax.ShapeDtypeStruct(amplitudes.shape, jnp.float32),
            jax.ShapeDtypeStruct((GATHERED_ROWS, modes), jnp.float32),
        ],
        compiler_params=params(),
        name="adjoint",
    )(amplitudes, keep, inverse_t)


def absorb_body(first, *refs):
    if first:
        in_ref, up_ref, mask_ref, edge_ref, adj_ref, out_ref, sum_ref = refs
    else:
        in_ref, up_ref, mask_ref, edge_ref, adj_ref, before_ref, out_ref, sum_ref = refs
    rows, _, freqs, _ = in_ref.shape
    ends = edge_ref.shape[1]
    keep = mask_ref[...]

    @pl.when(pl.program_id(0) == 0)
    def _():
        if first:
            sum_ref[...] = jnp.zeros(sum_ref.shape, jnp.float32)
        else:
            sum_ref[...] = before_ref[...]

    sides = []
    for part in range(2):
        forced = in_ref[:, 0, :, part * NB : (part + 1) * NB].reshape(rows, freqs * NB)
        side = (forced + up_ref[part, 0]) * keep
        out_ref[part, 0] = side
        at = slice(part * ends, (part + 1) * ends)
        sum_ref[at] += jnp.dot(
            edge_ref[0], side, precision=SPLIT, preferred_element_type=jnp.float32
        )
        sides.append(side)
    real, imag = adj_ref[0, 0], adj_ref[1, 0]
    at = 2 * ends
    sum_ref[at : at + 1] += jnp.sum(real * sides[0] + imag * sides[1], axis=0, keepdims=True)
    sum_ref[at + 1 : at + 2] += jnp.sum(real * sides[1] - imag * sides[0], axis=0, keepdims=True)


def absorb(block, upstream, keep, edges, adjoint_modes, before, start):
    rows, variables, freqs, lanes = block.shape
    modes = keep.shape[1]
    at = start // rows
    ends = edges.shape[1]
    grid_spec = pl.BlockSpec((2, 1, rows, modes), lambda v: (0, v, at, 0))
    sums = pl.BlockSpec((GATHERED_ROWS, modes), lambda v: (0, 0))
    operands = [block, upstream, keep, edges, adjoint_modes]
    in_specs = [
        pl.BlockSpec((rows, 1, freqs, lanes), lambda v: (0, v, 0, 0)),
        grid_spec,
        pl.BlockSpec((1, modes), lambda v: (0, 0)),
        pl.BlockSpec((1, ends, rows), lambda v: (v, 0, 0)),
        grid_spec,
    ]
    if before is not None:
        operands.append(before)
        in_specs.append(sums)
    return pl.pallas_call(
        functools.partial(absorb_body, before is None),
        grid=(variables,),
        in_specs=in_specs,
        out_specs=[pl.BlockSpec((2, 1, rows, modes), lambda v: (0, v, 0, 0)), sums],
        out_shape=[
            jax.ShapeDtypeStruct((2, variables, rows, modes), jnp.float32),
            jax.ShapeDtypeStruct((GATHERED_ROWS, modes), jnp.float32),
        ],
        compiler_params=params(),
        name="absorb",
    )(*operands)


def finish_body(chunks, walls, *refs):
    sides, refs = refs[:chunks], refs[chunks:]
    bounds, refs = refs[:walls], refs[walls:]
    edges, refs = refs[:walls], refs[walls:]
    solve_ref, chain_ref, out_ref, shift_ref = refs
    _, variables, heights, lanes = out_ref.shape
    ends = 2 * variables
    pushed = []
    for part in range(2):
        at = slice(part * ends, (part + 1) * ends)
        everywhere = jnp.concatenate([ref[at] for ref in bounds], axis=0)
        pushed.append(
            jnp.dot(
                chain_ref[...], everywhere, precision=FULL, preferred_element_type=jnp.float32
            )
        )
        stacked = [ref[part].reshape(-1, lanes) for ref in sides]
        stacked = jnp.concatenate(stacked + [pushed[part][:ends]], axis=0)
        moved = jnp.dot(
            solve_ref[...], stacked, precision=SPLIT, preferred_element_type=jnp.float32
        )
        out_ref[part] = moved.reshape(variables, heights, lanes)
    real = imag = weight = 0.0
    for wall in range(walls):
        at = slice(wall * ends, (wall + 1) * ends)
        push = [pushed[part][at] for part in range(2)]
        edge = [edges[wall][part * ends : (part + 1) * ends] for part in range(2)]
        row = 2 * ends
        squares = edges[wall][row : row + 1]
        taken = jnp.sum(edge[0] * push[0] + edge[1] * push[1], axis=0, keepdims=True)
        real = real + (bounds[wall][row : row + 1] - taken - squares)
        taken = jnp.sum(edge[0] * push[1] - edge[1] * push[0], axis=0, keepdims=True)
        imag = imag + (bounds[wall][row + 1 : row + 2] - taken)
        weight = weight + squares
    weight = weight + epsilon
    shift_ref[0:1] = imag / weight
    shift_ref[1:2] = -real / weight


def finish(sides, bounds, edges, solve, chain, heights):
    _, variables, _, modes = sides[0].shape
    walls = len(bounds)
    small = pl.BlockSpec((GATHERED_ROWS, NB), lambda i: (0, i))
    return pl.pallas_call(
        functools.partial(finish_body, len(sides), walls),
        grid=(modes // NB,),
        in_specs=[
            pl.BlockSpec((2, variables, side.shape[2], NB), lambda i: (0, 0, 0, i))
            for side in sides
        ]
        + [small] * (2 * walls)
        + [whole(solve), whole(chain)],
        out_specs=[
            pl.BlockSpec((2, variables, heights, NB), lambda i: (0, 0, 0, i)),
            pl.BlockSpec((2, NB), lambda i: (0, i)),
        ],
        out_shape=[
            jax.ShapeDtypeStruct((2, variables, heights, modes), jnp.float32),
            jax.ShapeDtypeStruct((2, modes), jnp.float32),
        ],
        compiler_params=params(),
        name="finish",
    )(*sides, *bounds, *edges, solve, chain)


def around(block, axis):
    count = lax.axis_size(axis)
    return [block] + [
        lax.ppermute(block, axis, [(i, (i + d) % count) for i in range(count)])
        for d in range(1, count)
    ]


def interface_chain(lower_coupling, upper_coupling, reduced_lower, reduced_upper, reduced_pivot):
    gathered = [
        lax.all_gather(part[0], "wall")
        for part in (lower_coupling, upper_coupling, reduced_lower, reduced_upper, reduced_pivot)
    ]
    low, up, red_low, red_up, pivot = gathered
    walls = low.shape[0]
    ends = red_low.shape[1]
    half = ends // 2
    dot = functools.partial(jnp.dot, precision=FULL)
    units = jnp.eye(walls * ends, dtype=jnp.float32).reshape(walls, ends, walls * ends)
    ahead = [units[0]]
    for j in range(1, walls):
        ahead.append(units[j] - dot(red_low[j], ahead[j - 1]))
    interface = [None] * walls
    interface[-1] = dot(pivot[-1], ahead[-1])
    for j in range(walls - 2, -1, -1):
        interface[j] = dot(pivot[j], ahead[j] - dot(red_up[j], interface[j + 1]))
    none = jnp.zeros((half, walls * ends), jnp.float32)
    rows = []
    for j in range(walls):
        rows.append(dot(low[j], interface[j - 1][half:]) if j > 0 else none)
        rows.append(dot(up[j], interface[j + 1][:half]) if j < walls - 1 else none)
    chain = jnp.concatenate(rows, axis=0).reshape(walls, ends, walls, ends)
    order = (lax.axis_index("wall") - jnp.arange(walls)) % walls
    chain = jnp.take(jnp.take(chain, order, axis=0), order, axis=2)
    return chain.reshape(walls * ends, walls * ends)


def local(
    amplitudes,
    upstream,
    harmonic_mask,
    quadratic_coefficients,
    slab_inverse,
    lower_coupling,
    upper_coupling,
    reduced_lower,
    reduced_upper,
    reduced_pivot,
):
    _, variables, heights, modes = amplitudes.shape
    freqs = modes // NB
    extent = variables * heights
    axes = ("freq", "span")
    devices = lax.axis_size("freq") * lax.axis_size("span")
    points = heights // devices
    sizes = [points // 2, points // 2] if points % 2 == 0 else [points]
    starts = [devices * sum(sizes[:i]) for i in range(len(sizes))]
    transforms = tables()
    keep = harmonic_mask.astype(jnp.float32).reshape(1, modes)
    coefficients = quadratic_coefficients.reshape(variables * variables, variables)

    def exchange(block):
        return lax.all_to_all(block, axes, split_axis=0, concat_axis=0, tiled=True)

    arrived = []
    for start, size in zip(starts, sizes):
        arrived.append(exchange(prepare(amplitudes, keep, start, devices * size)))

    inverse = slab_inverse[0]
    columns = inverse.reshape(extent, variables, heights)
    end_rows = inverse.reshape(variables, heights, variables, heights)
    end_rows = jnp.concatenate([end_rows[:, 0], end_rows[:, heights - 1]], axis=0)
    end_rows = jnp.swapaxes(end_rows, 0, 1)
    end_columns = jnp.concatenate([columns[:, :, 0], columns[:, :, heights - 1]], axis=1)
    cuts = [slice(start, start + devices * size) for start, size in zip(starts, sizes)]
    solve = jnp.concatenate(
        [columns[:, :, cut].reshape(extent, -1) for cut in cuts] + [-end_columns], axis=1
    )
    adjoint_modes, edge = adjoint(amplitudes, keep, inverse.T)
    edges = around(edge, "wall")
    chain = interface_chain(
        lower_coupling, upper_coupling, reduced_lower, reduced_upper, reduced_pivot
    )

    returned = []
    for block, size in zip(arrived, sizes):
        shape = block.shape
        forced = nonlinear(block.reshape((devices, size) + shape[1:]), coefficients, transforms)
        returned.append(exchange(forced.reshape(shape)))

    sides = []
    sums = None
    for block, start, cut in zip(returned, starts, cuts):
        side, sums = absorb(
            block, upstream, keep, end_rows[:, :, cut], adjoint_modes, sums, start
        )
        sides.append(side)
    bounds = around(sums, "wall")
    new_amplitudes, wavenumber_shift = finish(sides, bounds, edges, solve, chain, heights)
    return (new_amplitudes, wavenumber_shift)


def solution(mesh):
    placed = (
        P(None, None, "wall", ("freq", "span")),
        P(None, None, "wall", ("freq", "span")),
        P(("freq", "span")),
        P(),
        P("wall", None, None),
        P("wall", None, None),
        P("wall", None, None),
        P("wall", None, None),
        P("wall", None, None),
        P("wall", None, None),
    )
    return jax.shard_map(
        local,
        mesh=mesh,
        in_specs=placed,
        out_specs=(P(None, None, "wall", ("freq", "span")), P(None, ("freq", "span"))),
        check_vma=False,
    )
```

```python
import functools
import math

import jax
import jax.numpy as jnp
import numpy as np
from jax import lax
from jax.experimental import pallas as pl
from jax.experimental.pallas import tpu as pltpu
from jax.sharding import PartitionSpec as P

NF = 128
NB = 256

epsilon = 1e-06

SPLIT = lax.Precision.HIGH
FULL = lax.Precision.HIGHEST
GATHERED_ROWS = 24


def tables():
    def turns(length):
        counter = np.arange(length)
        angles = (counter[:, None] * counter[None, :] % length) * (2.0 * math.pi / length)
        return np.cos(angles), np.sin(angles)

    cos_time, sin_time = turns(NF)
    cos_span, sin_span = turns(NB)
    scale = 1.0 / math.sqrt(NF * NB)
    out = (
        np.block([[cos_time, -sin_time], [sin_time, cos_time]]),
        np.concatenate([cos_span, -sin_span], 0) * scale,
        np.concatenate([cos_span, -sin_span], 1) * scale,
        np.block([[cos_time, sin_time], [-sin_time, cos_time]]),
    )
    return [jnp.asarray(table.astype(np.float32)) for table in out]


def params(megabytes=16):
    return pltpu.CompilerParams(vmem_limit_bytes=megabytes * 1024 * 1024)


def whole(array):
    zeros = (0,) * array.ndim
    return pl.BlockSpec(array.shape, lambda *_: zeros)


def in_hbm(array):
    return pltpu.with_memory_space_constraint(array, pltpu.HBM)


def kept_modes(mask_ref):
    return mask_ref[...].astype(jnp.float32).reshape(1, -1)


def prepare_body(x_ref, mask_ref, out_ref):
    keep = kept_modes(mask_ref)
    rows, _, freqs, _ = out_ref.shape
    for part in range(2):
        kept = x_ref[part, 0] * keep
        out_ref[:, 0, :, part * NB : (part + 1) * NB] = kept.reshape(rows, freqs, NB)


def prepare(amplitudes, keep, cut):
    _, variables, _, modes = amplitudes.shape
    freqs = modes // NB
    rows = cut.stop - cut.start
    at = cut.start // rows
    return pl.pallas_call(
        prepare_body,
        grid=(variables,),
        in_specs=[
            pl.BlockSpec((2, 1, rows, modes), lambda v: (0, v, at, 0)),
            pl.BlockSpec((modes,), lambda v: (0,)),
        ],
        out_specs=pl.BlockSpec((rows, 1, freqs, 2 * NB), lambda v: (0, v, 0, 0)),
        out_shape=pltpu.HBM((rows, variables, freqs, 2 * NB), jnp.float32),
        compiler_params=params(),
        name="prepare",
    )(in_hbm(amplitudes), keep)


def partner(place_ref, j, i, spans):
    return (place_ref[0] ^ j) * spans + (place_ref[1] ^ i)


def prepare_apart_body(place_ref, x_ref, mask_ref, *refs):
    out_refs, rows_ref = refs[:-1], refs[-1]
    keep = kept_modes(mask_ref)
    rows, freqs, _ = rows_ref.shape
    spans = len(out_refs)
    for part in range(2):
        kept = x_ref[part, 0] * keep
        rows_ref[:, :, part * NB : (part + 1) * NB] = kept.reshape(rows, freqs, NB)
    for i, out_ref in enumerate(out_refs):
        for j in range(out_ref.shape[0]):
            out_ref[j, 0] = rows_ref[partner(place_ref, j, i, spans)]


def prepare_apart(place, amplitudes, keep, cut, groups, spans):
    _, variables, _, modes = amplitudes.shape
    freqs = modes // NB
    rows = cut.stop - cut.start
    at = cut.start // rows
    return pl.pallas_call(
        prepare_apart_body,
        grid=(variables,),
        in_specs=[
            pl.BlockSpec(memory_space=pltpu.SMEM),
            pl.BlockSpec((2, 1, rows, modes), lambda v: (0, v, at, 0)),
            pl.BlockSpec((modes,), lambda v: (0,)),
        ],
        out_specs=[pl.BlockSpec((groups, 1, freqs, 2 * NB), lambda v: (0, v, 0, 0))] * spans,
        out_shape=[jax.ShapeDtypeStruct((groups, variables, freqs, 2 * NB), jnp.float32)] * spans,
        scratch_shapes=[pltpu.VMEM((rows, freqs, 2 * NB), jnp.float32)],
        compiler_params=params(),
        name="prepare_apart",
    )(place, in_hbm(amplitudes), keep)


def transform(read, write, q_ref, table_refs, field_ref, force_ref):
    wi_ref, ei_ref, ef_ref, wf_ref = table_refs
    variables = field_ref.shape[0]
    for v in range(variables):
        modes = read(v)
        stacked = jnp.concatenate([modes[:, :NB], modes[:, NB:]], axis=0)
        turned = jnp.dot(
            wi_ref[...], stacked, precision=SPLIT, preferred_element_type=jnp.float32
        )
        beside = jnp.concatenate([turned[:NF], turned[NF:]], axis=1)
        field_ref[v] = jnp.dot(
            beside, ei_ref[...], precision=SPLIT, preferred_element_type=jnp.float32
        )
    pairs = [(a, b) for a in range(variables) for b in range(a + 1, variables)]
    weights = [
        [q_ref[w * variables + a, b] + q_ref[w * variables + b, a] for a, b in pairs]
        for w in range(variables)
    ]
    step = 8
    for row in range(0, NF, step):
        at = slice(row, row + step)
        values = [field_ref[v, at] for v in range(variables)]
        total = [None] * variables
        for i, (a, b) in enumerate(pairs):
            product = values[a] * values[b]
            for w in range(variables):
                term = weights[w][i] * product
                total[w] = term if total[w] is None else total[w] + term
        for w in range(variables):
            force_ref[w, at] = total[w]
    for w in range(variables):
        spread = jnp.dot(
            force_ref[w], ef_ref[...], precision=SPLIT, preferred_element_type=jnp.float32
        )
        stacked = jnp.concatenate([spread[:, :NB], spread[:, NB:]], axis=0)
        turned = jnp.dot(
            wf_ref[...], stacked, precision=SPLIT, preferred_element_type=jnp.float32
        )
        for part in range(2):
            write(w, part, turned[part * NF : (part + 1) * NF])


def nonlinear_body(q_ref, in_ref, *refs):
    table_refs, out_ref, work_refs = refs[:4], refs[4], refs[5:]
    devices, _, _, freqs, _ = in_ref.shape

    def read(v):
        return in_ref[:, 0, v].reshape(NF, 2 * NB)

    def write(w, part, piece):
        at = slice(part * NB, (part + 1) * NB)
        out_ref[:, 0, w, :, at] = piece.reshape(devices, freqs, NB)

    transform(read, write, q_ref, table_refs, *work_refs)


def work_shapes(variables):
    return [pltpu.VMEM((variables, NF, NB), jnp.float32)] * 2


def nonlinear_cost(points, variables):
    return pl.CostEstimate(
        flops=points * variables * 12 * NF * NB * (NF + NB) * 2,
        bytes_accessed=points * variables * NF * NB * 16,
        transcendentals=0,
    )


def nonlinear(block, coefficients, transforms):
    devices, points, variables, freqs, lanes = block.shape
    spec = pl.BlockSpec((devices, 1, variables, freqs, lanes), lambda j: (0, j, 0, 0, 0))
    return pl.pallas_call(
        nonlinear_body,
        grid=(points,),
        in_specs=[pl.BlockSpec(memory_space=pltpu.SMEM), spec] + [whole(t) for t in transforms],
        out_specs=spec,
        out_shape=pltpu.HBM(block.shape, jnp.float32),
        scratch_shapes=work_shapes(variables),
        compiler_params=params(24),
        cost_estimate=nonlinear_cost(points, variables),
        name="nonlinear",
    )(coefficients, block, *transforms)


def nonlinear_apart_body(groups, place_ref, q_ref, *refs):
    in_refs, refs = refs[:groups], refs[groups:]
    table_refs, refs = refs[:4], refs[4:]
    out_refs, refs = refs[:groups], refs[groups:]
    rows_ref, work_refs = refs[0], refs[1:]
    devices, _, freqs, _ = rows_ref.shape
    spans = devices // groups
    for j in range(groups):
        for i in range(spans):
            rows_ref[partner(place_ref, j, i, spans)] = in_refs[j][i]

    def read(v):
        return rows_ref[:, v].reshape(NF, 2 * NB)

    def write(w, part, piece):
        at = slice(part * NB, (part + 1) * NB)
        rows_ref[:, w, :, at] = piece.reshape(devices, freqs, NB)

    transform(read, write, q_ref, table_refs, *work_refs)
    for j in range(groups):
        for i in range(spans):
            out_refs[j][i] = rows_ref[partner(place_ref, j, i, spans)]


def nonlinear_apart(place, blocks, coefficients, transforms):
    groups = len(blocks)
    spans, variables, freqs, lanes = blocks[0].shape
    smem = pl.BlockSpec(memory_space=pltpu.SMEM)
    return pl.pallas_call(
        functools.partial(nonlinear_apart_body, groups),
        grid=(1,),
        in_specs=[smem, smem]
        + [whole(block) for block in blocks]
        + [whole(table) for table in transforms],
        out_specs=[whole(block) for block in blocks],
        out_shape=[jax.ShapeDtypeStruct(block.shape, jnp.float32) for block in blocks],
        scratch_shapes=[pltpu.VMEM((groups * spans, variables, freqs, lanes), jnp.float32)]
        + work_shapes(variables),
        compiler_params=params(24),
        cost_estimate=nonlinear_cost(1, variables),
        name="nonlinear_apart",
    )(place, coefficients, *blocks, *transforms)


def base_body(cuts, x_ref, up_ref, mask_ref, inverse_ref, turned_ref, *refs):
    out_refs, (edge_ref, solved_ref, sum_ref) = refs[: len(cuts)], refs[len(cuts) :]
    _, variables, heights, lanes = x_ref.shape
    extent = variables * heights
    ends = 2 * variables
    keep = kept_modes(mask_ref)
    kept, solved = [], []
    for part in range(2):
        kept.append(x_ref[part].reshape(extent, lanes) * keep)
        moved = jnp.dot(
            turned_ref[...], kept[part], precision=SPLIT, preferred_element_type=jnp.float32
        )
        grid = moved.reshape(variables, heights, lanes)
        for cut, out_ref in zip(cuts, out_refs):
            out_ref[part] = grid[:, cut]
        side = up_ref[part].reshape(extent, lanes) * keep
        solved.append(
            jnp.dot(inverse_ref[...], side, precision=SPLIT, preferred_element_type=jnp.float32)
        )
        solved_ref[part] = solved[part].reshape(variables, heights, lanes)
        for end, point in enumerate((0, heights - 1)):
            for v in range(variables):
                row = part * ends + end * variables + v
                at = v * heights + point
                edge_ref[row : row + 1] = moved[at : at + 1]
                sum_ref[row : row + 1] = solved[part][at : at + 1]

    def total(value):
        return jnp.sum(value, axis=0, keepdims=True)

    row = 2 * ends
    none = jnp.zeros((GATHERED_ROWS - row - 1, lanes), jnp.float32)
    edge_ref[row : row + 1] = total(kept[0] * kept[0] + kept[1] * kept[1])
    edge_ref[row + 1 :] = none
    sum_ref[row : row + 1] = total(kept[0] * solved[0] + kept[1] * solved[1])
    sum_ref[row + 1 : row + 2] = total(kept[0] * solved[1] - kept[1] * solved[0])
    sum_ref[row + 2 :] = none[1:]


def base(amplitudes, upstream, keep, inverse, turned, cuts):
    _, variables, heights, modes = amplitudes.shape

    def rows_spec(rows):
        return pl.BlockSpec((2, variables, rows, NB), lambda i: (0, 0, 0, i))

    def rows_shape(rows):
        return jax.ShapeDtypeStruct((2, variables, rows, modes), jnp.float32)

    lengths = [cut.stop - cut.start for cut in cuts]
    small = pl.BlockSpec((GATHERED_ROWS, NB), lambda i: (0, i))
    small_shape = jax.ShapeDtypeStruct((GATHERED_ROWS, modes), jnp.float32)
    return pl.pallas_call(
        functools.partial(base_body, cuts),
        grid=(modes // NB,),
        in_specs=[rows_spec(heights)] * 2
        + [pl.BlockSpec((NB,), lambda i: (i,)), whole(inverse), whole(turned)],
        out_specs=[rows_spec(rows) for rows in lengths] + [small, rows_spec(heights), small],
        out_shape=[rows_shape(rows) for rows in lengths]
        + [small_shape, rows_shape(heights), small_shape],
        compiler_params=params(24),
        name="base",
    )(in_hbm(amplitudes), in_hbm(upstream), keep, inverse, turned)


def absorb_rows(read, mask_ref, edge_ref, adj_ref, before_ref, out_ref, sum_ref):
    ends = edge_ref.shape[1]
    rows = out_ref.shape[2]
    keep = kept_modes(mask_ref)

    @pl.when(pl.program_id(0) == 0)
    def _():
        sum_ref[...] = before_ref[...]

    sides = []
    for part in range(2):
        side = read(part).reshape(rows, -1) * keep
        out_ref[part, 0] = side
        at = slice(part * ends, (part + 1) * ends)
        sum_ref[at] += jnp.dot(
            edge_ref[0], side, precision=SPLIT, preferred_element_type=jnp.float32
        )
        sides.append(side)
    real, imag = adj_ref[0, 0], adj_ref[1, 0]
    at = 2 * ends
    sum_ref[at : at + 1] += jnp.sum(real * sides[0] + imag * sides[1], axis=0, keepdims=True)
    sum_ref[at + 1 : at + 2] += jnp.sum(real * sides[1] - imag * sides[0], axis=0, keepdims=True)


def absorb_body(in_ref, *refs):
    def read(part):
        return in_ref[:, 0, :, part * NB : (part + 1) * NB]

    absorb_rows(read, *refs)


def absorb_apart_body(spans, place_ref, *refs):
    in_refs, refs, rows_ref = refs[:spans], refs[spans:-1], refs[-1]
    for i, in_ref in enumerate(in_refs):
        for j in range(in_ref.shape[0]):
            rows_ref[partner(place_ref, j, i, spans)] = in_ref[j, 0]

    def read(part):
        return rows_ref[:, :, part * NB : (part + 1) * NB]

    absorb_rows(read, *refs)


def absorb(place, blocks, keep, edges, adjoint_modes, before):
    blocks = list(blocks)
    apart = place is not None
    _, variables, rows, modes = adjoint_modes.shape
    ends = edges.shape[1]
    grid_spec = pl.BlockSpec((2, 1, rows, modes), lambda v: (0, v, 0, 0))
    sums = pl.BlockSpec((GATHERED_ROWS, modes), lambda v: (0, 0))
    length, _, freqs, lanes = blocks[0].shape
    in_specs = [pl.BlockSpec((length, 1, freqs, lanes), lambda v: (0, v, 0, 0))] * len(blocks)
    in_specs += [
        pl.BlockSpec((modes,), lambda v: (0,)),
        pl.BlockSpec((1, ends, rows), lambda v: (v, 0, 0)),
        grid_spec,
        sums,
    ]
    operands = blocks + [keep, edges, adjoint_modes, before]
    body, scratch = absorb_body, []
    if apart:
        operands = [place] + operands
        in_specs = [pl.BlockSpec(memory_space=pltpu.SMEM)] + in_specs
        body = functools.partial(absorb_apart_body, len(blocks))
        scratch = [pltpu.VMEM((rows, freqs, lanes), jnp.float32)]
    return pl.pallas_call(
        body,
        grid=(variables,),
        in_specs=in_specs,
        out_specs=[grid_spec, sums],
        out_shape=[
            jax.ShapeDtypeStruct((2, variables, rows, modes), jnp.float32),
            jax.ShapeDtypeStruct((GATHERED_ROWS, modes), jnp.float32),
        ],
        scratch_shapes=scratch,
        compiler_params=params(),
        name="absorb_apart" if apart else "absorb",
    )(*operands)


def solve_body(side_ref, before_ref, inverse_ref, out_ref):
    _, variables, heights, lanes = out_ref.shape
    for part in range(2):
        moved = jnp.dot(
            inverse_ref[...],
            side_ref[part].reshape(-1, lanes),
            precision=SPLIT,
            preferred_element_type=jnp.float32,
        )
        out_ref[part] = before_ref[part] + moved.reshape(variables, heights, lanes)


def solve(side, before, inverse):
    _, variables, rows, modes = side.shape
    heights = before.shape[2]
    spec = pl.BlockSpec((2, variables, heights, NB), lambda i: (0, 0, 0, i))
    side_spec = pl.BlockSpec((2, variables, rows, NB), lambda i: (0, 0, 0, i))
    return pl.pallas_call(
        solve_body,
        grid=(modes // NB,),
        in_specs=[side_spec, spec, whole(inverse)],
        out_specs=spec,
        out_shape=jax.ShapeDtypeStruct(before.shape, jnp.float32),
        compiler_params=params(),
        name="solve",
    )(side, before, inverse)


def finish_body(walls, extent, solved_ref, *refs):
    bounds, refs = refs[:walls], refs[walls:]
    edges, refs = refs[:walls], refs[walls:]
    chain_ref, out_ref, shift_ref = refs
    _, variables, heights, lanes = out_ref.shape
    ends = 2 * variables
    pushed = []
    for part in range(2):
        at = slice(part * ends, (part + 1) * ends)
        everywhere = [ref[at] for ref in bounds]
        spare = chain_ref.shape[1] // 3 - walls * ends
        if spare:
            everywhere.append(jnp.zeros((spare, lanes), jnp.float32))
        everywhere = jnp.concatenate(everywhere, axis=0)
        high = everywhere.astype(jnp.bfloat16)
        low = (everywhere - high.astype(jnp.float32)).astype(jnp.bfloat16)
        moved = jnp.dot(
            chain_ref[...],
            jnp.concatenate([high, low, high], axis=0),
            preferred_element_type=jnp.float32,
        )
        pushed.append(moved[extent:])
        out_ref[part] = solved_ref[part] - moved[:extent].reshape(variables, heights, lanes)
    real = imag = weight = 0.0
    for wall in range(walls):
        at = slice(wall * ends, (wall + 1) * ends)
        push = [pushed[part][at] for part in range(2)]
        edge = [edges[wall][part * ends : (part + 1) * ends] for part in range(2)]
        row = 2 * ends
        squares = edges[wall][row : row + 1]
        taken = jnp.sum(edge[0] * push[0] + edge[1] * push[1], axis=0, keepdims=True)
        real = real + (bounds[wall][row : row + 1] - taken - squares)
        taken = jnp.sum(edge[0] * push[1] - edge[1] * push[0], axis=0, keepdims=True)
        imag = imag + (bounds[wall][row + 1 : row + 2] - taken)
        weight = weight + squares
    weight = weight + epsilon
    shift_ref[0:1] = imag / weight
    shift_ref[1:2] = -real / weight


def finish(solved, bounds, edges, chain):
    _, variables, heights, modes = solved.shape
    walls = len(bounds)
    lanes = min(2 * NB, modes)
    small = pl.BlockSpec((GATHERED_ROWS, lanes), lambda i: (0, i))
    spec = pl.BlockSpec((2, variables, heights, lanes), lambda i: (0, 0, 0, i))
    return pl.pallas_call(
        functools.partial(finish_body, walls, variables * heights),
        grid=(modes // lanes,),
        in_specs=[spec] + [small] * (2 * walls) + [whole(chain)],
        out_specs=[spec, pl.BlockSpec((2, lanes), lambda i: (0, i))],
        out_shape=[
            jax.ShapeDtypeStruct(solved.shape, jnp.float32),
            jax.ShapeDtypeStruct((2, modes), jnp.float32),
        ],
        compiler_params=params(),
        name="finish",
    )(solved, *bounds, *edges, chain)


def around(block, axis):
    count = lax.axis_size(axis)
    return [block] + [
        lax.ppermute(block, axis, [(i, (i + d) % count) for i in range(count)])
        for d in range(1, count)
    ]


PACKED_ROWS = 16


def pack_body(*refs):
    in_refs, out_ref = refs[:-1], refs[-1]
    out_ref[...] = jnp.zeros(out_ref.shape, jnp.float32)
    for i, ref in enumerate(in_refs):
        rows, columns = ref.shape[1:]
        out_ref[i, :rows, :columns] = ref[0]


def pack(parts):
    return pl.pallas_call(
        pack_body,
        out_shape=jax.ShapeDtypeStruct((len(parts), PACKED_ROWS, 128), jnp.float32),
        name="pack",
    )(*parts)


def upper_bits(value):
    return value.astype(jnp.bfloat16).astype(jnp.float32)


def constants_body(cuts, variables, walls, place_ref, inverse_ref, *refs):
    packed, refs = refs[:walls], refs[walls:]
    turned_ref, refs = refs[0], refs[1:]
    column_refs, refs = refs[: len(cuts)], refs[len(cuts) :]
    row_refs, refs = refs[: len(cuts)], refs[len(cuts) :]
    chain_ref, all_ref, step_ref = refs
    extent = inverse_ref.shape[0]
    heights = extent // variables
    ends = 2 * variables
    matrix = inverse_ref[...]
    turned = matrix.T
    turned_ref[...] = turned
    for cut, column_ref, row_ref in zip(cuts, column_refs, row_refs):
        pieces = []
        for v in range(variables):
            part = matrix[:, v * heights : (v + 1) * heights][:, cut]
            pieces.append(part)
            for end, point in enumerate((0, heights - 1)):
                for w in range(variables):
                    at = w * heights + point
                    row = end * variables + w
                    row_ref[v, row : row + 1] = part[at : at + 1]
        column_ref[...] = jnp.concatenate(pieces, axis=1)

    def dot(a, b):
        return jnp.dot(a, b, precision=FULL, preferred_element_type=jnp.float32)

    size = walls * PACKED_ROWS
    for d in range(walls):
        all_ref[(place_ref[0] - d + walls) % walls] = packed[d][...]

    def small(j, kind):
        return all_ref[j, kind][:, :PACKED_ROWS]

    row = lax.broadcasted_iota(jnp.int32, (PACKED_ROWS, size), 0)
    column = lax.broadcasted_iota(jnp.int32, (PACKED_ROWS, size), 1)
    units = []
    for j in range(walls):
        d = (place_ref[0] - j + walls) % walls
        hit = (column == d * ends + row) & (row < ends)
        units.append(jnp.where(hit, 1.0, 0.0))
    ahead = [units[0]]
    for j in range(1, walls):
        ahead.append(units[j] - dot(small(j, 2), ahead[j - 1]))
    interface = [None] * walls
    interface[-1] = dot(small(walls - 1, 4), ahead[-1])
    for j in range(walls - 2, -1, -1):
        interface[j] = dot(small(j, 4), ahead[j] - dot(small(j, 3), interface[j + 1]))
    for j in range(walls):
        none = jnp.zeros((variables, size), jnp.float32)
        under, over = none, none
        if j > 0:
            last = jnp.concatenate([interface[j - 1][variables:], none], axis=0)[:PACKED_ROWS]
            under = dot(small(j, 0), last)[:variables]
        if j < walls - 1:
            over = dot(small(j, 1), interface[j + 1])[:variables]
        step_ref[(place_ref[0] - j + walls) % walls] = jnp.concatenate(
            [under, over, jnp.zeros((PACKED_ROWS - ends, size), jnp.float32)], axis=0
        )
    pushes = [step_ref[d][:ends] for d in range(walls)]
    edge = [turned[v * heights : v * heights + 1] for v in range(variables)]
    edge += [turned[(v + 1) * heights - 1 : (v + 1) * heights] for v in range(variables)]
    edge.append(jnp.zeros((PACKED_ROWS - ends, extent), jnp.float32))
    edge = jnp.concatenate(edge, axis=0).T
    own = dot(edge, step_ref[0])
    spare = chain_ref.shape[0] - extent - walls * ends
    full = [own] + pushes
    if spare:
        full.append(jnp.zeros((spare, size), jnp.float32))
    full = jnp.concatenate(full, axis=0)
    high = upper_bits(full)
    chain_ref[...] = jnp.concatenate([high, high, full - high], axis=1).astype(jnp.bfloat16)


def constants(place, inverse, packed, cuts, variables):
    walls = len(packed)
    extent = inverse.shape[0]
    heights = extent // variables
    ends = 2 * variables
    lengths = [cut.stop - cut.start for cut in cuts]
    size = walls * PACKED_ROWS
    rows = extent + walls * ends + (-walls * ends) % 16
    f32 = jnp.float32
    return pl.pallas_call(
        functools.partial(constants_body, cuts, variables, walls),
        in_specs=[pl.BlockSpec(memory_space=pltpu.SMEM)]
        + [pl.BlockSpec(memory_space=pltpu.VMEM)] * (1 + walls),
        out_shape=[jax.ShapeDtypeStruct((extent, extent), f32)]
        + [jax.ShapeDtypeStruct((extent, variables * n), f32) for n in lengths]
        + [jax.ShapeDtypeStruct((variables, ends, n), f32) for n in lengths]
        + [jax.ShapeDtypeStruct((rows, 3 * size), jnp.bfloat16)],
        scratch_shapes=[
            pltpu.VMEM((walls,) + packed[0].shape, f32),
            pltpu.VMEM((walls, PACKED_ROWS, size), f32),
        ],
        compiler_params=params(),
        name="constants",
    )(place, inverse, *packed)


def local(
    amplitudes,
    upstream,
    harmonic_mask,
    quadratic_coefficients,
    slab_inverse,
    lower_coupling,
    upper_coupling,
    reduced_lower,
    reduced_upper,
    reduced_pivot,
):
    _, variables, heights, modes = amplitudes.shape
    axes = ("freq", "span")
    groups, spans = lax.axis_size("freq"), lax.axis_size("span")
    devices = groups * spans
    points = heights // devices
    apart = points > 1 and groups & (groups - 1) == 0 and spans & (spans - 1) == 0
    edge_at = heights - devices if apart else heights
    cuts = [slice(0, edge_at)] + ([slice(edge_at, heights)] if apart else [])
    keep = harmonic_mask
    place = jnp.stack([lax.axis_index("freq"), lax.axis_index("span")]).astype(jnp.int32)
    wall = lax.axis_index("wall").reshape(1).astype(jnp.int32)
    transforms = tables()
    coefficients = quadratic_coefficients.reshape(variables * variables, variables)

    def exchange(block):
        return lax.all_to_all(block, axes, split_axis=0, concat_axis=0, tiled=True)

    def swap(blocks, axis, only=None):
        count = len(blocks)
        return [
            lax.ppermute(block, axis, [(at, at ^ i) for at in range(count)])
            if i and (only is None or i in only)
            else block
            for i, block in enumerate(blocks)
        ]

    def regroup(blocks):
        return [jnp.stack([block[j] for block in blocks]) for j in range(blocks[0].shape[0])]

    far = {spans // 2}
    main = prepare(amplitudes, keep, cuts[0])
    if apart:
        main, amplitudes = lax.optimization_barrier((main, amplitudes))
        sent = prepare_apart(place, amplitudes, keep, cuts[1], groups, spans)
        arrived = swap(sent, "span", set(range(spans)) - far)
    main = exchange(main)

    inverse = slab_inverse[0]
    parts = (lower_coupling, upper_coupling, reduced_lower, reduced_upper, reduced_pivot)
    packed = around(pack(parts), "wall")
    turned, *rest, chain = constants(wall, inverse, packed, cuts, variables)
    columns, end_rows = rest[: len(cuts)], rest[len(cuts) :]
    *adjoint_modes, edge, solved, sums = base(
        amplitudes, upstream, keep, inverse, turned, cuts
    )
    edges = around(edge, "wall")
    held = (main, columns, end_rows, chain, adjoint_modes, edges, solved, sums)
    held = lax.optimization_barrier(held)
    main, columns, end_rows, chain, adjoint_modes, edges, solved, sums = held

    if apart:
        main, arrived = lax.optimization_barrier((main, arrived))
        arrived = swap(arrived, "span", far)
    size = edge_at // devices
    shape = main.shape
    main = nonlinear(main.reshape((devices, size) + shape[1:]), coefficients, transforms)
    main = main.reshape(shape)
    if apart:
        main, arrived = lax.optimization_barrier((main, arrived))
    main = exchange(main)
    if apart:
        arrived = swap(regroup(arrived), "freq")
        forced = nonlinear_apart(place, arrived, coefficients, transforms)
        returned = swap(regroup(swap(forced, "freq")), "span")

    side, sums = absorb(None, [main], keep, end_rows[0], adjoint_modes[0], sums)
    if apart:
        solved = solve(side, solved, columns[0])
        solved, sums, adjoint_modes[1], edges, chain, columns[1] = lax.optimization_barrier(
            (solved, sums, adjoint_modes[1], edges, chain, columns[1])
        )
        side, sums = absorb(place, returned, keep, end_rows[1], adjoint_modes[1], sums)
    bounds = around(sums, "wall")
    solved = solve(side, solved, columns[-1])
    new_amplitudes, wavenumber_shift = finish(solved, bounds, edges, chain)
    return (new_amplitudes, wavenumber_shift)


def solution(mesh):
    placed = (
        P(None, None, "wall", ("freq", "span")),
        P(None, None, "wall", ("freq", "span")),
        P(("freq", "span")),
        P(),
        P("wall", None, None),
        P("wall", None, None),
        P("wall", None, None),
        P("wall", None, None),
        P("wall", None, None),
        P("wall", None, None),
    )
    return jax.shard_map(
        local,
        mesh=mesh,
        in_specs=placed,
        out_specs=(P(None, None, "wall", ("freq", "span")), P(None, ("freq", "span"))),
        check_vma=False,
    )
```

```python
import functools
import math

import jax
import jax.numpy as jnp
import numpy as np
from jax import lax
from jax.experimental import pallas as pl
from jax.experimental.pallas import tpu as pltpu
from jax.sharding import PartitionSpec as P

NF = 128
NB = 256

epsilon = 1e-06

SPLIT = lax.Precision.HIGH
FULL = lax.Precision.HIGHEST
GATHERED_ROWS = 24


def tables():
    def turns(length):
        counter = np.arange(length)
        angles = (counter[:, None] * counter[None, :] % length) * (2.0 * math.pi / length)
        return np.cos(angles), np.sin(angles)

    cos_time, sin_time = turns(NF)
    cos_span, sin_span = turns(NB)
    scale = 1.0 / math.sqrt(NF * NB)
    out = (
        np.block([[cos_time, -sin_time], [sin_time, cos_time]]),
        np.concatenate([cos_span, -sin_span], 0) * scale,
        np.concatenate([cos_span, -sin_span], 1) * scale,
        np.block([[cos_time, sin_time], [-sin_time, cos_time]]),
    )
    return [jnp.asarray(table.astype(np.float32)) for table in out]


def params(megabytes=16):
    return pltpu.CompilerParams(vmem_limit_bytes=megabytes * 1024 * 1024)


def whole(array):
    zeros = (0,) * len(array.shape)
    return pl.BlockSpec(array.shape, lambda *_: zeros)


def in_hbm(array):
    return pltpu.with_memory_space_constraint(array, pltpu.HBM)


def kept_modes(mask_ref):
    return mask_ref[...].astype(jnp.float32).reshape(1, -1)


def prepare_body(x_ref, mask_ref, out_ref):
    keep = kept_modes(mask_ref)
    rows, _, freqs, _ = out_ref.shape
    for part in range(2):
        kept = x_ref[part, 0] * keep
        out_ref[:, 0, :, part * NB : (part + 1) * NB] = kept.reshape(rows, freqs, NB)


def prepare(amplitudes, keep, cut):
    _, variables, _, modes = amplitudes.shape
    freqs = modes // NB
    rows = cut.stop - cut.start
    at = cut.start // rows
    return pl.pallas_call(
        prepare_body,
        grid=(variables,),
        in_specs=[
            pl.BlockSpec((2, 1, rows, modes), lambda v: (0, v, at, 0)),
            pl.BlockSpec((modes,), lambda v: (0,)),
        ],
        out_specs=pl.BlockSpec((rows, 1, freqs, 2 * NB), lambda v: (0, v, 0, 0)),
        out_shape=pltpu.HBM((rows, variables, freqs, 2 * NB), jnp.float32),
        compiler_params=params(),
        name="prepare",
    )(in_hbm(amplitudes), in_hbm(keep))


def partner(place_ref, j, i, spans):
    return (place_ref[0] ^ j) * spans + (place_ref[1] ^ i)


def prepare_apart_body(place_ref, x_ref, mask_ref, *refs):
    out_refs, rows_ref = refs[:-1], refs[-1]
    keep = kept_modes(mask_ref)
    rows, freqs, _ = rows_ref.shape
    spans = out_refs[0].shape[0]
    for part in range(2):
        kept = x_ref[part, 0] * keep
        rows_ref[:, :, part * NB : (part + 1) * NB] = kept.reshape(rows, freqs, NB)
    for j, out_ref in enumerate(out_refs):
        for i in range(spans):
            out_ref[i, 0] = rows_ref[partner(place_ref, j, i, spans)]


def prepare_apart(place, amplitudes, keep, cut, groups, spans):
    _, variables, _, modes = amplitudes.shape
    freqs = modes // NB
    rows = cut.stop - cut.start
    at = cut.start // rows
    return pl.pallas_call(
        prepare_apart_body,
        grid=(variables,),
        in_specs=[
            pl.BlockSpec(memory_space=pltpu.SMEM),
            pl.BlockSpec((2, 1, rows, modes), lambda v: (0, v, at, 0)),
            pl.BlockSpec((modes,), lambda v: (0,)),
        ],
        out_specs=[pl.BlockSpec((spans, 1, freqs, 2 * NB), lambda v: (0, v, 0, 0))] * groups,
        out_shape=[jax.ShapeDtypeStruct((spans, variables, freqs, 2 * NB), jnp.float32)] * groups,
        scratch_shapes=[pltpu.VMEM((rows, freqs, 2 * NB), jnp.float32)],
        compiler_params=params(),
        name="prepare_apart",
    )(place, in_hbm(amplitudes), keep)


def transform(read, write, q_ref, table_refs, field_ref, force_ref):
    wi_ref, ei_ref, ef_ref, wf_ref = table_refs
    variables = field_ref.shape[0]
    for v in range(variables):
        modes = read(v)
        stacked = jnp.concatenate([modes[:, :NB], modes[:, NB:]], axis=0)
        turned = jnp.dot(
            wi_ref[...], stacked, precision=SPLIT, preferred_element_type=jnp.float32
        )
        beside = jnp.concatenate([turned[:NF], turned[NF:]], axis=1)
        field_ref[v] = jnp.dot(
            beside, ei_ref[...], precision=SPLIT, preferred_element_type=jnp.float32
        )
    pairs = [(a, b) for a in range(variables) for b in range(a + 1, variables)]
    weights = [
        [q_ref[w * variables + a, b] + q_ref[w * variables + b, a] for a, b in pairs]
        for w in range(variables)
    ]
    step = 8
    for row in range(0, NF, step):
        at = slice(row, row + step)
        values = [field_ref[v, at] for v in range(variables)]
        total = [None] * variables
        for i, (a, b) in enumerate(pairs):
            product = values[a] * values[b]
            for w in range(variables):
                term = weights[w][i] * product
                total[w] = term if total[w] is None else total[w] + term
        for w in range(variables):
            force_ref[w, at] = total[w]
    for w in range(variables):
        spread = jnp.dot(
            force_ref[w], ef_ref[...], precision=SPLIT, preferred_element_type=jnp.float32
        )
        stacked = jnp.concatenate([spread[:, :NB], spread[:, NB:]], axis=0)
        turned = jnp.dot(
            wf_ref[...], stacked, precision=SPLIT, preferred_element_type=jnp.float32
        )
        for part in range(2):
            write(w, part, turned[part * NF : (part + 1) * NF])


def nonlinear_body(q_ref, in_ref, *refs):
    table_refs, out_ref, work_refs = refs[:4], refs[4], refs[5:]
    devices, _, _, freqs, _ = in_ref.shape

    def read(v):
        return in_ref[:, 0, v].reshape(NF, 2 * NB)

    def write(w, part, piece):
        at = slice(part * NB, (part + 1) * NB)
        out_ref[:, 0, w, :, at] = piece.reshape(devices, freqs, NB)

    transform(read, write, q_ref, table_refs, *work_refs)


def work_shapes(variables):
    return [pltpu.VMEM((variables, NF, NB), jnp.float32)] * 2


def nonlinear_cost(points, variables):
    return pl.CostEstimate(
        flops=points * variables * 12 * NF * NB * (NF + NB) * 2,
        bytes_accessed=points * variables * NF * NB * 16,
        transcendentals=0,
    )


def nonlinear(block, coefficients, transforms):
    devices, points, variables, freqs, lanes = block.shape
    spec = pl.BlockSpec((devices, 1, variables, freqs, lanes), lambda j: (0, j, 0, 0, 0))
    return pl.pallas_call(
        nonlinear_body,
        grid=(points,),
        in_specs=[pl.BlockSpec(memory_space=pltpu.SMEM), spec] + [whole(t) for t in transforms],
        out_specs=spec,
        out_shape=pltpu.HBM(block.shape, jnp.float32),
        scratch_shapes=work_shapes(variables),
        compiler_params=params(24),
        cost_estimate=nonlinear_cost(points, variables),
        name="nonlinear",
    )(coefficients, block, *[in_hbm(table) for table in transforms])


def nonlinear_apart_body(groups, spans, place_ref, q_ref, *refs):
    in_refs, refs = refs[:spans], refs[spans:]
    table_refs, refs = refs[:4], refs[4:]
    out_refs, refs = refs[:groups], refs[groups:]
    rows_ref, work_refs = refs[0], refs[1:]
    devices, _, freqs, _ = rows_ref.shape
    for j in range(groups):
        for i in range(spans):
            rows_ref[partner(place_ref, j, i, spans)] = in_refs[i][j]

    def read(v):
        return rows_ref[:, v].reshape(NF, 2 * NB)

    def write(w, part, piece):
        at = slice(part * NB, (part + 1) * NB)
        rows_ref[:, w, :, at] = piece.reshape(devices, freqs, NB)

    transform(read, write, q_ref, table_refs, *work_refs)
    for j in range(groups):
        for i in range(spans):
            out_refs[j][i] = rows_ref[partner(place_ref, j, i, spans)]


def nonlinear_apart(place, blocks, coefficients, transforms):
    spans = len(blocks)
    groups, variables, freqs, lanes = blocks[0].shape
    result = jax.ShapeDtypeStruct((spans, variables, freqs, lanes), jnp.float32)
    smem = pl.BlockSpec(memory_space=pltpu.SMEM)
    return pl.pallas_call(
        functools.partial(nonlinear_apart_body, groups, spans),
        grid=(1,),
        in_specs=[smem, smem]
        + [whole(block) for block in blocks]
        + [whole(table) for table in transforms],
        out_specs=[whole(result)] * groups,
        out_shape=[result] * groups,
        scratch_shapes=[pltpu.VMEM((groups * spans, variables, freqs, lanes), jnp.float32)]
        + work_shapes(variables),
        compiler_params=params(24),
        cost_estimate=nonlinear_cost(1, variables),
        name="nonlinear_apart",
    )(place, coefficients, *blocks, *[in_hbm(table) for table in transforms])


def base_body(cuts, x_ref, up_ref, mask_ref, edge_rows_ref, turned_ref, *refs):
    out_refs, (edge_ref, sum_ref) = refs[: len(cuts)], refs[len(cuts) :]
    _, variables, heights, lanes = x_ref.shape
    extent = variables * heights
    ends = 2 * variables
    keep = kept_modes(mask_ref)
    squares, moved, sides = 0.0, [], []
    for part in range(2):
        kept = x_ref[part].reshape(extent, lanes) * keep
        squares = squares + total(kept * kept)
        moved.append(
            jnp.dot(turned_ref[...], kept, precision=SPLIT, preferred_element_type=jnp.float32)
        )
        grid = moved[part].reshape(variables, heights, lanes)
        for cut, out_ref in zip(cuts, out_refs):
            out_ref[part] = grid[:, cut]
        sides.append(up_ref[part].reshape(extent, lanes) * keep)
        sum_ref[part * ends : (part + 1) * ends] = jnp.dot(
            edge_rows_ref[...], sides[part], precision=SPLIT, preferred_element_type=jnp.float32
        )
        for end, point in enumerate((0, heights - 1)):
            for v in range(variables):
                row = part * ends + end * variables + v
                at = v * heights + point
                edge_ref[row : row + 1] = moved[part][at : at + 1]
    row = 2 * ends
    none = jnp.zeros((GATHERED_ROWS - row - 1, lanes), jnp.float32)
    edge_ref[row : row + 1] = squares
    edge_ref[row + 1 :] = none
    sum_ref[row : row + 1] = total(moved[0] * sides[0] + moved[1] * sides[1])
    sum_ref[row + 1 : row + 2] = total(moved[0] * sides[1] - moved[1] * sides[0])
    sum_ref[row + 2 :] = none[1:]


def total(value):
    return jnp.sum(value, axis=0, keepdims=True)


def base(amplitudes, upstream, keep, edge_rows, turned, cuts):
    _, variables, heights, modes = amplitudes.shape
    lengths = [cut.stop - cut.start for cut in cuts]
    shapes = [(2, variables, rows, modes) for rows in lengths]
    spec = pl.BlockSpec((2, variables, heights, NB), lambda i: (0, 0, 0, i))
    small = pl.BlockSpec((GATHERED_ROWS, NB), lambda i: (0, i))
    small_shape = jax.ShapeDtypeStruct((GATHERED_ROWS, modes), jnp.float32)
    return pl.pallas_call(
        functools.partial(base_body, cuts),
        grid=(modes // NB,),
        in_specs=[spec] * 2
        + [pl.BlockSpec((NB,), lambda i: (i,)), whole(edge_rows), whole(turned)],
        out_specs=[
            pl.BlockSpec((2, variables, rows, NB), lambda i: (0, 0, 0, i)) for rows in lengths
        ]
        + [small] * 2,
        out_shape=[pltpu.HBM(shapes[0], jnp.float32)]
        + [jax.ShapeDtypeStruct(shape, jnp.float32) for shape in shapes[1:]]
        + [small_shape] * 2,
        compiler_params=params(24),
        name="base",
    )(in_hbm(amplitudes), in_hbm(upstream), keep, edge_rows, turned)


def absorb_rows(read, mask_ref, edge_ref, adj_ref, before_ref, out_ref, sum_ref):
    ends = edge_ref.shape[1]
    rows = out_ref.shape[2]
    keep = kept_modes(mask_ref)

    @pl.when(pl.program_id(0) == 0)
    def _():
        sum_ref[...] = before_ref[...]

    sides = []
    for part in range(2):
        side = read(part).reshape(rows, -1) * keep
        out_ref[part, 0] = side
        at = slice(part * ends, (part + 1) * ends)
        sum_ref[at] += jnp.dot(
            edge_ref[0], side, precision=SPLIT, preferred_element_type=jnp.float32
        )
        sides.append(side)
    real, imag = adj_ref[0, 0], adj_ref[1, 0]
    at = 2 * ends
    sum_ref[at : at + 1] += jnp.sum(real * sides[0] + imag * sides[1], axis=0, keepdims=True)
    sum_ref[at + 1 : at + 2] += jnp.sum(real * sides[1] - imag * sides[0], axis=0, keepdims=True)


def absorb_body(in_ref, *refs):
    def read(part):
        return in_ref[:, 0, :, part * NB : (part + 1) * NB]

    absorb_rows(read, *refs)


def absorb_apart_body(spans, place_ref, *refs):
    in_refs, refs, rows_ref = refs[:spans], refs[spans:-1], refs[-1]
    for i, in_ref in enumerate(in_refs):
        for j in range(in_ref.shape[0]):
            rows_ref[partner(place_ref, j, i, spans)] = in_ref[j, 0]

    def read(part):
        return rows_ref[:, :, part * NB : (part + 1) * NB]

    absorb_rows(read, *refs)


def absorb(place, blocks, keep, edges, adjoint_modes, before):
    blocks = list(blocks)
    apart = place is not None
    _, variables, rows, modes = adjoint_modes.shape
    ends = edges.shape[1]
    grid_spec = pl.BlockSpec((2, 1, rows, modes), lambda v: (0, v, 0, 0))
    sums = pl.BlockSpec((GATHERED_ROWS, modes), lambda v: (0, 0))
    length, _, freqs, lanes = blocks[0].shape
    in_specs = [pl.BlockSpec((length, 1, freqs, lanes), lambda v: (0, v, 0, 0))] * len(blocks)
    in_specs += [
        pl.BlockSpec((modes,), lambda v: (0,)),
        pl.BlockSpec((1, ends, rows), lambda v: (v, 0, 0)),
        grid_spec,
        sums,
    ]
    operands = blocks + [keep, edges, adjoint_modes if apart else in_hbm(adjoint_modes), before]
    body, scratch = absorb_body, []
    if apart:
        operands = [place] + operands
        in_specs = [pl.BlockSpec(memory_space=pltpu.SMEM)] + in_specs
        body = functools.partial(absorb_apart_body, len(blocks))
        scratch = [pltpu.VMEM((rows, freqs, lanes), jnp.float32)]
    return pl.pallas_call(
        body,
        grid=(variables,),
        in_specs=in_specs,
        out_specs=[grid_spec, sums],
        out_shape=[
            jax.ShapeDtypeStruct((2, variables, rows, modes), jnp.float32),
            jax.ShapeDtypeStruct((GATHERED_ROWS, modes), jnp.float32),
        ],
        scratch_shapes=scratch,
        compiler_params=params(),
        name="absorb_apart" if apart else "absorb",
    )(*operands)


def solve_body(groups, *refs):
    side_refs, (up_ref, mask_ref, inverse_ref, out_ref) = refs[:groups], refs[groups:]
    _, variables, heights, lanes = out_ref.shape
    keep = kept_modes(mask_ref)
    for part in range(2):
        forced = [ref[part] for ref in side_refs]
        forced = forced[0] if groups == 1 else jnp.concatenate(forced, axis=1)
        side = forced + up_ref[part] * keep
        side = side.reshape(variables * heights, lanes)
        high = side.astype(jnp.bfloat16)
        low = (side - high.astype(jnp.float32)).astype(jnp.bfloat16)
        moved = jnp.dot(
            inverse_ref[...],
            jnp.concatenate([high, low, high], axis=0),
            preferred_element_type=jnp.float32,
        )
        out_ref[part] = moved.reshape(variables, heights, lanes)


def solve(sides, upstream, keep, inverse):
    _, variables, heights, modes = upstream.shape
    spec = pl.BlockSpec((2, variables, heights, NB), lambda i: (0, 0, 0, i))
    return pl.pallas_call(
        functools.partial(solve_body, len(sides)),
        grid=(modes // NB,),
        in_specs=[
            pl.BlockSpec((2, variables, side.shape[2], NB), lambda i: (0, 0, 0, i))
            for side in sides
        ]
        + [spec, pl.BlockSpec((NB,), lambda i: (i,)), whole(inverse)],
        out_specs=spec,
        out_shape=jax.ShapeDtypeStruct(upstream.shape, jnp.float32),
        compiler_params=params(),
        name="solve",
    )(*sides, in_hbm(upstream), keep, inverse)


def finish_body(walls, extent, solved_ref, *refs):
    bounds, refs = refs[:walls], refs[walls:]
    edges, refs = refs[:walls], refs[walls:]
    chain_ref, out_ref, shift_ref = refs
    _, variables, heights, lanes = out_ref.shape
    ends = 2 * variables
    pushed = []
    for part in range(2):
        at = slice(part * ends, (part + 1) * ends)
        everywhere = [ref[at] for ref in bounds]
        spare = chain_ref.shape[1] // 3 - walls * ends
        if spare:
            everywhere.append(jnp.zeros((spare, lanes), jnp.float32))
        everywhere = jnp.concatenate(everywhere, axis=0)
        high = everywhere.astype(jnp.bfloat16)
        low = (everywhere - high.astype(jnp.float32)).astype(jnp.bfloat16)
        moved = jnp.dot(
            chain_ref[...],
            jnp.concatenate([high, low, high], axis=0),
            preferred_element_type=jnp.float32,
        )
        pushed.append(moved[extent:])
        out_ref[part] = solved_ref[part] - moved[:extent].reshape(variables, heights, lanes)
    real = imag = weight = 0.0
    for wall in range(walls):
        at = slice(wall * ends, (wall + 1) * ends)
        push = [pushed[part][at] for part in range(2)]
        edge = [edges[wall][part * ends : (part + 1) * ends] for part in range(2)]
        row = 2 * ends
        squares = edges[wall][row : row + 1]
        taken = jnp.sum(edge[0] * push[0] + edge[1] * push[1], axis=0, keepdims=True)
        real = real + (bounds[wall][row : row + 1] - taken - squares)
        taken = jnp.sum(edge[0] * push[1] - edge[1] * push[0], axis=0, keepdims=True)
        imag = imag + (bounds[wall][row + 1 : row + 2] - taken)
        weight = weight + squares
    weight = weight + epsilon
    shift_ref[0:1] = imag / weight
    shift_ref[1:2] = -real / weight


def finish(solved, bounds, edges, chain):
    _, variables, heights, modes = solved.shape
    walls = len(bounds)
    lanes = min(2 * NB, modes)
    small = pl.BlockSpec((GATHERED_ROWS, lanes), lambda i: (0, i))
    spec = pl.BlockSpec((2, variables, heights, lanes), lambda i: (0, 0, 0, i))
    return pl.pallas_call(
        functools.partial(finish_body, walls, variables * heights),
        grid=(modes // lanes,),
        in_specs=[spec] + [small] * (2 * walls) + [whole(chain)],
        out_specs=[spec, pl.BlockSpec((2, lanes), lambda i: (0, i))],
        out_shape=[
            jax.ShapeDtypeStruct(solved.shape, jnp.float32),
            jax.ShapeDtypeStruct((2, modes), jnp.float32),
        ],
        compiler_params=params(),
        name="finish",
    )(solved, *bounds, *edges, chain)


def around(block, axis):
    count = lax.axis_size(axis)
    return [block] + [
        lax.ppermute(block, axis, [(i, (i + d) % count) for i in range(count)])
        for d in range(1, count)
    ]


PACKED_ROWS = 16


def pack_body(*refs):
    in_refs, out_ref = refs[:-1], refs[-1]
    out_ref[...] = jnp.zeros(out_ref.shape, jnp.float32)
    for i, ref in enumerate(in_refs):
        rows, columns = ref.shape[1:]
        out_ref[i, :rows, :columns] = ref[0]


def pack(parts):
    return pl.pallas_call(
        pack_body,
        out_shape=jax.ShapeDtypeStruct((len(parts), PACKED_ROWS, 128), jnp.float32),
        name="pack",
    )(*parts)


def upper_bits(value):
    return value.astype(jnp.bfloat16).astype(jnp.float32)


def split_columns(matrix):
    high = upper_bits(matrix)
    return jnp.concatenate([high, high, matrix - high], axis=1).astype(jnp.bfloat16)


def constants_body(cuts, variables, walls, place_ref, inverse_ref, *refs):
    packed, refs = refs[:walls], refs[walls:]
    turned_ref, split_ref, rows_ref = refs[:3]
    row_refs, (chain_ref, all_ref, step_ref) = refs[3 : 3 + len(cuts)], refs[3 + len(cuts) :]
    extent = inverse_ref.shape[0]
    heights = extent // variables
    ends = 2 * variables
    matrix = inverse_ref[...]
    turned = matrix.T
    turned_ref[...] = turned
    split_ref[...] = split_columns(matrix)
    for end, point in enumerate((0, heights - 1)):
        for w in range(variables):
            at = w * heights + point
            row = end * variables + w
            rows_ref[row : row + 1] = matrix[at : at + 1]
            for v in range(variables):
                part = matrix[at : at + 1, v * heights : (v + 1) * heights]
                for cut, row_ref in zip(cuts, row_refs):
                    row_ref[v, row : row + 1] = part[:, cut]

    def dot(a, b):
        return jnp.dot(a, b, precision=FULL, preferred_element_type=jnp.float32)

    size = walls * PACKED_ROWS
    for d in range(walls):
        all_ref[(place_ref[0] - d + walls) % walls] = packed[d][...]

    def small(j, kind):
        return all_ref[j, kind][:, :PACKED_ROWS]

    row = lax.broadcasted_iota(jnp.int32, (PACKED_ROWS, size), 0)
    column = lax.broadcasted_iota(jnp.int32, (PACKED_ROWS, size), 1)
    units = []
    for j in range(walls):
        d = (place_ref[0] - j + walls) % walls
        hit = (column == d * ends + row) & (row < ends)
        units.append(jnp.where(hit, 1.0, 0.0))
    ahead = [units[0]]
    for j in range(1, walls):
        ahead.append(units[j] - dot(small(j, 2), ahead[j - 1]))
    interface = [None] * walls
    interface[-1] = dot(small(walls - 1, 4), ahead[-1])
    for j in range(walls - 2, -1, -1):
        interface[j] = dot(small(j, 4), ahead[j] - dot(small(j, 3), interface[j + 1]))
    for j in range(walls):
        none = jnp.zeros((variables, size), jnp.float32)
        under, over = none, none
        if j > 0:
            last = jnp.concatenate([interface[j - 1][variables:], none], axis=0)[:PACKED_ROWS]
            under = dot(small(j, 0), last)[:variables]
        if j < walls - 1:
            over = dot(small(j, 1), interface[j + 1])[:variables]
        step_ref[(place_ref[0] - j + walls) % walls] = jnp.concatenate(
            [under, over, jnp.zeros((PACKED_ROWS - ends, size), jnp.float32)], axis=0
        )
    pushes = [step_ref[d][:ends] for d in range(walls)]
    edge = [turned[v * heights : v * heights + 1] for v in range(variables)]
    edge += [turned[(v + 1) * heights - 1 : (v + 1) * heights] for v in range(variables)]
    edge.append(jnp.zeros((PACKED_ROWS - ends, extent), jnp.float32))
    edge = jnp.concatenate(edge, axis=0).T
    own = dot(edge, step_ref[0])
    spare = chain_ref.shape[0] - extent - walls * ends
    full = [own] + pushes
    if spare:
        full.append(jnp.zeros((spare, size), jnp.float32))
    full = jnp.concatenate(full, axis=0)
    chain_ref[...] = split_columns(full)


def constants(place, inverse, packed, cuts, variables):
    walls = len(packed)
    extent = inverse.shape[0]
    heights = extent // variables
    ends = 2 * variables
    lengths = [cut.stop - cut.start for cut in cuts]
    size = walls * PACKED_ROWS
    rows = extent + walls * ends + (-walls * ends) % 16
    f32 = jnp.float32
    return pl.pallas_call(
        functools.partial(constants_body, cuts, variables, walls),
        in_specs=[pl.BlockSpec(memory_space=pltpu.SMEM)]
        + [pl.BlockSpec(memory_space=pltpu.VMEM)] * (1 + walls),
        out_shape=[
            jax.ShapeDtypeStruct((extent, extent), f32),
            jax.ShapeDtypeStruct((extent, 3 * extent), jnp.bfloat16),
            jax.ShapeDtypeStruct((ends, extent), f32),
        ]
        + [jax.ShapeDtypeStruct((variables, ends, n), f32) for n in lengths]
        + [jax.ShapeDtypeStruct((rows, 3 * size), jnp.bfloat16)],
        scratch_shapes=[
            pltpu.VMEM((walls,) + packed[0].shape, f32),
            pltpu.VMEM((walls, PACKED_ROWS, size), f32),
        ],
        compiler_params=params(),
        name="constants",
    )(place, inverse, *packed)


def local(
    amplitudes,
    upstream,
    harmonic_mask,
    quadratic_coefficients,
    slab_inverse,
    lower_coupling,
    upper_coupling,
    reduced_lower,
    reduced_upper,
    reduced_pivot,
):
    _, variables, heights, modes = amplitudes.shape
    axes = ("freq", "span")
    groups, spans = lax.axis_size("freq"), lax.axis_size("span")
    devices = groups * spans
    points = heights // devices
    apart = points > 1 and groups & (groups - 1) == 0 and spans & (spans - 1) == 0
    edge_at = heights - devices if apart else heights
    cuts = [slice(0, edge_at)] + ([slice(edge_at, heights)] if apart else [])
    keep = harmonic_mask
    place = jnp.stack([lax.axis_index("freq"), lax.axis_index("span")]).astype(jnp.int32)
    wall = lax.axis_index("wall").reshape(1).astype(jnp.int32)
    transforms = tables()
    coefficients = quadratic_coefficients.reshape(variables * variables, variables)

    def exchange(block):
        return lax.all_to_all(block, axes, split_axis=0, concat_axis=0, tiled=True)

    def swap(blocks, axis, only=None):
        count = len(blocks)
        return [
            lax.ppermute(block, axis, [(at, at ^ i) for at in range(count)])
            if i and (only is None or i in only)
            else block
            for i, block in enumerate(blocks)
        ]

    def regroup(blocks):
        return [jnp.stack([block[j] for block in blocks]) for j in range(blocks[0].shape[0])]

    far = {spans // 2}
    main = prepare(amplitudes, keep, cuts[0])
    if apart:
        main, amplitudes = lax.optimization_barrier((main, amplitudes))
        sent = prepare_apart(place, amplitudes, keep, cuts[1], groups, spans)
        arrived = swap(regroup(swap(sent, "freq")), "span", set(range(spans)) - far)
    main = exchange(main)

    if apart:
        main, arrived = lax.optimization_barrier((main, arrived))
        arrived = swap(arrived, "span", far)
    size = edge_at // devices
    shape = main.shape
    main = nonlinear(main.reshape((devices, size) + shape[1:]), coefficients, transforms)
    main = main.reshape(shape)
    if apart:
        main, arrived[spans // 2] = lax.optimization_barrier((main, arrived[spans // 2]))
    main = exchange(main)
    inverse = slab_inverse[0]
    parts = (lower_coupling, upper_coupling, reduced_lower, reduced_upper, reduced_pivot)
    packed = around(pack(parts), "wall")
    turned, split, edge_rows, *end_rows, chain = constants(wall, inverse, packed, cuts, variables)
    *adjoint_modes, edge, sums = base(amplitudes, upstream, keep, edge_rows, turned, cuts)
    edges = around(edge, "wall")
    if apart:
        forced = nonlinear_apart(place, arrived, coefficients, transforms)
        returned = regroup(swap(forced, "freq"))
        held = (returned, split, end_rows, chain, adjoint_modes, edges, sums)
        held = lax.optimization_barrier(held)
        returned, split, end_rows, chain, adjoint_modes, edges, sums = held
        returned = swap(returned, "span")

    sides = [None] * len(cuts)
    sides[0], sums = absorb(None, [main], keep, end_rows[0], adjoint_modes[0], sums)
    if apart:
        sides[1], sums = absorb(place, returned, keep, end_rows[1], adjoint_modes[1], sums)
    bounds = around(sums, "wall")
    solved = solve(sides, upstream, keep, split)
    new_amplitudes, wavenumber_shift = finish(solved, bounds, edges, chain)
    return (new_amplitudes, wavenumber_shift)


def solution(mesh):
    placed = (
        P(None, None, "wall", ("freq", "span")),
        P(None, None, "wall", ("freq", "span")),
        P(("freq", "span")),
        P(),
        P("wall", None, None),
        P("wall", None, None),
        P("wall", None, None),
        P("wall", None, None),
        P("wall", None, None),
        P("wall", None, None),
    )
    return jax.shard_map(
        local,
        mesh=mesh,
        in_specs=placed,
        out_specs=(P(None, None, "wall", ("freq", "span")), P(None, ("freq", "span"))),
        check_vma=False,
    )
```

```python
import functools
import math

import jax
import jax.numpy as jnp
import ml_dtypes
import numpy as np
from jax import lax
from jax.experimental import pallas as pl
from jax.experimental.pallas import tpu as pltpu
from jax.sharding import PartitionSpec as P

NF = 128
NB = 256

epsilon = 1e-06

SPLIT = lax.Precision.HIGH
FULL = lax.Precision.HIGHEST
GATHERED_ROWS = 24


def tables():
    def turns(length):
        counter = np.arange(length)
        angles = (counter[:, None] * counter[None, :] % length) * (2.0 * math.pi / length)
        return np.cos(angles), np.sin(angles)

    cos_time, sin_time = turns(NF)
    cos_span, sin_span = turns(NB)
    scale = 1.0 / math.sqrt(NF * NB)
    out = (
        (np.block([[cos_time, -sin_time], [sin_time, cos_time]]), 1),
        (np.concatenate([cos_span, -sin_span], 0) * scale, 0),
        (np.concatenate([cos_span, -sin_span], 1) * scale, 0),
        (np.block([[cos_time, sin_time], [-sin_time, cos_time]]), 1),
    )

    def split(table, axis):
        high = table.astype(ml_dtypes.bfloat16)
        low = (table - high.astype(np.float64)).astype(ml_dtypes.bfloat16)
        return jnp.asarray(np.concatenate([high, high, low], axis))

    return [split(table, axis) for table, axis in out]


def params(megabytes=16):
    return pltpu.CompilerParams(vmem_limit_bytes=megabytes * 1024 * 1024)


def whole(array):
    zeros = (0,) * len(array.shape)
    return pl.BlockSpec(array.shape, lambda *_: zeros)


def in_hbm(array):
    return pltpu.with_memory_space_constraint(array, pltpu.HBM)


def kept_modes(mask_ref):
    return mask_ref[...].astype(jnp.float32).reshape(1, -1)


def row_step(rows):
    return rows // 2 if rows % 16 == 0 and rows > 16 else rows


def prepare_body(x_ref, mask_ref, out_ref):
    keep = kept_modes(mask_ref)
    rows, variables, freqs, _ = out_ref.shape
    for v in range(variables):
        for part in range(2):
            kept = x_ref[part, v] * keep
            out_ref[:, v, :, part * NB : (part + 1) * NB] = kept.reshape(rows, freqs, NB)


def prepare(amplitudes, keep, cut):
    _, variables, _, modes = amplitudes.shape
    freqs = modes // NB
    rows = cut.stop - cut.start
    step = row_step(rows)
    at = cut.start // step
    return pl.pallas_call(
        prepare_body,
        grid=(rows // step,),
        in_specs=[
            pl.BlockSpec((2, variables, step, modes), lambda r: (0, 0, at + r, 0)),
            pl.BlockSpec((modes,), lambda r: (0,)),
        ],
        out_specs=pl.BlockSpec((step, variables, freqs, 2 * NB), lambda r: (r, 0, 0, 0)),
        out_shape=pltpu.HBM((rows, variables, freqs, 2 * NB), jnp.float32),
        compiler_params=params(24),
        name="prepare",
    )(in_hbm(amplitudes), in_hbm(keep))


def partner(place_ref, j, i, spans):
    return (place_ref[0] ^ j) * spans + (place_ref[1] ^ i)


def prepare_apart_body(place_ref, x_ref, mask_ref, *refs):
    out_refs, rows_ref = refs[:-1], refs[-1]
    keep = kept_modes(mask_ref)
    rows, freqs, _ = rows_ref.shape
    spans = out_refs[0].shape[0]
    for part in range(2):
        kept = x_ref[part, 0] * keep
        rows_ref[:, :, part * NB : (part + 1) * NB] = kept.reshape(rows, freqs, NB)
    for j, out_ref in enumerate(out_refs):
        for i in range(spans):
            out_ref[i, 0] = rows_ref[partner(place_ref, j, i, spans)]


def prepare_apart(place, amplitudes, keep, cut, groups, spans):
    _, variables, _, modes = amplitudes.shape
    freqs = modes // NB
    rows = cut.stop - cut.start
    at = cut.start // rows
    return pl.pallas_call(
        prepare_apart_body,
        grid=(variables,),
        in_specs=[
            pl.BlockSpec(memory_space=pltpu.SMEM),
            pl.BlockSpec((2, 1, rows, modes), lambda v: (0, v, at, 0)),
            pl.BlockSpec((modes,), lambda v: (0,)),
        ],
        out_specs=[pl.BlockSpec((spans, 1, freqs, 2 * NB), lambda v: (0, v, 0, 0))] * groups,
        out_shape=[jax.ShapeDtypeStruct((spans, variables, freqs, 2 * NB), jnp.float32)] * groups,
        scratch_shapes=[pltpu.VMEM((rows, freqs, 2 * NB), jnp.float32)],
        compiler_params=params(),
        name="prepare_apart",
    )(place, in_hbm(amplitudes), keep)


def halves(value):
    high = value.astype(jnp.bfloat16)
    return high, (value - high.astype(jnp.float32)).astype(jnp.bfloat16)


def table_times(table, value):
    high, low = halves(value)
    value = jnp.concatenate([high, low, high], axis=0)
    return jnp.dot(table, value, preferred_element_type=jnp.float32)


def times_table(value, table):
    high, low = halves(value)
    value = jnp.concatenate([high, low, high], axis=1)
    return jnp.dot(value, table, preferred_element_type=jnp.float32)


def transform(read, write, q_ref, table_refs, field_ref, force_ref):
    wi_ref, ei_ref, ef_ref, wf_ref = table_refs
    variables = field_ref.shape[0]
    for v in range(variables):
        modes = read(v)
        stacked = jnp.concatenate([modes[:, :NB], modes[:, NB:]], axis=0)
        turned = table_times(wi_ref[...], stacked)
        beside = jnp.concatenate([turned[:NF], turned[NF:]], axis=1)
        field_ref[v] = times_table(beside, ei_ref[...])
    pairs = [(a, b) for a in range(variables) for b in range(a + 1, variables)]
    weights = [
        [q_ref[w * variables + a, b] + q_ref[w * variables + b, a] for a, b in pairs]
        for w in range(variables)
    ]
    step = 8
    for row in range(0, NF, step):
        at = slice(row, row + step)
        values = [field_ref[v, at] for v in range(variables)]
        total = [None] * variables
        for i, (a, b) in enumerate(pairs):
            product = values[a] * values[b]
            for w in range(variables):
                term = weights[w][i] * product
                total[w] = term if total[w] is None else total[w] + term
        for w in range(variables):
            force_ref[w, at] = total[w]
    for w in range(variables):
        spread = times_table(force_ref[w], ef_ref[...])
        stacked = jnp.concatenate([spread[:, :NB], spread[:, NB:]], axis=0)
        turned = table_times(wf_ref[...], stacked)
        for part in range(2):
            write(w, part, turned[part * NF : (part + 1) * NF])


def nonlinear_body(q_ref, in_ref, *refs):
    table_refs, out_ref, work_refs = refs[:4], refs[4], refs[5:]
    devices, _, _, freqs, _ = in_ref.shape

    def read(v):
        return in_ref[:, 0, v].reshape(NF, 2 * NB)

    def write(w, part, piece):
        at = slice(part * NB, (part + 1) * NB)
        out_ref[:, 0, w, :, at] = piece.reshape(devices, freqs, NB)

    transform(read, write, q_ref, table_refs, *work_refs)


def work_shapes(variables):
    return [pltpu.VMEM((variables, NF, NB), jnp.float32)] * 2


def nonlinear_cost(points, variables):
    return pl.CostEstimate(
        flops=points * variables * 12 * NF * NB * (NF + NB) * 2,
        bytes_accessed=points * variables * NF * NB * 16,
        transcendentals=0,
    )


def nonlinear(block, coefficients, transforms):
    devices, points, variables, freqs, lanes = block.shape
    spec = pl.BlockSpec((devices, 1, variables, freqs, lanes), lambda j: (0, j, 0, 0, 0))
    return pl.pallas_call(
        nonlinear_body,
        grid=(points,),
        in_specs=[pl.BlockSpec(memory_space=pltpu.SMEM), spec] + [whole(t) for t in transforms],
        out_specs=spec,
        out_shape=pltpu.HBM(block.shape, jnp.float32),
        scratch_shapes=work_shapes(variables),
        compiler_params=params(24),
        cost_estimate=nonlinear_cost(points, variables),
        name="nonlinear",
    )(coefficients, block, *[in_hbm(table) for table in transforms])


def nonlinear_apart_body(groups, spans, place_ref, q_ref, *refs):
    in_refs, refs = refs[:spans], refs[spans:]
    table_refs, refs = refs[:4], refs[4:]
    out_refs, refs = refs[:groups], refs[groups:]
    rows_ref, work_refs = refs[0], refs[1:]
    devices, _, freqs, _ = rows_ref.shape
    for j in range(groups):
        for i in range(spans):
            rows_ref[partner(place_ref, j, i, spans)] = in_refs[i][j]

    def read(v):
        return rows_ref[:, v].reshape(NF, 2 * NB)

    def write(w, part, piece):
        at = slice(part * NB, (part + 1) * NB)
        rows_ref[:, w, :, at] = piece.reshape(devices, freqs, NB)

    transform(read, write, q_ref, table_refs, *work_refs)
    for j in range(groups):
        for i in range(spans):
            out_refs[j][i] = rows_ref[partner(place_ref, j, i, spans)]


def nonlinear_apart(place, blocks, coefficients, transforms):
    spans = len(blocks)
    groups, variables, freqs, lanes = blocks[0].shape
    result = jax.ShapeDtypeStruct((spans, variables, freqs, lanes), jnp.float32)
    smem = pl.BlockSpec(memory_space=pltpu.SMEM)
    return pl.pallas_call(
        functools.partial(nonlinear_apart_body, groups, spans),
        grid=(1,),
        in_specs=[smem, smem]
        + [whole(block) for block in blocks]
        + [whole(table) for table in transforms],
        out_specs=[whole(result)] * groups,
        out_shape=[result] * groups,
        scratch_shapes=[pltpu.VMEM((groups * spans, variables, freqs, lanes), jnp.float32)]
        + work_shapes(variables),
        compiler_params=params(24),
        cost_estimate=nonlinear_cost(1, variables),
        name="nonlinear_apart",
    )(place, coefficients, *blocks, *[in_hbm(table) for table in transforms])


def base_body(cuts, x_ref, up_ref, mask_ref, edge_rows_ref, turned_ref, *refs):
    out_refs, (edge_ref, sum_ref) = refs[: len(cuts)], refs[len(cuts) :]
    _, variables, heights, lanes = x_ref.shape
    extent = variables * heights
    ends = 2 * variables
    keep = kept_modes(mask_ref)
    squares, moved, sides = 0.0, [], []
    for part in range(2):
        kept = x_ref[part].reshape(extent, lanes) * keep
        squares = squares + total(kept * kept)
        moved.append(
            jnp.dot(turned_ref[...], kept, precision=SPLIT, preferred_element_type=jnp.float32)
        )
        grid = moved[part].reshape(variables, heights, lanes)
        for cut, out_ref in zip(cuts, out_refs):
            out_ref[part] = grid[:, cut]
        sides.append(up_ref[part].reshape(extent, lanes) * keep)
        sum_ref[part * ends : (part + 1) * ends] = jnp.dot(
            edge_rows_ref[...], sides[part], precision=SPLIT, preferred_element_type=jnp.float32
        )
        for end, point in enumerate((0, heights - 1)):
            for v in range(variables):
                row = part * ends + end * variables + v
                at = v * heights + point
                edge_ref[row : row + 1] = moved[part][at : at + 1]
    row = 2 * ends
    none = jnp.zeros((GATHERED_ROWS - row - 1, lanes), jnp.float32)
    edge_ref[row : row + 1] = squares
    edge_ref[row + 1 :] = none
    sum_ref[row : row + 1] = total(moved[0] * sides[0] + moved[1] * sides[1])
    sum_ref[row + 1 : row + 2] = total(moved[0] * sides[1] - moved[1] * sides[0])
    sum_ref[row + 2 :] = none[1:]


def total(value):
    return jnp.sum(value, axis=0, keepdims=True)


def base(amplitudes, upstream, keep, edge_rows, turned, cuts):
    _, variables, heights, modes = amplitudes.shape
    lengths = [cut.stop - cut.start for cut in cuts]
    shapes = [(2, variables, rows, modes) for rows in lengths]
    spec = pl.BlockSpec((2, variables, heights, NB), lambda i: (0, 0, 0, i))
    small = pl.BlockSpec((GATHERED_ROWS, NB), lambda i: (0, i))
    small_shape = jax.ShapeDtypeStruct((GATHERED_ROWS, modes), jnp.float32)
    return pl.pallas_call(
        functools.partial(base_body, cuts),
        grid=(modes // NB,),
        in_specs=[spec] * 2
        + [pl.BlockSpec((NB,), lambda i: (i,)), whole(edge_rows), whole(turned)],
        out_specs=[
            pl.BlockSpec((2, variables, rows, NB), lambda i: (0, 0, 0, i)) for rows in lengths
        ]
        + [small] * 2,
        out_shape=[pltpu.HBM(shapes[0], jnp.float32)]
        + [jax.ShapeDtypeStruct(shape, jnp.float32) for shape in shapes[1:]]
        + [small_shape] * 2,
        compiler_params=params(24),
        name="base",
    )(in_hbm(amplitudes), in_hbm(upstream), keep, edge_rows, turned)


def absorb_rows(read, mask_ref, edge_ref, adj_ref, before_ref, out_ref, sum_ref):
    _, variables, rows, lanes = out_ref.shape
    ends = edge_ref.shape[1]
    keep = kept_modes(mask_ref)

    @pl.when(pl.program_id(0) == 0)
    def _():
        sum_ref[...] = before_ref[...]

    for v in range(variables):
        for part in range(2):
            out_ref[part, v] = read(v, part).reshape(rows, lanes) * keep
    sides = [out_ref[part].reshape(variables * rows, lanes) for part in range(2)]
    for part in range(2):
        at = slice(part * ends, (part + 1) * ends)
        sum_ref[at] += jnp.dot(
            edge_ref[0], sides[part], precision=SPLIT, preferred_element_type=jnp.float32
        )
    real, imag = (adj_ref[part].reshape(variables * rows, lanes) for part in range(2))
    at = 2 * ends
    sum_ref[at : at + 1] += total(real * sides[0] + imag * sides[1])
    sum_ref[at + 1 : at + 2] += total(real * sides[1] - imag * sides[0])


def absorb_body(in_ref, *refs):
    def read(v, part):
        return in_ref[:, v, :, part * NB : (part + 1) * NB]

    absorb_rows(read, *refs)


def absorb_apart_body(spans, place_ref, *refs):
    in_refs, refs, rows_ref = refs[:spans], refs[spans:-1], refs[-1]
    for i, in_ref in enumerate(in_refs):
        for j in range(in_ref.shape[0]):
            rows_ref[partner(place_ref, j, i, spans)] = in_ref[j]

    def read(v, part):
        return rows_ref[:, v, :, part * NB : (part + 1) * NB]

    absorb_rows(read, *refs)


def absorb(place, blocks, keep, edges, adjoint_modes, before):
    blocks = list(blocks)
    apart = place is not None
    _, variables, rows, modes = adjoint_modes.shape
    steps, ends, width = edges.shape
    step = rows // steps
    grid_spec = pl.BlockSpec((2, variables, step, modes), lambda r: (0, 0, r, 0))
    sums = pl.BlockSpec((GATHERED_ROWS, modes), lambda r: (0, 0))
    _, _, freqs, lanes = blocks[0].shape
    operands = blocks + [keep, edges, adjoint_modes if apart else in_hbm(adjoint_modes), before]
    in_specs = [
        whole(block)
        if apart
        else pl.BlockSpec((step, variables, freqs, lanes), lambda r: (r, 0, 0, 0))
        for block in blocks
    ] + [
        pl.BlockSpec((modes,), lambda r: (0,)),
        pl.BlockSpec((1, ends, width), lambda r: (r, 0, 0)),
        grid_spec,
        sums,
    ]
    body, scratch = absorb_body, []
    if apart:
        operands = [place] + operands
        in_specs = [pl.BlockSpec(memory_space=pltpu.SMEM)] + in_specs
        body = functools.partial(absorb_apart_body, len(blocks))
        scratch = [pltpu.VMEM((rows, variables, freqs, lanes), jnp.float32)]
    return pl.pallas_call(
        body,
        grid=(steps,),
        in_specs=in_specs,
        out_specs=[grid_spec, sums],
        out_shape=[
            jax.ShapeDtypeStruct((2, variables, rows, modes), jnp.float32),
            jax.ShapeDtypeStruct((GATHERED_ROWS, modes), jnp.float32),
        ],
        scratch_shapes=scratch,
        compiler_params=params(24),
        name="absorb_apart" if apart else "absorb",
    )(*operands)


def solve_body(groups, *refs):
    side_refs, (up_ref, mask_ref, inverse_ref, out_ref) = refs[:groups], refs[groups:]
    _, variables, heights, lanes = out_ref.shape
    keep = kept_modes(mask_ref)
    for part in range(2):
        forced = [ref[part] for ref in side_refs]
        forced = forced[0] if groups == 1 else jnp.concatenate(forced, axis=1)
        side = forced + up_ref[part] * keep
        side = side.reshape(variables * heights, lanes)
        moved = table_times(inverse_ref[...], side)
        out_ref[part] = moved.reshape(variables, heights, lanes)


def solve(sides, upstream, keep, inverse):
    _, variables, heights, modes = upstream.shape
    lanes = min(2 * NB, modes)
    spec = pl.BlockSpec((2, variables, heights, lanes), lambda i: (0, 0, 0, i))
    return pl.pallas_call(
        functools.partial(solve_body, len(sides)),
        grid=(modes // lanes,),
        in_specs=[
            pl.BlockSpec((2, variables, side.shape[2], lanes), lambda i: (0, 0, 0, i))
            for side in sides
        ]
        + [spec, pl.BlockSpec((lanes,), lambda i: (i,)), whole(inverse)],
        out_specs=spec,
        out_shape=jax.ShapeDtypeStruct(upstream.shape, jnp.float32),
        compiler_params=params(24),
        name="solve",
    )(*sides, in_hbm(upstream), keep, inverse)


def finish_body(walls, extent, solved_ref, *refs):
    bounds, refs = refs[:walls], refs[walls:]
    edges, refs = refs[:walls], refs[walls:]
    chain_ref, out_ref, shift_ref = refs
    _, variables, heights, lanes = out_ref.shape
    ends = 2 * variables
    pushed = []
    for part in range(2):
        at = slice(part * ends, (part + 1) * ends)
        everywhere = [ref[at] for ref in bounds]
        spare = chain_ref.shape[1] // 3 - walls * ends
        if spare:
            everywhere.append(jnp.zeros((spare, lanes), jnp.float32))
        everywhere = jnp.concatenate(everywhere, axis=0)
        moved = table_times(chain_ref[...], everywhere)
        pushed.append(moved[extent:])
        out_ref[part] = solved_ref[part] - moved[:extent].reshape(variables, heights, lanes)
    real = imag = weight = 0.0
    for wall in range(walls):
        at = slice(wall * ends, (wall + 1) * ends)
        push = [pushed[part][at] for part in range(2)]
        edge = [edges[wall][part * ends : (part + 1) * ends] for part in range(2)]
        row = 2 * ends
        squares = edges[wall][row : row + 1]
        taken = jnp.sum(edge[0] * push[0] + edge[1] * push[1], axis=0, keepdims=True)
        real = real + (bounds[wall][row : row + 1] - taken - squares)
        taken = jnp.sum(edge[0] * push[1] - edge[1] * push[0], axis=0, keepdims=True)
        imag = imag + (bounds[wall][row + 1 : row + 2] - taken)
        weight = weight + squares
    weight = weight + epsilon
    shift_ref[0:1] = imag / weight
    shift_ref[1:2] = -real / weight


def finish(solved, bounds, edges, chain):
    _, variables, heights, modes = solved.shape
    walls = len(bounds)
    lanes = min(2 * NB, modes)
    small = pl.BlockSpec((GATHERED_ROWS, lanes), lambda i: (0, i))
    spec = pl.BlockSpec((2, variables, heights, lanes), lambda i: (0, 0, 0, i))
    return pl.pallas_call(
        functools.partial(finish_body, walls, variables * heights),
        grid=(modes // lanes,),
        in_specs=[spec] + [small] * (2 * walls) + [whole(chain)],
        out_specs=[spec, pl.BlockSpec((2, lanes), lambda i: (0, i))],
        out_shape=[
            jax.ShapeDtypeStruct(solved.shape, jnp.float32),
            jax.ShapeDtypeStruct((2, modes), jnp.float32),
        ],
        compiler_params=params(),
        name="finish",
    )(solved, *bounds, *edges, chain)


def around(block, axis):
    count = lax.axis_size(axis)
    return [block] + [
        lax.ppermute(block, axis, [(i, (i + d) % count) for i in range(count)])
        for d in range(1, count)
    ]


PACKED_ROWS = 16


def pack_body(*refs):
    in_refs, out_ref = refs[:-1], refs[-1]
    out_ref[...] = jnp.zeros(out_ref.shape, jnp.float32)
    for i, ref in enumerate(in_refs):
        rows, columns = ref.shape[1:]
        out_ref[i, :rows, :columns] = ref[0]


def pack(parts):
    return pl.pallas_call(
        pack_body,
        out_shape=jax.ShapeDtypeStruct((len(parts), PACKED_ROWS, 128), jnp.float32),
        name="pack",
    )(*parts)


def upper_bits(value):
    return value.astype(jnp.bfloat16).astype(jnp.float32)


def split_columns(matrix):
    high = upper_bits(matrix)
    return jnp.concatenate([high, high, matrix - high], axis=1).astype(jnp.bfloat16)


def constants_body(cuts, variables, walls, place_ref, inverse_ref, *refs):
    packed, refs = refs[:walls], refs[walls:]
    turned_ref, split_ref, rows_ref = refs[:3]
    row_refs, (chain_ref, all_ref, step_ref) = refs[3 : 3 + len(cuts)], refs[3 + len(cuts) :]
    extent = inverse_ref.shape[0]
    heights = extent // variables
    ends = 2 * variables
    matrix = inverse_ref[...]
    turned = matrix.T
    turned_ref[...] = turned
    split_ref[...] = split_columns(matrix)
    for end, point in enumerate((0, heights - 1)):
        for w in range(variables):
            at = w * heights + point
            row = end * variables + w
            rows_ref[row : row + 1] = matrix[at : at + 1]
    ends_rows = rows_ref[...]
    for cut, row_ref in zip(cuts, row_refs):
        step = row_step(cut.stop - cut.start)
        for r in range(row_ref.shape[0]):
            at = cut.start + r * step
            pieces = [
                ends_rows[:, v * heights + at : v * heights + at + step] for v in range(variables)
            ]
            row_ref[r] = jnp.concatenate(pieces, axis=1)

    def dot(a, b):
        return jnp.dot(a, b, precision=FULL, preferred_element_type=jnp.float32)

    size = walls * PACKED_ROWS
    for d in range(walls):
        all_ref[(place_ref[0] - d + walls) % walls] = packed[d][...]

    def small(j, kind):
        return all_ref[j, kind][:, :PACKED_ROWS]

    row = lax.broadcasted_iota(jnp.int32, (PACKED_ROWS, size), 0)
    column = lax.broadcasted_iota(jnp.int32, (PACKED_ROWS, size), 1)
    units = []
    for j in range(walls):
        d = (place_ref[0] - j + walls) % walls
        hit = (column == d * ends + row) & (row < ends)
        units.append(jnp.where(hit, 1.0, 0.0))
    ahead = [units[0]]
    for j in range(1, walls):
        ahead.append(units[j] - dot(small(j, 2), ahead[j - 1]))
    interface = [None] * walls
    interface[-1] = dot(small(walls - 1, 4), ahead[-1])
    for j in range(walls - 2, -1, -1):
        interface[j] = dot(small(j, 4), ahead[j] - dot(small(j, 3), interface[j + 1]))
    for j in range(walls):
        none = jnp.zeros((variables, size), jnp.float32)
        under, over = none, none
        if j > 0:
            last = jnp.concatenate([interface[j - 1][variables:], none], axis=0)[:PACKED_ROWS]
            under = dot(small(j, 0), last)[:variables]
        if j < walls - 1:
            over = dot(small(j, 1), interface[j + 1])[:variables]
        step_ref[(place_ref[0] - j + walls) % walls] = jnp.concatenate(
            [under, over, jnp.zeros((PACKED_ROWS - ends, size), jnp.float32)], axis=0
        )
    pushes = [step_ref[d][:ends] for d in range(walls)]
    edge = [turned[v * heights : v * heights + 1] for v in range(variables)]
    edge += [turned[(v + 1) * heights - 1 : (v + 1) * heights] for v in range(variables)]
    edge.append(jnp.zeros((PACKED_ROWS - ends, extent), jnp.float32))
    edge = jnp.concatenate(edge, axis=0).T
    own = dot(edge, step_ref[0])
    spare = chain_ref.shape[0] - extent - walls * ends
    full = [own] + pushes
    if spare:
        full.append(jnp.zeros((spare, size), jnp.float32))
    full = jnp.concatenate(full, axis=0)
    chain_ref[...] = split_columns(full)


def constants(place, inverse, packed, cuts, variables):
    walls = len(packed)
    extent = inverse.shape[0]
    heights = extent // variables
    ends = 2 * variables
    lengths = [cut.stop - cut.start for cut in cuts]
    size = walls * PACKED_ROWS
    rows = extent + walls * ends + (-walls * ends) % 16
    f32 = jnp.float32
    return pl.pallas_call(
        functools.partial(constants_body, cuts, variables, walls),
        in_specs=[pl.BlockSpec(memory_space=pltpu.SMEM)]
        + [pl.BlockSpec(memory_space=pltpu.VMEM)] * (1 + walls),
        out_shape=[
            jax.ShapeDtypeStruct((extent, extent), f32),
            jax.ShapeDtypeStruct((extent, 3 * extent), jnp.bfloat16),
            jax.ShapeDtypeStruct((ends, extent), f32),
        ]
        + [
            jax.ShapeDtypeStruct((n // row_step(n), ends, variables * row_step(n)), f32)
            for n in lengths
        ]
        + [jax.ShapeDtypeStruct((rows, 3 * size), jnp.bfloat16)],
        scratch_shapes=[
            pltpu.VMEM((walls,) + packed[0].shape, f32),
            pltpu.VMEM((walls, PACKED_ROWS, size), f32),
        ],
        compiler_params=params(),
        name="constants",
    )(place, inverse, *packed)


def local(
    amplitudes,
    upstream,
    harmonic_mask,
    quadratic_coefficients,
    slab_inverse,
    lower_coupling,
    upper_coupling,
    reduced_lower,
    reduced_upper,
    reduced_pivot,
):
    _, variables, heights, modes = amplitudes.shape
    axes = ("freq", "span")
    groups, spans = lax.axis_size("freq"), lax.axis_size("span")
    devices = groups * spans
    points = heights // devices
    apart = points > 1 and groups & (groups - 1) == 0 and spans & (spans - 1) == 0
    edge_at = heights - devices if apart else heights
    cuts = [slice(0, edge_at)] + ([slice(edge_at, heights)] if apart else [])
    keep = harmonic_mask
    place = jnp.stack([lax.axis_index("freq"), lax.axis_index("span")]).astype(jnp.int32)
    wall = lax.axis_index("wall").reshape(1).astype(jnp.int32)
    transforms = tables()
    coefficients = quadratic_coefficients.reshape(variables * variables, variables)

    def exchange(block):
        return lax.all_to_all(block, axes, split_axis=0, concat_axis=0, tiled=True)

    def swap(blocks, axis, only=None):
        count = len(blocks)
        return [
            lax.ppermute(block, axis, [(at, at ^ i) for at in range(count)])
            if i and (only is None or i in only)
            else block
            for i, block in enumerate(blocks)
        ]

    def regroup(blocks):
        return [jnp.stack([block[j] for block in blocks]) for j in range(blocks[0].shape[0])]

    far = {spans // 2}
    main = prepare(amplitudes, keep, cuts[0])
    if apart:
        main, amplitudes = lax.optimization_barrier((main, amplitudes))
        sent = prepare_apart(place, amplitudes, keep, cuts[1], groups, spans)
        arrived = swap(regroup(swap(sent, "freq")), "span", set(range(spans)) - far)
    main = exchange(main)

    if apart:
        main, arrived = lax.optimization_barrier((main, arrived))
        arrived = swap(arrived, "span", far)
    size = edge_at // devices
    shape = main.shape
    main = nonlinear(main.reshape((devices, size) + shape[1:]), coefficients, transforms)
    main = main.reshape(shape)
    if apart:
        main, arrived[spans // 2] = lax.optimization_barrier((main, arrived[spans // 2]))
    main = exchange(main)
    inverse = slab_inverse[0]
    parts = (lower_coupling, upper_coupling, reduced_lower, reduced_upper, reduced_pivot)
    packed = around(pack(parts), "wall")
    turned, split, edge_rows, *end_rows, chain = constants(wall, inverse, packed, cuts, variables)
    *adjoint_modes, edge, sums = base(amplitudes, upstream, keep, edge_rows, turned, cuts)
    edges = around(edge, "wall")
    if apart:
        forced = nonlinear_apart(place, arrived, coefficients, transforms)
        returned = regroup(swap(forced, "freq"))
        held = (returned, split, end_rows, chain, adjoint_modes, edges, sums)
        held = lax.optimization_barrier(held)
        returned, split, end_rows, chain, adjoint_modes, edges, sums = held
        returned = swap(returned, "span")

    sides = [None] * len(cuts)
    sides[0], sums = absorb(None, [main], keep, end_rows[0], adjoint_modes[0], sums)
    if apart:
        sides[1], sums = absorb(place, returned, keep, end_rows[1], adjoint_modes[1], sums)
    bounds = around(sums, "wall")
    solved = solve(sides, upstream, keep, split)
    new_amplitudes, wavenumber_shift = finish(solved, bounds, edges, chain)
    return (new_amplitudes, wavenumber_shift)


def solution(mesh):
    placed = (
        P(None, None, "wall", ("freq", "span")),
        P(None, None, "wall", ("freq", "span")),
        P(("freq", "span")),
        P(),
        P("wall", None, None),
        P("wall", None, None),
        P("wall", None, None),
        P("wall", None, None),
        P("wall", None, None),
        P("wall", None, None),
    )
    return jax.shard_map(
        local,
        mesh=mesh,
        in_specs=placed,
        out_specs=(P(None, None, "wall", ("freq", "span")), P(None, ("freq", "span"))),
        check_vma=False,
    )
```

```python
import functools
import math

import jax
import jax.numpy as jnp
import ml_dtypes
import numpy as np
from jax import lax
from jax.experimental import pallas as pl
from jax.experimental.pallas import tpu as pltpu
from jax.sharding import PartitionSpec as P

NF = 128
NB = 256

epsilon = 1e-06

SPLIT = lax.Precision.HIGH
FULL = lax.Precision.HIGHEST


def tables():
    def turns(length):
        counter = np.arange(length)
        angles = (counter[:, None] * counter[None, :] % length) * (2.0 * math.pi / length)
        return np.cos(angles), np.sin(angles)

    cos_time, sin_time = turns(NF)
    cos_span, sin_span = turns(NB)
    scale = 1.0 / math.sqrt(NF * NB)
    out = (
        (np.block([[cos_time, -sin_time], [sin_time, cos_time]]), 1),
        (np.concatenate([cos_span, -sin_span], 0) * scale, 0),
        (np.concatenate([cos_span, -sin_span], 1) * scale, 0),
        (np.block([[cos_time, sin_time], [-sin_time, cos_time]]), 1),
    )

    def split(table, axis):
        high = table.astype(ml_dtypes.bfloat16)
        low = (table - high.astype(np.float64)).astype(ml_dtypes.bfloat16)
        return jnp.asarray(np.concatenate([high, high, low], axis))

    return [split(table, axis) for table, axis in out]


def params(megabytes=16):
    return pltpu.CompilerParams(vmem_limit_bytes=megabytes * 1024 * 1024)


def whole(array):
    zeros = (0,) * len(array.shape)
    return pl.BlockSpec(array.shape, lambda *_: zeros)


def in_hbm(array):
    return pltpu.with_memory_space_constraint(array, pltpu.HBM)


def kept_modes(mask_ref):
    return mask_ref[...].astype(jnp.float32).reshape(1, -1)


def row_step(rows):
    return rows // 2 if rows % 16 == 0 and rows > 16 else rows


def prepare_body(x_ref, mask_ref, out_ref):
    keep = kept_modes(mask_ref)
    rows, variables, freqs, _ = out_ref.shape
    for v in range(variables):
        for part in range(2):
            kept = x_ref[part, v] * keep
            out_ref[:, v, :, part * NB : (part + 1) * NB] = kept.reshape(rows, freqs, NB)


def prepare(amplitudes, keep, cut):
    _, variables, _, modes = amplitudes.shape
    freqs = modes // NB
    rows = cut.stop - cut.start
    step = row_step(rows)
    at = cut.start // step
    return pl.pallas_call(
        prepare_body,
        grid=(rows // step,),
        in_specs=[
            pl.BlockSpec((2, variables, step, modes), lambda r: (0, 0, at + r, 0)),
            pl.BlockSpec((modes,), lambda r: (0,)),
        ],
        out_specs=pl.BlockSpec((step, variables, freqs, 2 * NB), lambda r: (r, 0, 0, 0)),
        out_shape=pltpu.HBM((rows, variables, freqs, 2 * NB), jnp.float32),
        compiler_params=params(24),
        name="prepare",
    )(in_hbm(amplitudes), in_hbm(keep))


def partner(place_ref, j, i, spans):
    return (place_ref[0] ^ j) * spans + (place_ref[1] ^ i)


def prepare_apart_body(place_ref, x_ref, mask_ref, *refs):
    out_refs, rows_ref = refs[:-1], refs[-1]
    keep = kept_modes(mask_ref)
    rows, freqs, _ = rows_ref.shape
    spans = out_refs[0].shape[0]
    for part in range(2):
        kept = x_ref[part, 0] * keep
        rows_ref[:, :, part * NB : (part + 1) * NB] = kept.reshape(rows, freqs, NB)
    for j, out_ref in enumerate(out_refs):
        for i in range(spans):
            out_ref[i, 0] = rows_ref[partner(place_ref, j, i, spans)]


def prepare_apart(place, amplitudes, keep, cut, groups, spans):
    _, variables, _, modes = amplitudes.shape
    freqs = modes // NB
    rows = cut.stop - cut.start
    at = cut.start // rows
    return pl.pallas_call(
        prepare_apart_body,
        grid=(variables,),
        in_specs=[
            pl.BlockSpec(memory_space=pltpu.SMEM),
            pl.BlockSpec((2, 1, rows, modes), lambda v: (0, v, at, 0)),
            pl.BlockSpec((modes,), lambda v: (0,)),
        ],
        out_specs=[pl.BlockSpec((spans, 1, freqs, 2 * NB), lambda v: (0, v, 0, 0))] * groups,
        out_shape=[jax.ShapeDtypeStruct((spans, variables, freqs, 2 * NB), jnp.float32)] * groups,
        scratch_shapes=[pltpu.VMEM((rows, freqs, 2 * NB), jnp.float32)],
        compiler_params=params(),
        name="prepare_apart",
    )(place, in_hbm(amplitudes), keep)


def halves(value):
    high = value.astype(jnp.bfloat16)
    return high, (value - high.astype(jnp.float32)).astype(jnp.bfloat16)


def table_times(table, value):
    high, low = halves(value)
    value = jnp.concatenate([high, low, high], axis=0)
    return jnp.dot(table, value, preferred_element_type=jnp.float32)


def times_table(value, table):
    high, low = halves(value)
    value = jnp.concatenate([high, low, high], axis=1)
    return jnp.dot(value, table, preferred_element_type=jnp.float32)


def transform(read, write, q_ref, table_refs, field_ref, force_ref):
    wi_ref, ei_ref, ef_ref, wf_ref = table_refs
    variables = field_ref.shape[0]
    for v in range(variables):
        modes = read(v)
        stacked = jnp.concatenate([modes[:, :NB], modes[:, NB:]], axis=0)
        turned = table_times(wi_ref[...], stacked)
        beside = jnp.concatenate([turned[:NF], turned[NF:]], axis=1)
        field_ref[v] = times_table(beside, ei_ref[...])
    pairs = [(a, b) for a in range(variables) for b in range(a + 1, variables)]
    weights = [
        [q_ref[w * variables + a, b] + q_ref[w * variables + b, a] for a, b in pairs]
        for w in range(variables)
    ]
    step = 8
    for row in range(0, NF, step):
        at = slice(row, row + step)
        values = [field_ref[v, at] for v in range(variables)]
        total = [None] * variables
        for i, (a, b) in enumerate(pairs):
            product = values[a] * values[b]
            for w in range(variables):
                term = weights[w][i] * product
                total[w] = term if total[w] is None else total[w] + term
        for w in range(variables):
            force_ref[w, at] = total[w]
    for w in range(variables):
        spread = times_table(force_ref[w], ef_ref[...])
        stacked = jnp.concatenate([spread[:, :NB], spread[:, NB:]], axis=0)
        turned = table_times(wf_ref[...], stacked)
        for part in range(2):
            write(w, part, turned[part * NF : (part + 1) * NF])


def nonlinear_body(q_ref, in_ref, *refs):
    table_refs, out_ref, work_refs = refs[:4], refs[4], refs[5:]
    devices, _, _, freqs, _ = in_ref.shape

    def read(v):
        return in_ref[:, 0, v].reshape(NF, 2 * NB)

    def write(w, part, piece):
        at = slice(part * NB, (part + 1) * NB)
        out_ref[:, 0, w, :, at] = piece.reshape(devices, freqs, NB)

    transform(read, write, q_ref, table_refs, *work_refs)


def work_shapes(variables):
    return [pltpu.VMEM((variables, NF, NB), jnp.float32)] * 2


def nonlinear_cost(points, variables):
    return pl.CostEstimate(
        flops=points * variables * 12 * NF * NB * (NF + NB) * 2,
        bytes_accessed=points * variables * NF * NB * 16,
        transcendentals=0,
    )


def nonlinear(block, coefficients, transforms):
    devices, points, variables, freqs, lanes = block.shape
    spec = pl.BlockSpec((devices, 1, variables, freqs, lanes), lambda j: (0, j, 0, 0, 0))
    return pl.pallas_call(
        nonlinear_body,
        grid=(points,),
        in_specs=[pl.BlockSpec(memory_space=pltpu.SMEM), spec] + [whole(t) for t in transforms],
        out_specs=spec,
        out_shape=pltpu.HBM(block.shape, jnp.float32),
        scratch_shapes=work_shapes(variables),
        compiler_params=params(24),
        cost_estimate=nonlinear_cost(points, variables),
        name="nonlinear",
    )(coefficients, block, *[in_hbm(table) for table in transforms])


def nonlinear_apart_body(groups, spans, place_ref, q_ref, *refs):
    in_refs, refs = refs[:spans], refs[spans:]
    table_refs, refs = refs[:4], refs[4:]
    out_refs, refs = refs[:groups], refs[groups:]
    rows_ref, work_refs = refs[0], refs[1:]
    devices, _, freqs, _ = rows_ref.shape
    for j in range(groups):
        for i in range(spans):
            rows_ref[partner(place_ref, j, i, spans)] = in_refs[i][j]

    def read(v):
        return rows_ref[:, v].reshape(NF, 2 * NB)

    def write(w, part, piece):
        at = slice(part * NB, (part + 1) * NB)
        rows_ref[:, w, :, at] = piece.reshape(devices, freqs, NB)

    transform(read, write, q_ref, table_refs, *work_refs)
    for j in range(groups):
        for i in range(spans):
            out_refs[j][i] = rows_ref[partner(place_ref, j, i, spans)]


def nonlinear_apart(place, blocks, coefficients, transforms):
    spans = len(blocks)
    groups, variables, freqs, lanes = blocks[0].shape
    result = jax.ShapeDtypeStruct((spans, variables, freqs, lanes), jnp.float32)
    smem = pl.BlockSpec(memory_space=pltpu.SMEM)
    return pl.pallas_call(
        functools.partial(nonlinear_apart_body, groups, spans),
        grid=(1,),
        in_specs=[smem, smem]
        + [whole(block) for block in blocks]
        + [whole(table) for table in transforms],
        out_specs=[whole(result)] * groups,
        out_shape=[result] * groups,
        scratch_shapes=[pltpu.VMEM((groups * spans, variables, freqs, lanes), jnp.float32)]
        + work_shapes(variables),
        compiler_params=params(24),
        cost_estimate=nonlinear_cost(1, variables),
        name="nonlinear_apart",
    )(place, coefficients, *blocks, *[in_hbm(table) for table in transforms])


def total(value):
    return jnp.sum(value, axis=0, keepdims=True)


def padded(rows, multiple):
    return rows + -rows % multiple


def edge_body(width, x_ref, mask_ref, rows_ref, out_ref):
    _, variables, heights, lanes = x_ref.shape
    keep = kept_modes(mask_ref)
    squares = 0.0
    out_ref[...] = jnp.zeros(out_ref.shape, jnp.float32)
    for part in range(2):
        kept = x_ref[part].reshape(variables * heights, lanes) * keep
        squares = squares + total(kept * kept)
        out_ref[part * width : (part + 1) * width] = table_times(rows_ref[...], kept)[:width]
    out_ref[2 * width : 2 * width + 1] = squares


def edge(amplitudes, keep, rows, width):
    _, variables, heights, modes = amplitudes.shape
    length = padded(2 * width + 1, 8)
    return pl.pallas_call(
        functools.partial(edge_body, width),
        grid=(modes // NB,),
        in_specs=[
            pl.BlockSpec((2, variables, heights, NB), lambda i: (0, 0, 0, i)),
            pl.BlockSpec((NB,), lambda i: (i,)),
            whole(rows),
        ],
        out_specs=pl.BlockSpec((length, NB), lambda i: (0, i)),
        out_shape=jax.ShapeDtypeStruct((length, modes), jnp.float32),
        compiler_params=params(),
        name="edge",
    )(in_hbm(amplitudes), keep, rows)


def base_body(cuts, walls, width, x_ref, up_ref, mask_ref, turned_ref, ahead_ref, back_ref, *refs):
    edges, refs = refs[:walls], refs[walls:]
    out_refs, (sum_ref, square_ref) = refs[: len(cuts)], refs[len(cuts) :]
    _, variables, heights, lanes = x_ref.shape
    extent = variables * heights
    pushes = walls * width
    spare = back_ref.shape[1] // 3 - pushes
    keep = kept_modes(mask_ref)
    moved, sides = [], []
    sum_ref[...] = jnp.zeros(sum_ref.shape, jnp.float32)
    for part in range(2):
        kept = x_ref[part].reshape(extent, lanes) * keep
        taken = [ref[part * width : (part + 1) * width] for ref in edges]
        if spare:
            taken.append(jnp.zeros((spare, lanes), jnp.float32))
        taken = jnp.concatenate(taken, axis=0)
        moved.append(table_times(turned_ref[...], kept) - table_times(back_ref[...], taken))
        grid = moved[part].reshape(variables, heights, lanes)
        for cut, out_ref in zip(cuts, out_refs):
            out_ref[part] = grid[:, cut]
        sides.append(up_ref[part].reshape(extent, lanes) * keep)
        added = table_times(ahead_ref[...], sides[part])
        sum_ref[part * pushes : (part + 1) * pushes] = added[:pushes]
    row = 2 * pushes
    sum_ref[row : row + 1] = total(moved[0] * sides[0] + moved[1] * sides[1])
    sum_ref[row + 1 : row + 2] = total(moved[0] * sides[1] - moved[1] * sides[0])
    squares = sum(ref[2 * width : 2 * width + 1] for ref in edges)
    square_ref[...] = jnp.broadcast_to(squares, square_ref.shape)


def base(amplitudes, upstream, keep, turned, ahead, back, edges, width, cuts):
    _, variables, heights, modes = amplitudes.shape
    walls = len(edges)
    lengths = [cut.stop - cut.start for cut in cuts]
    shapes = [(2, variables, rows, modes) for rows in lengths]
    sums = padded(2 * walls * width + 2, 8)
    spec = pl.BlockSpec((2, variables, heights, NB), lambda i: (0, 0, 0, i))

    def rows_spec(rows):
        return pl.BlockSpec((rows, NB), lambda i: (0, i))

    return pl.pallas_call(
        functools.partial(base_body, cuts, walls, width),
        grid=(modes // NB,),
        in_specs=[spec] * 2
        + [pl.BlockSpec((NB,), lambda i: (i,)), whole(turned), whole(ahead), whole(back)]
        + [rows_spec(part.shape[0]) for part in edges],
        out_specs=[
            pl.BlockSpec((2, variables, rows, NB), lambda i: (0, 0, 0, i)) for rows in lengths
        ]
        + [rows_spec(sums), rows_spec(8)],
        out_shape=[pltpu.HBM(shapes[0], jnp.float32)]
        + [jax.ShapeDtypeStruct(shape, jnp.float32) for shape in shapes[1:]]
        + [jax.ShapeDtypeStruct((rows, modes), jnp.float32) for rows in (sums, 8)],
        compiler_params=params(24),
        name="base",
    )(in_hbm(amplitudes), in_hbm(upstream), keep, turned, ahead, back, *edges)


def absorb_rows(width, read, mask_ref, ahead_ref, adj_ref, before_ref, out_ref, sum_ref, *send_refs):
    _, variables, rows, lanes = out_ref.shape
    pushes = ahead_ref.shape[1]
    keep = kept_modes(mask_ref)

    @pl.when(pl.program_id(0) == 0)
    def _():
        sum_ref[...] = before_ref[...]

    for v in range(variables):
        for part in range(2):
            out_ref[part, v] = read(v, part).reshape(rows, lanes) * keep
    sides = [out_ref[part].reshape(variables * rows, lanes) for part in range(2)]
    for part in range(2):
        sum_ref[part * pushes : (part + 1) * pushes] += jnp.dot(
            ahead_ref[0], sides[part], precision=SPLIT, preferred_element_type=jnp.float32
        )
    real, imag = (adj_ref[part].reshape(variables * rows, lanes) for part in range(2))
    at = 2 * pushes
    sum_ref[at : at + 1] += total(real * sides[0] + imag * sides[1])
    sum_ref[at + 1 : at + 2] += total(real * sides[1] - imag * sides[0])

    if send_refs:

        @pl.when(pl.program_id(0) == pl.num_programs(0) - 1)
        def _():
            for d, send_ref in enumerate(send_refs, 1):
                for part in range(2):
                    at = part * pushes + d * width
                    send_ref[part * width : (part + 1) * width] = sum_ref[at : at + width]
                at = 2 * pushes
                send_ref[2 * width : 2 * width + 2] = sum_ref[at : at + 2]
                rest = send_ref.shape[0] - 2 * width - 2
                if rest:
                    send_ref[2 * width + 2 :] = jnp.zeros((rest, lanes), jnp.float32)


def absorb_body(width, in_ref, *refs):
    def read(v, part):
        return in_ref[:, v, :, part * NB : (part + 1) * NB]

    absorb_rows(width, read, *refs)


def absorb_apart_body(width, spans, place_ref, *refs):
    in_refs, refs, rows_ref = refs[:spans], refs[spans:-1], refs[-1]
    for i, in_ref in enumerate(in_refs):
        for j in range(in_ref.shape[0]):
            rows_ref[partner(place_ref, j, i, spans)] = in_ref[j]

    def read(v, part):
        return rows_ref[:, v, :, part * NB : (part + 1) * NB]

    absorb_rows(width, read, *refs)


def absorb(place, blocks, keep, ahead, adjoint_modes, before, width, sends):
    blocks = list(blocks)
    apart = place is not None
    _, variables, rows, modes = adjoint_modes.shape
    steps, pushes, depth = ahead.shape
    step = rows // steps
    grid_spec = pl.BlockSpec((2, variables, step, modes), lambda r: (0, 0, r, 0))
    _, _, freqs, lanes = blocks[0].shape
    sent = jax.ShapeDtypeStruct((padded(2 * width + 2, 8), modes), jnp.float32)
    operands = blocks + [keep, ahead, adjoint_modes if apart else in_hbm(adjoint_modes), before]
    in_specs = [
        whole(block)
        if apart
        else pl.BlockSpec((step, variables, freqs, lanes), lambda r: (r, 0, 0, 0))
        for block in blocks
    ] + [
        pl.BlockSpec((modes,), lambda r: (0,)),
        pl.BlockSpec((1, pushes, depth), lambda r: (r, 0, 0)),
        grid_spec,
        whole(before),
    ]
    body, scratch = functools.partial(absorb_body, width), []
    if apart:
        operands = [place] + operands
        in_specs = [pl.BlockSpec(memory_space=pltpu.SMEM)] + in_specs
        body = functools.partial(absorb_apart_body, width, len(blocks))
        scratch = [pltpu.VMEM((rows, variables, freqs, lanes), jnp.float32)]
    return pl.pallas_call(
        body,
        grid=(steps,),
        in_specs=in_specs,
        out_specs=[grid_spec, whole(before)] + [whole(sent)] * sends,
        out_shape=[
            jax.ShapeDtypeStruct((2, variables, rows, modes), jnp.float32),
            jax.ShapeDtypeStruct(before.shape, jnp.float32),
        ]
        + [sent] * sends,
        scratch_shapes=scratch,
        compiler_params=params(24),
        name="absorb_apart" if apart else "absorb",
    )(*operands)


def solve_body(side_ref, up_ref, mask_ref, inverse_ref, out_ref):
    _, variables, heights, lanes = out_ref.shape
    keep = kept_modes(mask_ref)
    spare = heights - side_ref.shape[2]
    for part in range(2):
        forced = side_ref[part]
        if spare:
            none = jnp.zeros((variables, spare, lanes), jnp.float32)
            forced = jnp.concatenate([forced, none], axis=1)
        side = (forced + up_ref[part] * keep).reshape(variables * heights, lanes)
        out_ref[part] = table_times(inverse_ref[...], side).reshape(variables, heights, lanes)


def solve(side, upstream, keep, inverse):
    _, variables, heights, modes = upstream.shape
    lanes = min(2 * NB, modes)
    spec = pl.BlockSpec((2, variables, heights, lanes), lambda i: (0, 0, 0, i))
    return pl.pallas_call(
        solve_body,
        grid=(modes // lanes,),
        in_specs=[
            pl.BlockSpec((2, variables, side.shape[2], lanes), lambda i: (0, 0, 0, i)),
            spec,
            pl.BlockSpec((lanes,), lambda i: (i,)),
            whole(inverse),
        ],
        out_specs=spec,
        out_shape=jax.ShapeDtypeStruct(upstream.shape, jnp.float32),
        compiler_params=params(24),
        name="solve",
    )(side, in_hbm(upstream), keep, inverse)


def solve_more_body(side_ref, before_ref, inverse_ref, out_ref):
    _, variables, heights, lanes = out_ref.shape
    for part in range(2):
        moved = table_times(inverse_ref[...], side_ref[part].reshape(-1, lanes))
        out_ref[part] = before_ref[part] + moved.reshape(variables, heights, lanes)


def solve_more(side, before, inverse):
    _, variables, rows, modes = side.shape
    lanes = min(2 * NB, modes)
    spec = pl.BlockSpec(before.shape[:3] + (lanes,), lambda i: (0, 0, 0, i))
    return pl.pallas_call(
        solve_more_body,
        grid=(modes // lanes,),
        in_specs=[
            pl.BlockSpec((2, variables, rows, lanes), lambda i: (0, 0, 0, i)),
            spec,
            whole(inverse),
        ],
        out_specs=spec,
        out_shape=jax.ShapeDtypeStruct(before.shape, jnp.float32),
        compiler_params=params(24),
        name="solve_more",
    )(side, before, inverse)


def finish_body(walls, width, solved_ref, sum_ref, square_ref, *refs):
    others, (columns_ref, out_ref, shift_ref) = refs[: walls - 1], refs[walls - 1 :]
    _, variables, heights, lanes = out_ref.shape
    spare = columns_ref.shape[1] // 3 - width
    pushes = walls * width
    for part in range(2):
        push = sum_ref[part * pushes : part * pushes + width]
        for ref in others:
            push = push + ref[part * width : (part + 1) * width]
        if spare:
            push = jnp.concatenate([push, jnp.zeros((spare, lanes), jnp.float32)], axis=0)
        moved = table_times(columns_ref[...], push)
        out_ref[part] = solved_ref[part] - moved.reshape(variables, heights, lanes)
    both = sum_ref[2 * pushes : 2 * pushes + 2]
    for ref in others:
        both = both + ref[2 * width : 2 * width + 2]
    squares = square_ref[:1]
    weight = squares + epsilon
    shift_ref[0:1] = both[1:2] / weight
    shift_ref[1:2] = (squares - both[0:1]) / weight


def finish(solved, sums, squares, others, columns, width):
    _, variables, heights, modes = solved.shape
    lanes = min(2 * NB, modes)
    spec = pl.BlockSpec((2, variables, heights, lanes), lambda i: (0, 0, 0, i))
    rows = [sums, squares] + others
    return pl.pallas_call(
        functools.partial(finish_body, len(others) + 1, width),
        grid=(modes // lanes,),
        in_specs=[spec]
        + [pl.BlockSpec((part.shape[0], lanes), lambda i: (0, i)) for part in rows]
        + [whole(columns)],
        out_specs=[spec, pl.BlockSpec((2, lanes), lambda i: (0, i))],
        out_shape=[
            jax.ShapeDtypeStruct(solved.shape, jnp.float32),
            jax.ShapeDtypeStruct((2, modes), jnp.float32),
        ],
        compiler_params=params(),
        name="finish",
    )(solved, *rows, columns)


def around(block, axis):
    count = lax.axis_size(axis)
    return [block] + [
        lax.ppermute(block, axis, [(i, (i + d) % count) for i in range(count)])
        for d in range(1, count)
    ]


def hand_back(blocks, axis):
    count = lax.axis_size(axis)
    return [
        lax.ppermute(block, axis, [(i, (i - d) % count) for i in range(count)])
        for d, block in enumerate(blocks, 1)
    ]


PACKED_ROWS = 16


def pack_body(*refs):
    in_refs, out_ref = refs[:-1], refs[-1]
    out_ref[...] = jnp.zeros(out_ref.shape, jnp.float32)
    for i, ref in enumerate(in_refs):
        rows, columns = ref.shape[1:]
        out_ref[i, :rows, :columns] = ref[0]


def pack(parts):
    return pl.pallas_call(
        pack_body,
        out_shape=jax.ShapeDtypeStruct((len(parts), PACKED_ROWS, 128), jnp.float32),
        name="pack",
    )(*parts)


def upper_bits(value):
    return value.astype(jnp.bfloat16).astype(jnp.float32)


def split_columns(matrix):
    high = upper_bits(matrix)
    return jnp.concatenate([high, high, matrix - high], axis=1).astype(jnp.bfloat16)


def push_width(walls, variables):
    return variables if walls == 2 else 2 * variables


def constants_body(cuts, variables, walls, place_ref, inverse_ref, *refs):
    packed, refs = refs[:walls], refs[walls:]
    turned_ref, split_ref, last_ref, column_ref, edge_ref, ahead_ref, back_ref = refs[:7]
    row_refs, (all_ref, step_ref) = refs[7 : 7 + len(cuts)], refs[7 + len(cuts) :]
    extent = inverse_ref.shape[0]
    heights = extent // variables
    ends = 2 * variables
    width = push_width(walls, variables)
    matrix = inverse_ref[...]
    turned = matrix.T
    turned_ref[...] = split_columns(turned)
    split_ref[...] = split_columns(matrix)
    cut = cuts[-1]
    last = [matrix[:, v * heights : (v + 1) * heights][:, cut] for v in range(variables)]
    last_ref[...] = split_columns(jnp.concatenate(last, axis=1))

    def dot(a, b):
        return jnp.dot(a, b, precision=FULL, preferred_element_type=jnp.float32)

    def ends_of(value):
        low = [value[v * heights : v * heights + 1] for v in range(variables)]
        high = [value[(v + 1) * heights - 1 : (v + 1) * heights] for v in range(variables)]
        return jnp.concatenate(low, axis=0), jnp.concatenate(high, axis=0)

    def extended(value, rows):
        spare = rows - value.shape[0]
        if not spare:
            return value
        return jnp.concatenate([value, jnp.zeros((spare, value.shape[1]), jnp.float32)], axis=0)

    size = walls * PACKED_ROWS
    for d in range(walls):
        all_ref[(place_ref[0] - d + walls) % walls] = packed[d][...]

    def small(j, kind):
        return all_ref[j, kind][:, :PACKED_ROWS]

    row = lax.broadcasted_iota(jnp.int32, (PACKED_ROWS, size), 0)
    column = lax.broadcasted_iota(jnp.int32, (PACKED_ROWS, size), 1)
    units = []
    for j in range(walls):
        d = (place_ref[0] - j + walls) % walls
        hit = (column == d * ends + row) & (row < ends)
        units.append(jnp.where(hit, 1.0, 0.0))
    ahead = [units[0]]
    for j in range(1, walls):
        ahead.append(units[j] - dot(small(j, 2), ahead[j - 1]))
    interface = [None] * walls
    interface[-1] = dot(small(walls - 1, 4), ahead[-1])
    for j in range(walls - 2, -1, -1):
        interface[j] = dot(small(j, 4), ahead[j] - dot(small(j, 3), interface[j + 1]))
    none = jnp.zeros((variables, size), jnp.float32)
    for j in range(walls):
        under, over = none, none
        if j > 0:
            lower = extended(interface[j - 1][variables:], PACKED_ROWS)
            under = dot(small(j, 0), lower)[:variables]
        if j < walls - 1:
            over = dot(small(j, 1), interface[j + 1])[:variables]
        push = under + over if walls == 2 else jnp.concatenate([under, over], axis=0)
        step_ref[(place_ref[0] - j + walls) % walls] = extended(push, PACKED_ROWS)

    low, high = ends_of(matrix)
    bounds = extended(jnp.concatenate([low, high], axis=0), PACKED_ROWS)
    steps = [step_ref[d][:width, :PACKED_ROWS] for d in range(walls)]
    steps = [jnp.where(column[:width, :PACKED_ROWS] < ends, step, 0.0) for step in steps]
    pushes = dot(jnp.concatenate(steps, axis=0), bounds)
    for cut, row_ref in zip(cuts, row_refs):
        step = row_step(cut.stop - cut.start)
        for r in range(row_ref.shape[0]):
            at = cut.start + r * step
            pieces = [pushes[:, v * heights + at : v * heights + at + step] for v in range(variables)]
            row_ref[r] = jnp.concatenate(pieces, axis=1)
    pushes = extended(pushes, ahead_ref.shape[0])
    ahead_ref[...] = split_columns(pushes)
    back_ref[...] = split_columns(pushes.T)
    low, high = ends_of(turned)
    edge = jnp.concatenate([low, high], axis=0)
    if walls == 2:
        edge = jnp.where(place_ref[0] == 0, high, low)
    edge = extended(edge, edge_ref.shape[0])
    edge_ref[...] = split_columns(edge)
    column_ref[...] = split_columns(edge.T)


def constants(place, inverse, packed, cuts, variables):
    walls = len(packed)
    extent = inverse.shape[0]
    width = push_width(walls, variables)
    lengths = [cut.stop - cut.start for cut in cuts]
    size = walls * PACKED_ROWS
    pushes, edge_rows = padded(walls * width, 16), padded(width, 16)

    def split_shape(rows, columns):
        return jax.ShapeDtypeStruct((rows, 3 * columns), jnp.bfloat16)

    return pl.pallas_call(
        functools.partial(constants_body, cuts, variables, walls),
        in_specs=[pl.BlockSpec(memory_space=pltpu.SMEM)]
        + [pl.BlockSpec(memory_space=pltpu.VMEM)] * (1 + walls),
        out_shape=[
            split_shape(extent, extent),
            split_shape(extent, extent),
            split_shape(extent, variables * lengths[-1]),
            split_shape(extent, edge_rows),
            split_shape(edge_rows, extent),
            split_shape(pushes, extent),
            split_shape(extent, pushes),
        ]
        + [
            jax.ShapeDtypeStruct(
                (n // row_step(n), walls * width, variables * row_step(n)), jnp.float32
            )
            for n in lengths
        ],
        scratch_shapes=[
            pltpu.VMEM((walls,) + packed[0].shape, jnp.float32),
            pltpu.VMEM((walls, PACKED_ROWS, size), jnp.float32),
        ],
        compiler_params=params(),
        name="constants",
    )(place, inverse, *packed)


def local(
    amplitudes,
    upstream,
    harmonic_mask,
    quadratic_coefficients,
    slab_inverse,
    lower_coupling,
    upper_coupling,
    reduced_lower,
    reduced_upper,
    reduced_pivot,
):
    _, variables, heights, modes = amplitudes.shape
    axes = ("freq", "span")
    groups, spans = lax.axis_size("freq"), lax.axis_size("span")
    devices = groups * spans
    points = heights // devices
    apart = points > 1 and groups & (groups - 1) == 0 and spans & (spans - 1) == 0
    edge_at = heights - devices if apart else heights
    cuts = [slice(0, edge_at)] + ([slice(edge_at, heights)] if apart else [])
    keep = harmonic_mask
    place = jnp.stack([lax.axis_index("freq"), lax.axis_index("span")]).astype(jnp.int32)
    wall = lax.axis_index("wall").reshape(1).astype(jnp.int32)
    transforms = tables()
    coefficients = quadratic_coefficients.reshape(variables * variables, variables)

    def exchange(block):
        return lax.all_to_all(block, axes, split_axis=0, concat_axis=0, tiled=True)

    def swap(blocks, axis, only=None):
        count = len(blocks)
        return [
            lax.ppermute(block, axis, [(at, at ^ i) for at in range(count)])
            if i and (only is None or i in only)
            else block
            for i, block in enumerate(blocks)
        ]

    def regroup(blocks):
        return [jnp.stack([block[j] for block in blocks]) for j in range(blocks[0].shape[0])]

    far = {spans // 2}
    main = prepare(amplitudes, keep, cuts[0])
    if apart:
        main, amplitudes = lax.optimization_barrier((main, amplitudes))
        sent = prepare_apart(place, amplitudes, keep, cuts[1], groups, spans)
        arrived = swap(regroup(swap(sent, "freq")), "span", set(range(spans)) - far)
    main = exchange(main)

    if apart:
        main, arrived = lax.optimization_barrier((main, arrived))
        arrived = swap(arrived, "span", far)
    size = edge_at // devices
    shape = main.shape
    main = nonlinear(main.reshape((devices, size) + shape[1:]), coefficients, transforms)
    main = main.reshape(shape)
    if apart:
        main, arrived[spans // 2] = lax.optimization_barrier((main, arrived[spans // 2]))
    main = exchange(main)
    inverse = slab_inverse[0]
    parts = (lower_coupling, upper_coupling, reduced_lower, reduced_upper, reduced_pivot)
    packed = around(pack(parts), "wall")
    turned, split, last, edge_columns, edge_rows, ahead, back, *rows = constants(
        wall, inverse, packed, cuts, variables
    )
    walls = len(packed)
    width = push_width(walls, variables)
    edges = around(edge(amplitudes, keep, edge_rows, width), "wall")
    *adjoint_modes, sums, squares = base(
        amplitudes, upstream, keep, turned, ahead, back, edges, width, cuts
    )
    if apart:
        forced = nonlinear_apart(place, arrived, coefficients, transforms)
        returned = regroup(swap(forced, "freq"))
        held = (returned, split, last, edge_columns, rows, adjoint_modes, sums, squares)
        held = lax.optimization_barrier(held)
        returned, split, last, edge_columns, rows, adjoint_modes, sums, squares = held
        returned = swap(returned, "span")

    sends = walls - 1
    side, sums, *sent = absorb(
        None, [main], keep, rows[0], adjoint_modes[0], sums, width, 0 if apart else sends
    )
    solved = solve(side, upstream, keep, split)
    if apart:
        solved, sums = lax.optimization_barrier((solved, sums))
        side, sums, *sent = absorb(
            place, returned, keep, rows[1], adjoint_modes[1], sums, width, sends
        )
    others = hand_back(sent, "wall")
    if apart:
        solved = solve_more(side, solved, last)
    new_amplitudes, wavenumber_shift = finish(solved, sums, squares, others, edge_columns, width)
    return (new_amplitudes, wavenumber_shift)


def solution(mesh):
    placed = (
        P(None, None, "wall", ("freq", "span")),
        P(None, None, "wall", ("freq", "span")),
        P(("freq", "span")),
        P(),
        P("wall", None, None),
        P("wall", None, None),
        P("wall", None, None),
        P("wall", None, None),
        P("wall", None, None),
        P("wall", None, None),
    )
    return jax.shard_map(
        local,
        mesh=mesh,
        in_specs=placed,
        out_specs=(P(None, None, "wall", ("freq", "span")), P(None, ("freq", "span"))),
        check_vma=False,
    )
```

```python
import functools
import math

import jax
import jax.numpy as jnp
import ml_dtypes
import numpy as np
from jax import lax
from jax.experimental import pallas as pl
from jax.experimental.pallas import tpu as pltpu
from jax.sharding import PartitionSpec as P

NF = 128
NB = 256

epsilon = 1e-06

SPLIT = lax.Precision.HIGH
FULL = lax.Precision.HIGHEST


def tables():
    def turns(length):
        counter = np.arange(length)
        angles = (counter[:, None] * counter[None, :] % length) * (2.0 * math.pi / length)
        return np.cos(angles), np.sin(angles)

    cos_time, sin_time = turns(NF)
    cos_span, sin_span = turns(NB)
    scale = 1.0 / math.sqrt(NF * NB)
    out = (
        (np.block([[cos_time, -sin_time], [sin_time, cos_time]]), 1),
        (np.concatenate([cos_span, -sin_span], 0) * scale, 0),
        (np.concatenate([cos_span, -sin_span], 1) * scale, 0),
        (np.block([[cos_time, sin_time], [-sin_time, cos_time]]), 1),
    )

    def split(table, axis):
        high = table.astype(ml_dtypes.bfloat16)
        low = (table - high.astype(np.float64)).astype(ml_dtypes.bfloat16)
        return jnp.asarray(np.concatenate([high, high, low], axis))

    return [split(table, axis) for table, axis in out]


def params(megabytes=16):
    return pltpu.CompilerParams(vmem_limit_bytes=megabytes * 1024 * 1024)


def whole(array):
    zeros = (0,) * len(array.shape)
    return pl.BlockSpec(array.shape, lambda *_: zeros)


def in_hbm(array):
    return pltpu.with_memory_space_constraint(array, pltpu.HBM)


def kept_modes(mask_ref):
    return mask_ref[...].astype(jnp.float32).reshape(1, -1)


def row_step(rows):
    return rows // 2 if rows % 16 == 0 and rows > 16 else rows


def prepare_body(x_ref, mask_ref, out_ref):
    keep = kept_modes(mask_ref)
    rows, variables, freqs, _ = out_ref.shape
    for v in range(variables):
        for part in range(2):
            kept = x_ref[part, v] * keep
            out_ref[:, v, :, part * NB : (part + 1) * NB] = kept.reshape(rows, freqs, NB)


def prepare(amplitudes, keep, cut):
    _, variables, _, modes = amplitudes.shape
    freqs = modes // NB
    rows = cut.stop - cut.start
    step = row_step(rows)
    at = cut.start // step
    return pl.pallas_call(
        prepare_body,
        grid=(rows // step,),
        in_specs=[
            pl.BlockSpec((2, variables, step, modes), lambda r: (0, 0, at + r, 0)),
            pl.BlockSpec((modes,), lambda r: (0,)),
        ],
        out_specs=pl.BlockSpec((step, variables, freqs, 2 * NB), lambda r: (r, 0, 0, 0)),
        out_shape=pltpu.HBM((rows, variables, freqs, 2 * NB), jnp.float32),
        compiler_params=params(24),
        name="prepare",
    )(in_hbm(amplitudes), in_hbm(keep))


def partner(place_ref, j, i, spans):
    return (place_ref[0] ^ j) * spans + (place_ref[1] ^ i)


def prepare_apart_body(place_ref, x_ref, mask_ref, *refs):
    out_refs, rows_ref = refs[:-1], refs[-1]
    keep = kept_modes(mask_ref)
    rows, freqs, _ = rows_ref.shape
    spans = out_refs[0].shape[0]
    for part in range(2):
        kept = x_ref[part, 0] * keep
        rows_ref[:, :, part * NB : (part + 1) * NB] = kept.reshape(rows, freqs, NB)
    for j, out_ref in enumerate(out_refs):
        for i in range(spans):
            out_ref[i, 0] = rows_ref[partner(place_ref, j, i, spans)]


def prepare_apart(place, amplitudes, keep, cut, groups, spans):
    _, variables, _, modes = amplitudes.shape
    freqs = modes // NB
    rows = cut.stop - cut.start
    at = cut.start // rows
    return pl.pallas_call(
        prepare_apart_body,
        grid=(variables,),
        in_specs=[
            pl.BlockSpec(memory_space=pltpu.SMEM),
            pl.BlockSpec((2, 1, rows, modes), lambda v: (0, v, at, 0)),
            pl.BlockSpec((modes,), lambda v: (0,)),
        ],
        out_specs=[pl.BlockSpec((spans, 1, freqs, 2 * NB), lambda v: (0, v, 0, 0))] * groups,
        out_shape=[jax.ShapeDtypeStruct((spans, variables, freqs, 2 * NB), jnp.float32)] * groups,
        scratch_shapes=[pltpu.VMEM((rows, freqs, 2 * NB), jnp.float32)],
        compiler_params=params(),
        name="prepare_apart",
    )(place, in_hbm(amplitudes), keep)


def halves(value):
    high = value.astype(jnp.bfloat16)
    return high, (value - high.astype(jnp.float32)).astype(jnp.bfloat16)


def table_times(table, value):
    high, low = halves(value)
    value = jnp.concatenate([high, low, high], axis=0)
    return jnp.dot(table, value, preferred_element_type=jnp.float32)


def times_table(value, table):
    high, low = halves(value)
    value = jnp.concatenate([high, low, high], axis=1)
    return jnp.dot(value, table, preferred_element_type=jnp.float32)


def transform(read, write, q_ref, table_refs, field_ref, force_ref):
    wi_ref, ei_ref, ef_ref, wf_ref = table_refs
    variables = field_ref.shape[0]
    for v in range(variables):
        modes = read(v)
        stacked = jnp.concatenate([modes[:, :NB], modes[:, NB:]], axis=0)
        turned = table_times(wi_ref[...], stacked)
        beside = jnp.concatenate([turned[:NF], turned[NF:]], axis=1)
        field_ref[v] = times_table(beside, ei_ref[...])
    pairs = [(a, b) for a in range(variables) for b in range(a + 1, variables)]
    weights = [
        [q_ref[w * variables + a, b] + q_ref[w * variables + b, a] for a, b in pairs]
        for w in range(variables)
    ]
    step = 8
    for row in range(0, NF, step):
        at = slice(row, row + step)
        values = [field_ref[v, at] for v in range(variables)]
        total = [None] * variables
        for i, (a, b) in enumerate(pairs):
            product = values[a] * values[b]
            for w in range(variables):
                term = weights[w][i] * product
                total[w] = term if total[w] is None else total[w] + term
        for w in range(variables):
            force_ref[w, at] = total[w]
    for w in range(variables):
        spread = times_table(force_ref[w], ef_ref[...])
        stacked = jnp.concatenate([spread[:, :NB], spread[:, NB:]], axis=0)
        turned = table_times(wf_ref[...], stacked)
        for part in range(2):
            write(w, part, turned[part * NF : (part + 1) * NF])


def nonlinear_body(q_ref, in_ref, *refs):
    table_refs, out_ref, work_refs = refs[:4], refs[4], refs[5:]
    devices, _, _, freqs, _ = in_ref.shape

    def read(v):
        return in_ref[:, 0, v].reshape(NF, 2 * NB)

    def write(w, part, piece):
        at = slice(part * NB, (part + 1) * NB)
        out_ref[:, 0, w, :, at] = piece.reshape(devices, freqs, NB)

    transform(read, write, q_ref, table_refs, *work_refs)


def work_shapes(variables):
    return [pltpu.VMEM((variables, NF, NB), jnp.float32)] * 2


def nonlinear_cost(points, variables):
    return pl.CostEstimate(
        flops=points * variables * 12 * NF * NB * (NF + NB) * 2,
        bytes_accessed=points * variables * NF * NB * 16,
        transcendentals=0,
    )


def nonlinear(block, coefficients, transforms):
    devices, points, variables, freqs, lanes = block.shape
    spec = pl.BlockSpec((devices, 1, variables, freqs, lanes), lambda j: (0, j, 0, 0, 0))
    return pl.pallas_call(
        nonlinear_body,
        grid=(points,),
        in_specs=[pl.BlockSpec(memory_space=pltpu.SMEM), spec] + [whole(t) for t in transforms],
        out_specs=spec,
        out_shape=pltpu.HBM(block.shape, jnp.float32),
        scratch_shapes=work_shapes(variables),
        compiler_params=params(24),
        cost_estimate=nonlinear_cost(points, variables),
        name="nonlinear",
    )(coefficients, block, *[in_hbm(table) for table in transforms])


def nonlinear_apart_body(groups, spans, place_ref, q_ref, *refs):
    in_refs, refs = refs[:spans], refs[spans:]
    table_refs, refs = refs[:4], refs[4:]
    out_refs, refs = refs[:groups], refs[groups:]
    rows_ref, work_refs = refs[0], refs[1:]
    devices, _, freqs, _ = rows_ref.shape
    for j in range(groups):
        for i in range(spans):
            rows_ref[partner(place_ref, j, i, spans)] = in_refs[i][j]

    def read(v):
        return rows_ref[:, v].reshape(NF, 2 * NB)

    def write(w, part, piece):
        at = slice(part * NB, (part + 1) * NB)
        rows_ref[:, w, :, at] = piece.reshape(devices, freqs, NB)

    transform(read, write, q_ref, table_refs, *work_refs)
    for j in range(groups):
        for i in range(spans):
            out_refs[j][i] = rows_ref[partner(place_ref, j, i, spans)]


def nonlinear_apart(place, blocks, coefficients, transforms):
    spans = len(blocks)
    groups, variables, freqs, lanes = blocks[0].shape
    result = jax.ShapeDtypeStruct((spans, variables, freqs, lanes), jnp.float32)
    smem = pl.BlockSpec(memory_space=pltpu.SMEM)
    return pl.pallas_call(
        functools.partial(nonlinear_apart_body, groups, spans),
        grid=(1,),
        in_specs=[smem, smem]
        + [whole(block) for block in blocks]
        + [whole(table) for table in transforms],
        out_specs=[whole(result)] * groups,
        out_shape=[result] * groups,
        scratch_shapes=[pltpu.VMEM((groups * spans, variables, freqs, lanes), jnp.float32)]
        + work_shapes(variables),
        compiler_params=params(24),
        cost_estimate=nonlinear_cost(1, variables),
        name="nonlinear_apart",
    )(place, coefficients, *blocks, *[in_hbm(table) for table in transforms])


def total(value):
    return jnp.sum(value, axis=0, keepdims=True)


def padded(rows, multiple):
    return rows + -rows % multiple


def edge_body(width, x_ref, mask_ref, rows_ref, out_ref):
    _, variables, heights, lanes = x_ref.shape
    keep = kept_modes(mask_ref)
    squares = 0.0
    out_ref[...] = jnp.zeros(out_ref.shape, jnp.float32)
    for part in range(2):
        kept = x_ref[part].reshape(variables * heights, lanes) * keep
        squares = squares + total(kept * kept)
        out_ref[part * width : (part + 1) * width] = table_times(rows_ref[...], kept)[:width]
    out_ref[2 * width : 2 * width + 1] = squares


def edge(amplitudes, keep, rows, width):
    _, variables, heights, modes = amplitudes.shape
    length = padded(2 * width + 1, 8)
    return pl.pallas_call(
        functools.partial(edge_body, width),
        grid=(modes // NB,),
        in_specs=[
            pl.BlockSpec((2, variables, heights, NB), lambda i: (0, 0, 0, i)),
            pl.BlockSpec((NB,), lambda i: (i,)),
            whole(rows),
        ],
        out_specs=pl.BlockSpec((length, NB), lambda i: (0, i)),
        out_shape=jax.ShapeDtypeStruct((length, modes), jnp.float32),
        compiler_params=params(),
        name="edge",
    )(in_hbm(amplitudes), keep, rows)


def base_body(cuts, walls, width, x_ref, up_ref, mask_ref, turned_ref, ahead_ref, back_ref, *refs):
    edges, refs = refs[:walls], refs[walls:]
    out_refs, (sum_ref, square_ref) = refs[: len(cuts)], refs[len(cuts) :]
    _, variables, heights, lanes = x_ref.shape
    extent = variables * heights
    pushes = walls * width
    spare = back_ref.shape[1] // 3 - pushes
    keep = kept_modes(mask_ref)
    moved, sides = [], []
    sum_ref[...] = jnp.zeros(sum_ref.shape, jnp.float32)
    for part in range(2):
        kept = x_ref[part].reshape(extent, lanes) * keep
        taken = [ref[part * width : (part + 1) * width] for ref in edges]
        if spare:
            taken.append(jnp.zeros((spare, lanes), jnp.float32))
        taken = jnp.concatenate(taken, axis=0)
        moved.append(table_times(turned_ref[...], kept) - table_times(back_ref[...], taken))
        grid = moved[part].reshape(variables, heights, lanes)
        for cut, out_ref in zip(cuts, out_refs):
            out_ref[part] = grid[:, cut]
        sides.append(up_ref[part].reshape(extent, lanes) * keep)
        added = table_times(ahead_ref[...], sides[part])
        sum_ref[part * pushes : (part + 1) * pushes] = added[:pushes]
    row = 2 * pushes
    sum_ref[row : row + 1] = total(moved[0] * sides[0] + moved[1] * sides[1])
    sum_ref[row + 1 : row + 2] = total(moved[0] * sides[1] - moved[1] * sides[0])
    squares = sum(ref[2 * width : 2 * width + 1] for ref in edges)
    square_ref[...] = jnp.broadcast_to(squares, square_ref.shape)


def base(amplitudes, upstream, keep, turned, ahead, back, edges, width, cuts):
    _, variables, heights, modes = amplitudes.shape
    walls = len(edges)
    lengths = [cut.stop - cut.start for cut in cuts]
    shapes = [(2, variables, rows, modes) for rows in lengths]
    sums = padded(2 * walls * width + 2, 8)
    spec = pl.BlockSpec((2, variables, heights, NB), lambda i: (0, 0, 0, i))

    def rows_spec(rows):
        return pl.BlockSpec((rows, NB), lambda i: (0, i))

    return pl.pallas_call(
        functools.partial(base_body, cuts, walls, width),
        grid=(modes // NB,),
        in_specs=[spec] * 2
        + [pl.BlockSpec((NB,), lambda i: (i,)), whole(turned), whole(ahead), whole(back)]
        + [rows_spec(part.shape[0]) for part in edges],
        out_specs=[
            pl.BlockSpec((2, variables, rows, NB), lambda i: (0, 0, 0, i)) for rows in lengths
        ]
        + [rows_spec(sums), rows_spec(8)],
        out_shape=[pltpu.HBM(shapes[0], jnp.float32)]
        + [jax.ShapeDtypeStruct(shape, jnp.float32) for shape in shapes[1:]]
        + [jax.ShapeDtypeStruct((rows, modes), jnp.float32) for rows in (sums, 8)],
        compiler_params=params(24),
        name="base",
    )(in_hbm(amplitudes), in_hbm(upstream), keep, turned, ahead, back, *edges)


def absorb_rows(width, read, mask_ref, ahead_ref, adj_ref, before_ref, out_ref, sum_ref, *send_refs):
    _, variables, rows, lanes = out_ref.shape
    pushes = ahead_ref.shape[1]
    keep = kept_modes(mask_ref)

    @pl.when(pl.program_id(0) == 0)
    def _():
        sum_ref[...] = before_ref[...]

    for v in range(variables):
        for part in range(2):
            out_ref[part, v] = read(v, part).reshape(rows, lanes) * keep
    sides = [out_ref[part].reshape(variables * rows, lanes) for part in range(2)]
    for part in range(2):
        sum_ref[part * pushes : (part + 1) * pushes] += jnp.dot(
            ahead_ref[0], sides[part], precision=SPLIT, preferred_element_type=jnp.float32
        )
    real, imag = (adj_ref[part].reshape(variables * rows, lanes) for part in range(2))
    at = 2 * pushes
    sum_ref[at : at + 1] += total(real * sides[0] + imag * sides[1])
    sum_ref[at + 1 : at + 2] += total(real * sides[1] - imag * sides[0])

    if send_refs:

        @pl.when(pl.program_id(0) == pl.num_programs(0) - 1)
        def _():
            for d, send_ref in enumerate(send_refs, 1):
                pieces = []
                for part in range(2):
                    at = part * pushes + d * width
                    pieces.append(sum_ref[at : at + width])
                pieces.append(sum_ref[2 * pushes : 2 * pushes + 2])
                pack_rows(send_ref, jnp.concatenate(pieces, axis=0))


def folded(rows, modes):
    return rows == 12 and modes % 256 == 0 and modes <= 8 * NB


def travelling(rows, modes):
    if folded(rows, modes):
        return jax.ShapeDtypeStruct((rows - 4, modes + modes // 2), jnp.float32)
    return jax.ShapeDtypeStruct((padded(rows, 8), modes), jnp.float32)


def pack_rows(out_ref, value):
    rows, modes = value.shape
    if folded(rows, modes):
        half = modes // 2
        out_ref[:, :modes] = value[: rows - 4]
        out_ref[:4, modes:] = value[rows - 4 :, :half]
        out_ref[4:8, modes:] = value[rows - 4 :, half:]
        return
    out_ref[:rows] = value
    if out_ref.shape[0] > rows:
        out_ref[rows:] = jnp.zeros((out_ref.shape[0] - rows, modes), jnp.float32)


def absorb_body(width, in_ref, *refs):
    def read(v, part):
        return in_ref[:, v, :, part * NB : (part + 1) * NB]

    absorb_rows(width, read, *refs)


def absorb_apart_body(width, spans, place_ref, *refs):
    in_refs, refs, rows_ref = refs[:spans], refs[spans:-1], refs[-1]
    for i, in_ref in enumerate(in_refs):
        for j in range(in_ref.shape[0]):
            rows_ref[partner(place_ref, j, i, spans)] = in_ref[j]

    def read(v, part):
        return rows_ref[:, v, :, part * NB : (part + 1) * NB]

    absorb_rows(width, read, *refs)


def absorb(place, blocks, keep, ahead, adjoint_modes, before, width, sends):
    blocks = list(blocks)
    apart = place is not None
    _, variables, rows, modes = adjoint_modes.shape
    steps, pushes, depth = ahead.shape
    step = rows // steps
    grid_spec = pl.BlockSpec((2, variables, step, modes), lambda r: (0, 0, r, 0))
    _, _, freqs, lanes = blocks[0].shape
    sent = travelling(2 * width + 2, modes)
    operands = blocks + [keep, ahead, adjoint_modes if apart else in_hbm(adjoint_modes), before]
    in_specs = [
        whole(block)
        if apart
        else pl.BlockSpec((step, variables, freqs, lanes), lambda r: (r, 0, 0, 0))
        for block in blocks
    ] + [
        pl.BlockSpec((modes,), lambda r: (0,)),
        pl.BlockSpec((1, pushes, depth), lambda r: (r, 0, 0)),
        grid_spec,
        whole(before),
    ]
    body, scratch = functools.partial(absorb_body, width), []
    if apart:
        operands = [place] + operands
        in_specs = [pl.BlockSpec(memory_space=pltpu.SMEM)] + in_specs
        body = functools.partial(absorb_apart_body, width, len(blocks))
        scratch = [pltpu.VMEM((rows, variables, freqs, lanes), jnp.float32)]
    return pl.pallas_call(
        body,
        grid=(steps,),
        in_specs=in_specs,
        out_specs=[grid_spec, whole(before)] + [whole(sent)] * sends,
        out_shape=[
            jax.ShapeDtypeStruct((2, variables, rows, modes), jnp.float32),
            jax.ShapeDtypeStruct(before.shape, jnp.float32),
        ]
        + [sent] * sends,
        scratch_shapes=scratch,
        compiler_params=params(24),
        name="absorb_apart" if apart else "absorb",
    )(*operands)


def solve_body(side_ref, up_ref, mask_ref, inverse_ref, out_ref):
    _, variables, heights, lanes = out_ref.shape
    keep = kept_modes(mask_ref)
    spare = heights - side_ref.shape[2]
    for part in range(2):
        forced = side_ref[part]
        if spare:
            none = jnp.zeros((variables, spare, lanes), jnp.float32)
            forced = jnp.concatenate([forced, none], axis=1)
        side = (forced + up_ref[part] * keep).reshape(variables * heights, lanes)
        out_ref[part] = table_times(inverse_ref[...], side).reshape(variables, heights, lanes)


def solve(side, upstream, keep, inverse):
    _, variables, heights, modes = upstream.shape
    lanes = min(4 * NB, modes)
    spec = pl.BlockSpec((2, variables, heights, lanes), lambda i: (0, 0, 0, i))
    return pl.pallas_call(
        solve_body,
        grid=(modes // lanes,),
        in_specs=[
            pl.BlockSpec((2, variables, side.shape[2], lanes), lambda i: (0, 0, 0, i)),
            spec,
            pl.BlockSpec((lanes,), lambda i: (i,)),
            whole(inverse),
        ],
        out_specs=spec,
        out_shape=jax.ShapeDtypeStruct(upstream.shape, jnp.float32),
        compiler_params=params(32),
        name="solve",
    )(side, in_hbm(upstream), keep, inverse)


def solve_more_body(side_ref, before_ref, inverse_ref, out_ref):
    _, variables, heights, lanes = out_ref.shape
    for part in range(2):
        moved = table_times(inverse_ref[...], side_ref[part].reshape(-1, lanes))
        out_ref[part] = before_ref[part] + moved.reshape(variables, heights, lanes)


def solve_more(side, before, inverse):
    _, variables, rows, modes = side.shape
    lanes = min(4 * NB, modes)
    spec = pl.BlockSpec(before.shape[:3] + (lanes,), lambda i: (0, 0, 0, i))
    return pl.pallas_call(
        solve_more_body,
        grid=(modes // lanes,),
        in_specs=[
            pl.BlockSpec((2, variables, rows, lanes), lambda i: (0, 0, 0, i)),
            spec,
            whole(inverse),
        ],
        out_specs=spec,
        out_shape=jax.ShapeDtypeStruct(before.shape, jnp.float32),
        compiler_params=params(32),
        name="solve_more",
    )(side, before, inverse)


def finish_body(walls, width, fold, solved_ref, sum_ref, square_ref, *refs):
    each = 2 if fold else 1
    other_refs, (columns_ref, out_ref, shift_ref) = refs[: each * (walls - 1)], refs[-3:]
    _, variables, heights, lanes = out_ref.shape
    spare = columns_ref.shape[1] // 3 - width
    pushes = walls * width
    others = [ref[...] for ref in other_refs]
    if fold:
        first = pl.program_id(0) == 0
        others = [
            jnp.concatenate([rows, jnp.where(first, rest[:4], rest[4:8])], axis=0)
            for rows, rest in zip(others[::2], others[1::2])
        ]
    for part in range(2):
        push = sum_ref[part * pushes : part * pushes + width]
        for other in others:
            push = push + other[part * width : (part + 1) * width]
        if spare:
            push = jnp.concatenate([push, jnp.zeros((spare, lanes), jnp.float32)], axis=0)
        moved = table_times(columns_ref[...], push)
        out_ref[part] = solved_ref[part] - moved.reshape(variables, heights, lanes)
    both = sum_ref[2 * pushes : 2 * pushes + 2]
    for other in others:
        both = both + other[2 * width : 2 * width + 2]
    squares = square_ref[:1]
    weight = squares + epsilon
    shift_ref[0:1] = both[1:2] / weight
    shift_ref[1:2] = (squares - both[0:1]) / weight


def finish(solved, sums, squares, others, columns, width):
    _, variables, heights, modes = solved.shape
    fold = folded(2 * width + 2, modes)
    lanes = modes // 2 if fold else min(4 * NB, modes)

    def rows_spec(rows):
        return pl.BlockSpec((rows, lanes), lambda i: (0, i))

    spec = pl.BlockSpec((2, variables, heights, lanes), lambda i: (0, 0, 0, i))
    operands, in_specs = [solved, sums, squares], [spec]
    in_specs += [rows_spec(part.shape[0]) for part in (sums, squares)]
    for part in others:
        operands.append(part)
        in_specs.append(rows_spec(part.shape[0]))
        if fold:
            operands.append(part)
            in_specs.append(pl.BlockSpec((8, lanes), lambda i: (0, 2)))
    return pl.pallas_call(
        functools.partial(finish_body, len(others) + 1, width, fold),
        grid=(modes // lanes,),
        in_specs=in_specs + [whole(columns)],
        out_specs=[spec, pl.BlockSpec((2, lanes), lambda i: (0, i))],
        out_shape=[
            jax.ShapeDtypeStruct(solved.shape, jnp.float32),
            jax.ShapeDtypeStruct((2, modes), jnp.float32),
        ],
        compiler_params=params(32),
        name="finish",
    )(*operands, columns)


def around(block, axis):
    count = lax.axis_size(axis)
    return [block] + [
        lax.ppermute(block, axis, [(i, (i + d) % count) for i in range(count)])
        for d in range(1, count)
    ]


def hand_back(blocks, axis):
    count = lax.axis_size(axis)
    return [
        lax.ppermute(block, axis, [(i, (i - d) % count) for i in range(count)])
        for d, block in enumerate(blocks, 1)
    ]


PACKED_ROWS = 16


def pack_body(*refs):
    in_refs, out_ref = refs[:-1], refs[-1]
    out_ref[...] = jnp.zeros(out_ref.shape, jnp.float32)
    for i, ref in enumerate(in_refs):
        rows, columns = ref.shape[1:]
        out_ref[i, :rows, :columns] = ref[0]


def pack(parts):
    return pl.pallas_call(
        pack_body,
        out_shape=jax.ShapeDtypeStruct((len(parts), PACKED_ROWS, 128), jnp.float32),
        name="pack",
    )(*parts)


def upper_bits(value):
    return value.astype(jnp.bfloat16).astype(jnp.float32)


def split_columns(matrix):
    high = upper_bits(matrix)
    return jnp.concatenate([high, high, matrix - high], axis=1).astype(jnp.bfloat16)


def push_width(walls, variables):
    return variables if walls == 2 else 2 * variables


def constants_body(cuts, variables, walls, place_ref, inverse_ref, *refs):
    packed, refs = refs[:walls], refs[walls:]
    turned_ref, split_ref, last_ref, column_ref, edge_ref, ahead_ref, back_ref = refs[:7]
    row_refs, (all_ref, step_ref) = refs[7 : 7 + len(cuts)], refs[7 + len(cuts) :]
    extent = inverse_ref.shape[0]
    heights = extent // variables
    ends = 2 * variables
    width = push_width(walls, variables)
    matrix = inverse_ref[...]
    turned = matrix.T
    turned_ref[...] = split_columns(turned)
    split_ref[...] = split_columns(matrix)
    cut = cuts[-1]
    last = [matrix[:, v * heights : (v + 1) * heights][:, cut] for v in range(variables)]
    last_ref[...] = split_columns(jnp.concatenate(last, axis=1))

    def dot(a, b):
        return jnp.dot(a, b, precision=FULL, preferred_element_type=jnp.float32)

    def ends_of(value):
        low = [value[v * heights : v * heights + 1] for v in range(variables)]
        high = [value[(v + 1) * heights - 1 : (v + 1) * heights] for v in range(variables)]
        return jnp.concatenate(low, axis=0), jnp.concatenate(high, axis=0)

    def extended(value, rows):
        spare = rows - value.shape[0]
        if not spare:
            return value
        return jnp.concatenate([value, jnp.zeros((spare, value.shape[1]), jnp.float32)], axis=0)

    size = walls * PACKED_ROWS
    for d in range(walls):
        all_ref[(place_ref[0] - d + walls) % walls] = packed[d][...]

    def small(j, kind):
        return all_ref[j, kind][:, :PACKED_ROWS]

    row = lax.broadcasted_iota(jnp.int32, (PACKED_ROWS, size), 0)
    column = lax.broadcasted_iota(jnp.int32, (PACKED_ROWS, size), 1)
    units = []
    for j in range(walls):
        d = (place_ref[0] - j + walls) % walls
        hit = (column == d * ends + row) & (row < ends)
        units.append(jnp.where(hit, 1.0, 0.0))
    ahead = [units[0]]
    for j in range(1, walls):
        ahead.append(units[j] - dot(small(j, 2), ahead[j - 1]))
    interface = [None] * walls
    interface[-1] = dot(small(walls - 1, 4), ahead[-1])
    for j in range(walls - 2, -1, -1):
        interface[j] = dot(small(j, 4), ahead[j] - dot(small(j, 3), interface[j + 1]))
    none = jnp.zeros((variables, size), jnp.float32)
    for j in range(walls):
        under, over = none, none
        if j > 0:
            lower = extended(interface[j - 1][variables:], PACKED_ROWS)
            under = dot(small(j, 0), lower)[:variables]
        if j < walls - 1:
            over = dot(small(j, 1), interface[j + 1])[:variables]
        push = under + over if walls == 2 else jnp.concatenate([under, over], axis=0)
        step_ref[(place_ref[0] - j + walls) % walls] = extended(push, PACKED_ROWS)

    low, high = ends_of(matrix)
    bounds = extended(jnp.concatenate([low, high], axis=0), PACKED_ROWS)
    steps = [step_ref[d][:width, :PACKED_ROWS] for d in range(walls)]
    steps = [jnp.where(column[:width, :PACKED_ROWS] < ends, step, 0.0) for step in steps]
    pushes = dot(jnp.concatenate(steps, axis=0), bounds)
    for cut, row_ref in zip(cuts, row_refs):
        step = row_step(cut.stop - cut.start)
        for r in range(row_ref.shape[0]):
            at = cut.start + r * step
            pieces = [pushes[:, v * heights + at : v * heights + at + step] for v in range(variables)]
            row_ref[r] = jnp.concatenate(pieces, axis=1)
    pushes = extended(pushes, ahead_ref.shape[0])
    ahead_ref[...] = split_columns(pushes)
    back_ref[...] = split_columns(pushes.T)
    low, high = ends_of(turned)
    edge = jnp.concatenate([low, high], axis=0)
    if walls == 2:
        edge = jnp.where(place_ref[0] == 0, high, low)
    edge = extended(edge, edge_ref.shape[0])
    edge_ref[...] = split_columns(edge)
    column_ref[...] = split_columns(edge.T)


def constants(place, inverse, packed, cuts, variables):
    walls = len(packed)
    extent = inverse.shape[0]
    width = push_width(walls, variables)
    lengths = [cut.stop - cut.start for cut in cuts]
    size = walls * PACKED_ROWS
    pushes, edge_rows = padded(walls * width, 16), padded(width, 16)

    def split_shape(rows, columns):
        return jax.ShapeDtypeStruct((rows, 3 * columns), jnp.bfloat16)

    return pl.pallas_call(
        functools.partial(constants_body, cuts, variables, walls),
        in_specs=[pl.BlockSpec(memory_space=pltpu.SMEM)]
        + [pl.BlockSpec(memory_space=pltpu.VMEM)] * (1 + walls),
        out_shape=[
            split_shape(extent, extent),
            split_shape(extent, extent),
            split_shape(extent, variables * lengths[-1]),
            split_shape(extent, edge_rows),
            split_shape(edge_rows, extent),
            split_shape(pushes, extent),
            split_shape(extent, pushes),
        ]
        + [
            jax.ShapeDtypeStruct(
                (n // row_step(n), walls * width, variables * row_step(n)), jnp.float32
            )
            for n in lengths
        ],
        scratch_shapes=[
            pltpu.VMEM((walls,) + packed[0].shape, jnp.float32),
            pltpu.VMEM((walls, PACKED_ROWS, size), jnp.float32),
        ],
        compiler_params=params(),
        name="constants",
    )(place, inverse, *packed)


def local(
    amplitudes,
    upstream,
    harmonic_mask,
    quadratic_coefficients,
    slab_inverse,
    lower_coupling,
    upper_coupling,
    reduced_lower,
    reduced_upper,
    reduced_pivot,
):
    _, variables, heights, modes = amplitudes.shape
    axes = ("freq", "span")
    groups, spans = lax.axis_size("freq"), lax.axis_size("span")
    devices = groups * spans
    points = heights // devices
    apart = points > 1 and groups & (groups - 1) == 0 and spans & (spans - 1) == 0
    edge_at = heights - devices if apart else heights
    cuts = [slice(0, edge_at)] + ([slice(edge_at, heights)] if apart else [])
    keep = harmonic_mask
    place = jnp.stack([lax.axis_index("freq"), lax.axis_index("span")]).astype(jnp.int32)
    wall = lax.axis_index("wall").reshape(1).astype(jnp.int32)
    transforms = tables()
    coefficients = quadratic_coefficients.reshape(variables * variables, variables)

    def exchange(block):
        return lax.all_to_all(block, axes, split_axis=0, concat_axis=0, tiled=True)

    def swap(blocks, axis, only=None):
        count = len(blocks)
        return [
            lax.ppermute(block, axis, [(at, at ^ i) for at in range(count)])
            if i and (only is None or i in only)
            else block
            for i, block in enumerate(blocks)
        ]

    def regroup(blocks):
        return [jnp.stack([block[j] for block in blocks]) for j in range(blocks[0].shape[0])]

    far = {spans // 2}
    main = prepare(amplitudes, keep, cuts[0])
    if apart:
        main, amplitudes = lax.optimization_barrier((main, amplitudes))
        sent = prepare_apart(place, amplitudes, keep, cuts[1], groups, spans)
        arrived = swap(regroup(swap(sent, "freq")), "span", set(range(spans)) - far)
    main = exchange(main)

    inverse = slab_inverse[0]
    parts = (lower_coupling, upper_coupling, reduced_lower, reduced_upper, reduced_pivot)
    packed = around(pack(parts), "wall")
    turned, split, last, edge_columns, edge_rows, ahead, back, *rows = constants(
        wall, inverse, packed, cuts, variables
    )
    walls = len(packed)
    width = push_width(walls, variables)
    edges = around(edge(amplitudes, keep, edge_rows, width), "wall")
    *adjoint_modes, sums, squares = base(
        amplitudes, upstream, keep, turned, ahead, back, edges, width, cuts
    )
    if apart:
        held = (arrived[1], arrived[spans // 2], adjoint_modes, sums, squares)
        held = lax.optimization_barrier(held)
        arrived[1], arrived[spans // 2], adjoint_modes, sums, squares = held
        arrived = swap(arrived, "span", far)
    size = edge_at // devices
    shape = main.shape
    main = nonlinear(main.reshape((devices, size) + shape[1:]), coefficients, transforms)
    main = main.reshape(shape)
    if apart:
        main, arrived = lax.optimization_barrier((main, arrived))
    main = exchange(main)
    if apart:
        forced = nonlinear_apart(place, arrived, coefficients, transforms)
        returned = regroup(swap(forced, "freq"))
        returned = swap(returned, "span")

    sends = walls - 1
    side, sums, *sent = absorb(
        None, [main], keep, rows[0], adjoint_modes[0], sums, width, 0 if apart else sends
    )
    solved = solve(side, upstream, keep, split)
    if apart:
        solved, sums = lax.optimization_barrier((solved, sums))
        side, sums, *sent = absorb(
            place, returned, keep, rows[1], adjoint_modes[1], sums, width, sends
        )
    others = hand_back(sent, "wall")
    if apart:
        solved = solve_more(side, solved, last)
    new_amplitudes, wavenumber_shift = finish(solved, sums, squares, others, edge_columns, width)
    return (new_amplitudes, wavenumber_shift)


def solution(mesh):
    placed = (
        P(None, None, "wall", ("freq", "span")),
        P(None, None, "wall", ("freq", "span")),
        P(("freq", "span")),
        P(),
        P("wall", None, None),
        P("wall", None, None),
        P("wall", None, None),
        P("wall", None, None),
        P("wall", None, None),
        P("wall", None, None),
    )
    return jax.shard_map(
        local,
        mesh=mesh,
        in_specs=placed,
        out_specs=(P(None, None, "wall", ("freq", "span")), P(None, ("freq", "span"))),
        check_vma=False,
    )
```

```python
import functools
import math

import jax
import jax.numpy as jnp
import ml_dtypes
import numpy as np
from jax import lax
from jax.experimental import pallas as pl
from jax.experimental.pallas import tpu as pltpu
from jax.sharding import PartitionSpec as P

NF = 128
NB = 256

epsilon = 1e-06

SPLIT = lax.Precision.HIGH
FULL = lax.Precision.HIGHEST


def tables():
    def turns(length):
        counter = np.arange(length)
        angles = (counter[:, None] * counter[None, :] % length) * (2.0 * math.pi / length)
        return np.cos(angles), np.sin(angles)

    cos_time, sin_time = turns(NF)
    cos_span, sin_span = turns(NB)
    scale = 1.0 / math.sqrt(NF * NB)
    out = (
        (np.block([[cos_time, -sin_time], [sin_time, cos_time]]), 1),
        (np.concatenate([cos_span, -sin_span], 0) * scale, 0),
        (np.concatenate([cos_span, -sin_span], 1) * scale, 0),
        (np.block([[cos_time, sin_time], [-sin_time, cos_time]]), 1),
    )

    def split(table, axis):
        high = table.astype(ml_dtypes.bfloat16)
        low = (table - high.astype(np.float64)).astype(ml_dtypes.bfloat16)
        return jnp.asarray(np.concatenate([high, high, low], axis))

    return [split(table, axis) for table, axis in out]


def params(megabytes=16):
    return pltpu.CompilerParams(vmem_limit_bytes=megabytes * 1024 * 1024)


def whole(array):
    zeros = (0,) * len(array.shape)
    return pl.BlockSpec(array.shape, lambda *_: zeros)


def in_hbm(array):
    return pltpu.with_memory_space_constraint(array, pltpu.HBM)


def kept_modes(mask_ref):
    return mask_ref[...].astype(jnp.float32).reshape(1, -1)


def row_step(rows):
    return rows // 2 if rows % 16 == 0 and rows > 16 else rows


def prepare_body(x_ref, mask_ref, out_ref):
    keep = kept_modes(mask_ref)
    rows, variables, freqs, _ = out_ref.shape
    for v in range(variables):
        for part in range(2):
            kept = x_ref[part, v] * keep
            out_ref[:, v, :, part * NB : (part + 1) * NB] = kept.reshape(rows, freqs, NB)


def prepare(amplitudes, keep, cut):
    _, variables, _, modes = amplitudes.shape
    freqs = modes // NB
    rows = cut.stop - cut.start
    step = row_step(rows)
    at = cut.start // step
    return pl.pallas_call(
        prepare_body,
        grid=(rows // step,),
        in_specs=[
            pl.BlockSpec((2, variables, step, modes), lambda r: (0, 0, at + r, 0)),
            pl.BlockSpec((modes,), lambda r: (0,)),
        ],
        out_specs=pl.BlockSpec((step, variables, freqs, 2 * NB), lambda r: (r, 0, 0, 0)),
        out_shape=pltpu.HBM((rows, variables, freqs, 2 * NB), jnp.float32),
        compiler_params=params(24),
        name="prepare",
    )(in_hbm(amplitudes), in_hbm(keep))


def partner(place_ref, j, i, spans):
    return (place_ref[0] ^ j) * spans + (place_ref[1] ^ i)


def prepare_apart_body(place_ref, x_ref, mask_ref, *refs):
    out_refs, rows_ref = refs[:-1], refs[-1]
    keep = kept_modes(mask_ref)
    rows, freqs, _ = rows_ref.shape
    spans = out_refs[0].shape[0]
    for part in range(2):
        kept = x_ref[part, 0] * keep
        rows_ref[:, :, part * NB : (part + 1) * NB] = kept.reshape(rows, freqs, NB)
    for j, out_ref in enumerate(out_refs):
        for i in range(spans):
            out_ref[i, 0] = rows_ref[partner(place_ref, j, i, spans)]


def prepare_apart(place, amplitudes, keep, cut, groups, spans):
    _, variables, _, modes = amplitudes.shape
    freqs = modes // NB
    rows = cut.stop - cut.start
    at = cut.start // rows
    return pl.pallas_call(
        prepare_apart_body,
        grid=(variables,),
        in_specs=[
            pl.BlockSpec(memory_space=pltpu.SMEM),
            pl.BlockSpec((2, 1, rows, modes), lambda v: (0, v, at, 0)),
            pl.BlockSpec((modes,), lambda v: (0,)),
        ],
        out_specs=[pl.BlockSpec((spans, 1, freqs, 2 * NB), lambda v: (0, v, 0, 0))] * groups,
        out_shape=[jax.ShapeDtypeStruct((spans, variables, freqs, 2 * NB), jnp.float32)] * groups,
        scratch_shapes=[pltpu.VMEM((rows, freqs, 2 * NB), jnp.float32)],
        compiler_params=params(),
        name="prepare_apart",
    )(place, in_hbm(amplitudes), keep)


def halves(value):
    high = value.astype(jnp.bfloat16)
    return high, (value - high.astype(jnp.float32)).astype(jnp.bfloat16)


def table_times(table, value):
    high, low = halves(value)
    value = jnp.concatenate([high, low, high], axis=0)
    return jnp.dot(table, value, preferred_element_type=jnp.float32)


def times_table(value, table):
    high, low = halves(value)
    value = jnp.concatenate([high, low, high], axis=1)
    return jnp.dot(value, table, preferred_element_type=jnp.float32)


def transform(read, write, q_ref, table_refs, field_ref, force_ref):
    wi_ref, ei_ref, ef_ref, wf_ref = table_refs
    variables = field_ref.shape[0]
    for v in range(variables):
        modes = read(v)
        stacked = jnp.concatenate([modes[:, :NB], modes[:, NB:]], axis=0)
        turned = table_times(wi_ref[...], stacked)
        beside = jnp.concatenate([turned[:NF], turned[NF:]], axis=1)
        field_ref[v] = times_table(beside, ei_ref[...])
    pairs = [(a, b) for a in range(variables) for b in range(a + 1, variables)]
    weights = [
        [q_ref[w * variables + a, b] + q_ref[w * variables + b, a] for a, b in pairs]
        for w in range(variables)
    ]
    step = 8
    for row in range(0, NF, step):
        at = slice(row, row + step)
        values = [field_ref[v, at] for v in range(variables)]
        total = [None] * variables
        for i, (a, b) in enumerate(pairs):
            product = values[a] * values[b]
            for w in range(variables):
                term = weights[w][i] * product
                total[w] = term if total[w] is None else total[w] + term
        for w in range(variables):
            force_ref[w, at] = total[w]
    for w in range(variables):
        spread = times_table(force_ref[w], ef_ref[...])
        stacked = jnp.concatenate([spread[:, :NB], spread[:, NB:]], axis=0)
        turned = table_times(wf_ref[...], stacked)
        for part in range(2):
            write(w, part, turned[part * NF : (part + 1) * NF])


def nonlinear_body(q_ref, in_ref, *refs):
    table_refs, out_ref, work_refs = refs[:4], refs[4], refs[5:]
    devices, _, _, freqs, _ = in_ref.shape

    def read(v):
        return in_ref[:, 0, v].reshape(NF, 2 * NB)

    def write(w, part, piece):
        at = slice(part * NB, (part + 1) * NB)
        out_ref[:, 0, w, :, at] = piece.reshape(devices, freqs, NB)

    transform(read, write, q_ref, table_refs, *work_refs)


def work_shapes(variables):
    return [pltpu.VMEM((variables, NF, NB), jnp.float32)] * 2


def nonlinear_cost(points, variables):
    return pl.CostEstimate(
        flops=points * variables * 12 * NF * NB * (NF + NB) * 2,
        bytes_accessed=points * variables * NF * NB * 16,
        transcendentals=0,
    )


def nonlinear(block, coefficients, transforms):
    devices, points, variables, freqs, lanes = block.shape
    spec = pl.BlockSpec((devices, 1, variables, freqs, lanes), lambda j: (0, j, 0, 0, 0))
    return pl.pallas_call(
        nonlinear_body,
        grid=(points,),
        in_specs=[pl.BlockSpec(memory_space=pltpu.SMEM), spec] + [whole(t) for t in transforms],
        out_specs=spec,
        out_shape=pltpu.HBM(block.shape, jnp.float32),
        scratch_shapes=work_shapes(variables),
        compiler_params=params(24),
        cost_estimate=nonlinear_cost(points, variables),
        name="nonlinear",
    )(coefficients, block, *[in_hbm(table) for table in transforms])


def nonlinear_apart_body(groups, spans, place_ref, q_ref, *refs):
    in_refs, refs = refs[:spans], refs[spans:]
    table_refs, refs = refs[:4], refs[4:]
    out_refs, refs = refs[:groups], refs[groups:]
    rows_ref, work_refs = refs[0], refs[1:]
    devices, _, freqs, _ = rows_ref.shape
    for j in range(groups):
        for i in range(spans):
            rows_ref[partner(place_ref, j, i, spans)] = in_refs[i][j]

    def read(v):
        return rows_ref[:, v].reshape(NF, 2 * NB)

    def write(w, part, piece):
        at = slice(part * NB, (part + 1) * NB)
        rows_ref[:, w, :, at] = piece.reshape(devices, freqs, NB)

    transform(read, write, q_ref, table_refs, *work_refs)
    for j in range(groups):
        for i in range(spans):
            out_refs[j][i] = rows_ref[partner(place_ref, j, i, spans)]


def nonlinear_apart(place, blocks, coefficients, transforms):
    spans = len(blocks)
    groups, variables, freqs, lanes = blocks[0].shape
    result = jax.ShapeDtypeStruct((spans, variables, freqs, lanes), jnp.float32)
    smem = pl.BlockSpec(memory_space=pltpu.SMEM)
    return pl.pallas_call(
        functools.partial(nonlinear_apart_body, groups, spans),
        grid=(1,),
        in_specs=[smem, smem]
        + [whole(block) for block in blocks]
        + [whole(table) for table in transforms],
        out_specs=[whole(result)] * groups,
        out_shape=[result] * groups,
        scratch_shapes=[pltpu.VMEM((groups * spans, variables, freqs, lanes), jnp.float32)]
        + work_shapes(variables),
        compiler_params=params(24),
        cost_estimate=nonlinear_cost(1, variables),
        name="nonlinear_apart",
    )(place, coefficients, *blocks, *[in_hbm(table) for table in transforms])


def total(value):
    return jnp.sum(value, axis=0, keepdims=True)


def padded(rows, multiple):
    return rows + -rows % multiple


def edge_body(width, x_ref, mask_ref, rows_ref, out_ref):
    _, variables, heights, lanes = x_ref.shape
    keep = kept_modes(mask_ref)
    squares = 0.0
    out_ref[...] = jnp.zeros(out_ref.shape, jnp.float32)
    for part in range(2):
        kept = x_ref[part].reshape(variables * heights, lanes) * keep
        squares = squares + total(kept * kept)
        out_ref[part * width : (part + 1) * width] = table_times(rows_ref[...], kept)[:width]
    out_ref[2 * width : 2 * width + 1] = squares


def edge(amplitudes, keep, rows, width):
    _, variables, heights, modes = amplitudes.shape
    length = padded(2 * width + 1, 8)
    return pl.pallas_call(
        functools.partial(edge_body, width),
        grid=(modes // NB,),
        in_specs=[
            pl.BlockSpec((2, variables, heights, NB), lambda i: (0, 0, 0, i)),
            pl.BlockSpec((NB,), lambda i: (i,)),
            whole(rows),
        ],
        out_specs=pl.BlockSpec((length, NB), lambda i: (0, i)),
        out_shape=jax.ShapeDtypeStruct((length, modes), jnp.float32),
        compiler_params=params(),
        name="edge",
    )(in_hbm(amplitudes), keep, rows)


def base_body(cuts, walls, width, x_ref, up_ref, mask_ref, turned_ref, ahead_ref, back_ref, *refs):
    edges, refs = refs[:walls], refs[walls:]
    out_refs, (sum_ref, square_ref) = refs[: len(cuts)], refs[len(cuts) :]
    _, variables, heights, lanes = x_ref.shape
    extent = variables * heights
    pushes = walls * width
    spare = back_ref.shape[1] // 3 - pushes
    keep = kept_modes(mask_ref)
    moved, sides = [], []
    sum_ref[...] = jnp.zeros(sum_ref.shape, jnp.float32)
    for part in range(2):
        kept = x_ref[part].reshape(extent, lanes) * keep
        taken = [ref[part * width : (part + 1) * width] for ref in edges]
        if spare:
            taken.append(jnp.zeros((spare, lanes), jnp.float32))
        taken = jnp.concatenate(taken, axis=0)
        moved.append(table_times(turned_ref[...], kept) - table_times(back_ref[...], taken))
        grid = moved[part].reshape(variables, heights, lanes)
        for cut, out_ref in zip(cuts, out_refs):
            out_ref[part] = grid[:, cut]
        sides.append(up_ref[part].reshape(extent, lanes) * keep)
        added = table_times(ahead_ref[...], sides[part])
        sum_ref[part * pushes : (part + 1) * pushes] = added[:pushes]
    row = 2 * pushes
    sum_ref[row : row + 1] = total(moved[0] * sides[0] + moved[1] * sides[1])
    sum_ref[row + 1 : row + 2] = total(moved[0] * sides[1] - moved[1] * sides[0])
    squares = sum(ref[2 * width : 2 * width + 1] for ref in edges)
    square_ref[...] = jnp.broadcast_to(squares, square_ref.shape)


def base(amplitudes, upstream, keep, turned, ahead, back, edges, width, cuts):
    _, variables, heights, modes = amplitudes.shape
    walls = len(edges)
    lengths = [cut.stop - cut.start for cut in cuts]
    shapes = [(2, variables, rows, modes) for rows in lengths]
    sums = padded(2 * walls * width + 2, 8)
    spec = pl.BlockSpec((2, variables, heights, NB), lambda i: (0, 0, 0, i))

    def rows_spec(rows):
        return pl.BlockSpec((rows, NB), lambda i: (0, i))

    return pl.pallas_call(
        functools.partial(base_body, cuts, walls, width),
        grid=(modes // NB,),
        in_specs=[spec] * 2
        + [pl.BlockSpec((NB,), lambda i: (i,)), whole(turned), whole(ahead), whole(back)]
        + [rows_spec(part.shape[0]) for part in edges],
        out_specs=[
            pl.BlockSpec((2, variables, rows, NB), lambda i: (0, 0, 0, i)) for rows in lengths
        ]
        + [rows_spec(sums), rows_spec(8)],
        out_shape=[pltpu.HBM(shapes[0], jnp.float32)]
        + [jax.ShapeDtypeStruct(shape, jnp.float32) for shape in shapes[1:]]
        + [jax.ShapeDtypeStruct((rows, modes), jnp.float32) for rows in (sums, 8)],
        compiler_params=params(24),
        name="base",
    )(in_hbm(amplitudes), in_hbm(upstream), keep, turned, ahead, back, *edges)


def absorb_rows(width, read, mask_ref, ahead_ref, adj_ref, before_ref, out_ref, sum_ref, *send_refs):
    _, variables, rows, lanes = out_ref.shape
    pushes = ahead_ref.shape[1]
    keep = kept_modes(mask_ref)

    @pl.when(pl.program_id(0) == 0)
    def _():
        sum_ref[...] = before_ref[...]

    for v in range(variables):
        for part in range(2):
            out_ref[part, v] = read(v, part).reshape(rows, lanes) * keep
    sides = [out_ref[part].reshape(variables * rows, lanes) for part in range(2)]
    for part in range(2):
        sum_ref[part * pushes : (part + 1) * pushes] += jnp.dot(
            ahead_ref[0], sides[part], precision=SPLIT, preferred_element_type=jnp.float32
        )
    real, imag = (adj_ref[part].reshape(variables * rows, lanes) for part in range(2))
    at = 2 * pushes
    sum_ref[at : at + 1] += total(real * sides[0] + imag * sides[1])
    sum_ref[at + 1 : at + 2] += total(real * sides[1] - imag * sides[0])

    if send_refs:

        @pl.when(pl.program_id(0) == pl.num_programs(0) - 1)
        def _():
            for d, send_ref in enumerate(send_refs, 1):
                pieces = []
                for part in range(2):
                    at = part * pushes + d * width
                    pieces.append(sum_ref[at : at + width])
                pieces.append(sum_ref[2 * pushes : 2 * pushes + 2])
                pack_rows(send_ref, jnp.concatenate(pieces, axis=0))


def folded(rows, modes):
    return rows == 12 and modes % 256 == 0 and modes <= 8 * NB


def travelling(rows, modes):
    if folded(rows, modes):
        return jax.ShapeDtypeStruct((rows - 4, modes + modes // 2), jnp.float32)
    return jax.ShapeDtypeStruct((padded(rows, 8), modes), jnp.float32)


def pack_rows(out_ref, value):
    rows, modes = value.shape
    if folded(rows, modes):
        half = modes // 2
        out_ref[:, :modes] = value[: rows - 4]
        out_ref[:4, modes:] = value[rows - 4 :, :half]
        out_ref[4:8, modes:] = value[rows - 4 :, half:]
        return
    out_ref[:rows] = value
    if out_ref.shape[0] > rows:
        out_ref[rows:] = jnp.zeros((out_ref.shape[0] - rows, modes), jnp.float32)


def absorb_body(width, in_ref, *refs):
    def read(v, part):
        return in_ref[:, v, :, part * NB : (part + 1) * NB]

    absorb_rows(width, read, *refs)


def absorb_apart_body(width, spans, place_ref, *refs):
    in_refs, refs, rows_ref = refs[:spans], refs[spans:-1], refs[-1]
    for i, in_ref in enumerate(in_refs):
        for j in range(in_ref.shape[0]):
            rows_ref[partner(place_ref, j, i, spans)] = in_ref[j]

    def read(v, part):
        return rows_ref[:, v, :, part * NB : (part + 1) * NB]

    absorb_rows(width, read, *refs)


def absorb(place, blocks, keep, ahead, adjoint_modes, before, width, sends):
    blocks = list(blocks)
    apart = place is not None
    _, variables, rows, modes = adjoint_modes.shape
    steps, pushes, depth = ahead.shape
    step = rows // steps
    grid_spec = pl.BlockSpec((2, variables, step, modes), lambda r: (0, 0, r, 0))
    _, _, freqs, lanes = blocks[0].shape
    sent = travelling(2 * width + 2, modes)
    operands = blocks + [keep, ahead, adjoint_modes if apart else in_hbm(adjoint_modes), before]
    in_specs = [
        whole(block)
        if apart
        else pl.BlockSpec((step, variables, freqs, lanes), lambda r: (r, 0, 0, 0))
        for block in blocks
    ] + [
        pl.BlockSpec((modes,), lambda r: (0,)),
        pl.BlockSpec((1, pushes, depth), lambda r: (r, 0, 0)),
        grid_spec,
        whole(before),
    ]
    body, scratch = functools.partial(absorb_body, width), []
    if apart:
        operands = [place] + operands
        in_specs = [pl.BlockSpec(memory_space=pltpu.SMEM)] + in_specs
        body = functools.partial(absorb_apart_body, width, len(blocks))
        scratch = [pltpu.VMEM((rows, variables, freqs, lanes), jnp.float32)]
    return pl.pallas_call(
        body,
        grid=(steps,),
        in_specs=in_specs,
        out_specs=[grid_spec, whole(before)] + [whole(sent)] * sends,
        out_shape=[
            jax.ShapeDtypeStruct((2, variables, rows, modes), jnp.float32),
            jax.ShapeDtypeStruct(before.shape, jnp.float32),
        ]
        + [sent] * sends,
        scratch_shapes=scratch,
        compiler_params=params(24),
        name="absorb_apart" if apart else "absorb",
    )(*operands)


def solve_body(side_ref, up_ref, mask_ref, inverse_ref, out_ref):
    _, variables, heights, lanes = out_ref.shape
    keep = kept_modes(mask_ref)
    spare = heights - side_ref.shape[2]
    for part in range(2):
        forced = side_ref[part]
        if spare:
            none = jnp.zeros((variables, spare, lanes), jnp.float32)
            forced = jnp.concatenate([forced, none], axis=1)
        side = (forced + up_ref[part] * keep).reshape(variables * heights, lanes)
        out_ref[part] = table_times(inverse_ref[...], side).reshape(variables, heights, lanes)


def solve(side, upstream, keep, inverse):
    _, variables, heights, modes = upstream.shape
    lanes = min(4 * NB, modes)
    spec = pl.BlockSpec((2, variables, heights, lanes), lambda i: (0, 0, 0, i))
    return pl.pallas_call(
        solve_body,
        grid=(modes // lanes,),
        in_specs=[
            pl.BlockSpec((2, variables, side.shape[2], lanes), lambda i: (0, 0, 0, i)),
            spec,
            pl.BlockSpec((lanes,), lambda i: (i,)),
            whole(inverse),
        ],
        out_specs=spec,
        out_shape=jax.ShapeDtypeStruct(upstream.shape, jnp.float32),
        compiler_params=params(32),
        name="solve",
    )(side, in_hbm(upstream), keep, inverse)


def solve_more_body(side_ref, before_ref, inverse_ref, out_ref):
    _, variables, heights, lanes = out_ref.shape
    for part in range(2):
        moved = table_times(inverse_ref[...], side_ref[part].reshape(-1, lanes))
        out_ref[part] = before_ref[part] + moved.reshape(variables, heights, lanes)


def solve_more(side, before, inverse):
    _, variables, rows, modes = side.shape
    lanes = min(4 * NB, modes)
    spec = pl.BlockSpec(before.shape[:3] + (lanes,), lambda i: (0, 0, 0, i))
    return pl.pallas_call(
        solve_more_body,
        grid=(modes // lanes,),
        in_specs=[
            pl.BlockSpec((2, variables, rows, lanes), lambda i: (0, 0, 0, i)),
            spec,
            whole(inverse),
        ],
        out_specs=spec,
        out_shape=jax.ShapeDtypeStruct(before.shape, jnp.float32),
        compiler_params=params(32),
        name="solve_more",
    )(side, before, inverse)


def finish_body(walls, width, fold, solved_ref, sum_ref, square_ref, *refs):
    each = 2 if fold else 1
    other_refs, (columns_ref, out_ref, shift_ref) = refs[: each * (walls - 1)], refs[-3:]
    _, variables, heights, lanes = out_ref.shape
    spare = columns_ref.shape[1] // 3 - width
    pushes = walls * width
    others = [ref[...] for ref in other_refs]
    if fold:
        first = pl.program_id(0) == 0
        others = [
            jnp.concatenate([rows, jnp.where(first, rest[:4], rest[4:8])], axis=0)
            for rows, rest in zip(others[::2], others[1::2])
        ]
    for part in range(2):
        push = sum_ref[part * pushes : part * pushes + width]
        for other in others:
            push = push + other[part * width : (part + 1) * width]
        if spare:
            push = jnp.concatenate([push, jnp.zeros((spare, lanes), jnp.float32)], axis=0)
        moved = table_times(columns_ref[...], push)
        out_ref[part] = solved_ref[part] - moved.reshape(variables, heights, lanes)
    both = sum_ref[2 * pushes : 2 * pushes + 2]
    for other in others:
        both = both + other[2 * width : 2 * width + 2]
    squares = square_ref[:1]
    weight = squares + epsilon
    shift_ref[0:1] = both[1:2] / weight
    shift_ref[1:2] = (squares - both[0:1]) / weight


def finish(solved, sums, squares, others, columns, width):
    _, variables, heights, modes = solved.shape
    fold = folded(2 * width + 2, modes)
    lanes = modes // 2 if fold else min(4 * NB, modes)

    def rows_spec(rows):
        return pl.BlockSpec((rows, lanes), lambda i: (0, i))

    spec = pl.BlockSpec((2, variables, heights, lanes), lambda i: (0, 0, 0, i))
    operands, in_specs = [solved, sums, squares], [spec]
    in_specs += [rows_spec(part.shape[0]) for part in (sums, squares)]
    for part in others:
        operands.append(part)
        in_specs.append(rows_spec(part.shape[0]))
        if fold:
            operands.append(part)
            in_specs.append(pl.BlockSpec((8, lanes), lambda i: (0, 2)))
    return pl.pallas_call(
        functools.partial(finish_body, len(others) + 1, width, fold),
        grid=(modes // lanes,),
        in_specs=in_specs + [whole(columns)],
        out_specs=[spec, pl.BlockSpec((2, lanes), lambda i: (0, i))],
        out_shape=[
            jax.ShapeDtypeStruct(solved.shape, jnp.float32),
            jax.ShapeDtypeStruct((2, modes), jnp.float32),
        ],
        compiler_params=params(32),
        name="finish",
    )(*operands, columns)


def around(block, axis):
    count = lax.axis_size(axis)
    return [block] + [
        lax.ppermute(block, axis, [(i, (i + d) % count) for i in range(count)])
        for d in range(1, count)
    ]


def hand_back(blocks, axis):
    count = lax.axis_size(axis)
    return [
        lax.ppermute(block, axis, [(i, (i - d) % count) for i in range(count)])
        for d, block in enumerate(blocks, 1)
    ]


PACKED_ROWS = 16


def pack_body(*refs):
    in_refs, out_ref = refs[:-1], refs[-1]
    out_ref[...] = jnp.zeros(out_ref.shape, jnp.float32)
    for i, ref in enumerate(in_refs):
        rows, columns = ref.shape[1:]
        out_ref[i, :rows, :columns] = ref[0]


def pack(parts):
    return pl.pallas_call(
        pack_body,
        out_shape=jax.ShapeDtypeStruct((len(parts), PACKED_ROWS, 128), jnp.float32),
        name="pack",
    )(*parts)


def upper_bits(value):
    return value.astype(jnp.bfloat16).astype(jnp.float32)


def split_columns(matrix):
    high = upper_bits(matrix)
    return jnp.concatenate([high, high, matrix - high], axis=1).astype(jnp.bfloat16)


def push_width(walls, variables):
    return variables if walls == 2 else 2 * variables


def constants_body(cuts, variables, walls, place_ref, inverse_ref, *refs):
    packed, refs = refs[:walls], refs[walls:]
    turned_ref, split_ref, last_ref, column_ref, edge_ref, ahead_ref, back_ref = refs[:7]
    row_refs, (all_ref, step_ref) = refs[7 : 7 + len(cuts)], refs[7 + len(cuts) :]
    extent = inverse_ref.shape[0]
    heights = extent // variables
    ends = 2 * variables
    width = push_width(walls, variables)
    matrix = inverse_ref[...]
    turned = matrix.T
    turned_ref[...] = split_columns(turned)
    split_ref[...] = split_columns(matrix)
    cut = cuts[-1]
    last = [matrix[:, v * heights : (v + 1) * heights][:, cut] for v in range(variables)]
    last_ref[...] = split_columns(jnp.concatenate(last, axis=1))

    def dot(a, b):
        return jnp.dot(a, b, precision=FULL, preferred_element_type=jnp.float32)

    def ends_of(value):
        low = [value[v * heights : v * heights + 1] for v in range(variables)]
        high = [value[(v + 1) * heights - 1 : (v + 1) * heights] for v in range(variables)]
        return jnp.concatenate(low, axis=0), jnp.concatenate(high, axis=0)

    def extended(value, rows):
        spare = rows - value.shape[0]
        if not spare:
            return value
        return jnp.concatenate([value, jnp.zeros((spare, value.shape[1]), jnp.float32)], axis=0)

    size = walls * PACKED_ROWS
    for d in range(walls):
        all_ref[(place_ref[0] - d + walls) % walls] = packed[d][...]

    def small(j, kind):
        return all_ref[j, kind][:, :PACKED_ROWS]

    row = lax.broadcasted_iota(jnp.int32, (PACKED_ROWS, size), 0)
    column = lax.broadcasted_iota(jnp.int32, (PACKED_ROWS, size), 1)
    units = []
    for j in range(walls):
        d = (place_ref[0] - j + walls) % walls
        hit = (column == d * ends + row) & (row < ends)
        units.append(jnp.where(hit, 1.0, 0.0))
    ahead = [units[0]]
    for j in range(1, walls):
        ahead.append(units[j] - dot(small(j, 2), ahead[j - 1]))
    interface = [None] * walls
    interface[-1] = dot(small(walls - 1, 4), ahead[-1])
    for j in range(walls - 2, -1, -1):
        interface[j] = dot(small(j, 4), ahead[j] - dot(small(j, 3), interface[j + 1]))
    none = jnp.zeros((variables, size), jnp.float32)
    for j in range(walls):
        under, over = none, none
        if j > 0:
            lower = extended(interface[j - 1][variables:], PACKED_ROWS)
            under = dot(small(j, 0), lower)[:variables]
        if j < walls - 1:
            over = dot(small(j, 1), interface[j + 1])[:variables]
        push = under + over if walls == 2 else jnp.concatenate([under, over], axis=0)
        step_ref[(place_ref[0] - j + walls) % walls] = extended(push, PACKED_ROWS)

    low, high = ends_of(matrix)
    bounds = extended(jnp.concatenate([low, high], axis=0), PACKED_ROWS)
    steps = [step_ref[d][:width, :PACKED_ROWS] for d in range(walls)]
    steps = [jnp.where(column[:width, :PACKED_ROWS] < ends, step, 0.0) for step in steps]
    pushes = dot(jnp.concatenate(steps, axis=0), bounds)
    for cut, row_ref in zip(cuts, row_refs):
        step = row_step(cut.stop - cut.start)
        for r in range(row_ref.shape[0]):
            at = cut.start + r * step
            pieces = [pushes[:, v * heights + at : v * heights + at + step] for v in range(variables)]
            row_ref[r] = jnp.concatenate(pieces, axis=1)
    pushes = extended(pushes, ahead_ref.shape[0])
    ahead_ref[...] = split_columns(pushes)
    back_ref[...] = split_columns(pushes.T)
    low, high = ends_of(turned)
    edge = jnp.concatenate([low, high], axis=0)
    if walls == 2:
        edge = jnp.where(place_ref[0] == 0, high, low)
    edge = extended(edge, edge_ref.shape[0])
    edge_ref[...] = split_columns(edge)
    column_ref[...] = split_columns(edge.T)


def constants(place, inverse, packed, cuts, variables):
    walls = len(packed)
    extent = inverse.shape[0]
    width = push_width(walls, variables)
    lengths = [cut.stop - cut.start for cut in cuts]
    size = walls * PACKED_ROWS
    pushes, edge_rows = padded(walls * width, 16), padded(width, 16)

    def split_shape(rows, columns):
        return jax.ShapeDtypeStruct((rows, 3 * columns), jnp.bfloat16)

    return pl.pallas_call(
        functools.partial(constants_body, cuts, variables, walls),
        in_specs=[pl.BlockSpec(memory_space=pltpu.SMEM)]
        + [pl.BlockSpec(memory_space=pltpu.VMEM)] * (1 + walls),
        out_shape=[
            split_shape(extent, extent),
            split_shape(extent, extent),
            split_shape(extent, variables * lengths[-1]),
            split_shape(extent, edge_rows),
            split_shape(edge_rows, extent),
            split_shape(pushes, extent),
            split_shape(extent, pushes),
        ]
        + [
            jax.ShapeDtypeStruct(
                (n // row_step(n), walls * width, variables * row_step(n)), jnp.float32
            )
            for n in lengths
        ],
        scratch_shapes=[
            pltpu.VMEM((walls,) + packed[0].shape, jnp.float32),
            pltpu.VMEM((walls, PACKED_ROWS, size), jnp.float32),
        ],
        compiler_params=params(),
        name="constants",
    )(place, inverse, *packed)


def local(
    amplitudes,
    upstream,
    harmonic_mask,
    quadratic_coefficients,
    slab_inverse,
    lower_coupling,
    upper_coupling,
    reduced_lower,
    reduced_upper,
    reduced_pivot,
):
    _, variables, heights, modes = amplitudes.shape
    axes = ("freq", "span")
    groups, spans = lax.axis_size("freq"), lax.axis_size("span")
    devices = groups * spans
    points = heights // devices
    apart = points > 1 and groups & (groups - 1) == 0 and spans & (spans - 1) == 0
    edge_at = heights - devices if apart else heights
    cuts = [slice(0, edge_at)] + ([slice(edge_at, heights)] if apart else [])
    keep = harmonic_mask
    place = jnp.stack([lax.axis_index("freq"), lax.axis_index("span")]).astype(jnp.int32)
    wall = lax.axis_index("wall").reshape(1).astype(jnp.int32)
    transforms = tables()
    coefficients = quadratic_coefficients.reshape(variables * variables, variables)

    def exchange(block):
        return lax.all_to_all(block, axes, split_axis=0, concat_axis=0, tiled=True)

    def swap(blocks, axis):
        count = len(blocks)
        return [blocks[0]] + [
            lax.ppermute(blocks[i], axis, [(at, at ^ i) for at in range(count)])
            for i in range(1, count)
        ]

    def regroup(blocks):
        return [jnp.stack([block[j] for block in blocks]) for j in range(blocks[0].shape[0])]

    main = prepare(amplitudes, keep, cuts[0])
    if apart:
        main, amplitudes = lax.optimization_barrier((main, amplitudes))
        sent = prepare_apart(place, amplitudes, keep, cuts[1], groups, spans)
        arrived = swap(regroup(swap(sent, "freq")), "span")
    main = exchange(main)

    inverse = slab_inverse[0]
    parts = (lower_coupling, upper_coupling, reduced_lower, reduced_upper, reduced_pivot)
    packed = around(pack(parts), "wall")
    turned, split, last, edge_columns, edge_rows, ahead, back, *rows = constants(
        wall, inverse, packed, cuts, variables
    )
    walls = len(packed)
    width = push_width(walls, variables)
    edges = around(edge(amplitudes, keep, edge_rows, width), "wall")
    *adjoint_modes, sums, squares = base(
        amplitudes, upstream, keep, turned, ahead, back, edges, width, cuts
    )
    size = edge_at // devices
    shape = main.shape
    main = nonlinear(main.reshape((devices, size) + shape[1:]), coefficients, transforms)
    main = main.reshape(shape)
    if apart:
        main, arrived = lax.optimization_barrier((main, arrived))
    main = exchange(main)
    if apart:
        forced = nonlinear_apart(place, arrived, coefficients, transforms)
        returned = regroup(swap(forced, "freq"))
        returned = swap(returned, "span")

    sends = walls - 1
    side, sums, *sent = absorb(
        None, [main], keep, rows[0], adjoint_modes[0], sums, width, 0 if apart else sends
    )
    solved = solve(side, upstream, keep, split)
    if apart:
        solved, sums = lax.optimization_barrier((solved, sums))
        side, sums, *sent = absorb(
            place, returned, keep, rows[1], adjoint_modes[1], sums, width, sends
        )
    others = hand_back(sent, "wall")
    if apart:
        solved = solve_more(side, solved, last)
    new_amplitudes, wavenumber_shift = finish(solved, sums, squares, others, edge_columns, width)
    return (new_amplitudes, wavenumber_shift)


def solution(mesh):
    placed = (
        P(None, None, "wall", ("freq", "span")),
        P(None, None, "wall", ("freq", "span")),
        P(("freq", "span")),
        P(),
        P("wall", None, None),
        P("wall", None, None),
        P("wall", None, None),
        P("wall", None, None),
        P("wall", None, None),
        P("wall", None, None),
    )
    return jax.shard_map(
        local,
        mesh=mesh,
        in_specs=placed,
        out_specs=(P(None, None, "wall", ("freq", "span")), P(None, ("freq", "span"))),
        check_vma=False,
    )
```

```python
import functools
import math

import jax
import jax.numpy as jnp
import ml_dtypes
import numpy as np
from jax import lax
from jax.experimental import pallas as pl
from jax.experimental.pallas import tpu as pltpu
from jax.sharding import PartitionSpec as P

NF = 128
NB = 256

epsilon = 1e-06

SPLIT = lax.Precision.HIGH
FULL = lax.Precision.HIGHEST


def tables():
    def turns(length):
        counter = np.arange(length)
        angles = (counter[:, None] * counter[None, :] % length) * (2.0 * math.pi / length)
        return np.cos(angles), np.sin(angles)

    cos_time, sin_time = turns(NF)
    cos_span, sin_span = turns(NB)
    scale = 1.0 / math.sqrt(NF * NB)
    out = (
        (np.block([[cos_time, -sin_time], [sin_time, cos_time]]), 1),
        (np.concatenate([cos_span, -sin_span], 0) * scale, 0),
        (np.concatenate([cos_span, -sin_span], 1) * scale, 0),
        (np.block([[cos_time, sin_time], [-sin_time, cos_time]]), 1),
    )

    def split(table, axis):
        high = table.astype(ml_dtypes.bfloat16)
        low = (table - high.astype(np.float64)).astype(ml_dtypes.bfloat16)
        return jnp.asarray(np.concatenate([high, high, low], axis))

    return [split(table, axis) for table, axis in out]


def params(megabytes=16):
    return pltpu.CompilerParams(vmem_limit_bytes=megabytes * 1024 * 1024)


def whole(array):
    zeros = (0,) * len(array.shape)
    return pl.BlockSpec(array.shape, lambda *_: zeros)


def in_hbm(array):
    return pltpu.with_memory_space_constraint(array, pltpu.HBM)


def kept_modes(mask_ref):
    return mask_ref[...].astype(jnp.float32).reshape(1, -1)


def row_step(rows):
    return rows // 2 if rows % 16 == 0 and rows > 16 else rows


def prepare_body(x_ref, mask_ref, out_ref):
    keep = kept_modes(mask_ref)
    rows, variables, freqs, _ = out_ref.shape
    for v in range(variables):
        for part in range(2):
            kept = x_ref[part, v] * keep
            out_ref[:, v, :, part * NB : (part + 1) * NB] = kept.reshape(rows, freqs, NB)


def prepare(amplitudes, keep, cut):
    _, variables, _, modes = amplitudes.shape
    freqs = modes // NB
    rows = cut.stop - cut.start
    step = row_step(rows)
    at = cut.start // step
    return pl.pallas_call(
        prepare_body,
        grid=(rows // step,),
        in_specs=[
            pl.BlockSpec((2, variables, step, modes), lambda r: (0, 0, at + r, 0)),
            pl.BlockSpec((modes,), lambda r: (0,)),
        ],
        out_specs=pl.BlockSpec((step, variables, freqs, 2 * NB), lambda r: (r, 0, 0, 0)),
        out_shape=pltpu.HBM((rows, variables, freqs, 2 * NB), jnp.float32),
        compiler_params=params(24),
        name="prepare",
    )(in_hbm(amplitudes), in_hbm(keep))


def partner(place_ref, j, i, spans):
    return (place_ref[0] ^ j) * spans + (place_ref[1] ^ i)


def prepare_apart_body(place_ref, x_ref, mask_ref, *refs):
    out_refs, rows_ref = refs[:-1], refs[-1]
    keep = kept_modes(mask_ref)
    rows, freqs, _ = rows_ref.shape
    spans = out_refs[0].shape[0]
    for part in range(2):
        kept = x_ref[part, 0] * keep
        rows_ref[:, :, part * NB : (part + 1) * NB] = kept.reshape(rows, freqs, NB)
    for j, out_ref in enumerate(out_refs):
        for i in range(spans):
            out_ref[i, 0] = rows_ref[partner(place_ref, j, i, spans)]


def prepare_apart(place, amplitudes, keep, cut, groups, spans):
    _, variables, _, modes = amplitudes.shape
    freqs = modes // NB
    rows = cut.stop - cut.start
    at = cut.start // rows
    return pl.pallas_call(
        prepare_apart_body,
        grid=(variables,),
        in_specs=[
            pl.BlockSpec(memory_space=pltpu.SMEM),
            pl.BlockSpec((2, 1, rows, modes), lambda v: (0, v, at, 0)),
            pl.BlockSpec((modes,), lambda v: (0,)),
        ],
        out_specs=[pl.BlockSpec((spans, 1, freqs, 2 * NB), lambda v: (0, v, 0, 0))] * groups,
        out_shape=[jax.ShapeDtypeStruct((spans, variables, freqs, 2 * NB), jnp.float32)] * groups,
        scratch_shapes=[pltpu.VMEM((rows, freqs, 2 * NB), jnp.float32)],
        compiler_params=params(),
        name="prepare_apart",
    )(place, in_hbm(amplitudes), keep)


def halves(value):
    high = value.astype(jnp.bfloat16)
    return high, (value - high.astype(jnp.float32)).astype(jnp.bfloat16)


def table_times(table, value):
    high, low = halves(value)
    value = jnp.concatenate([high, low, high], axis=0)
    return jnp.dot(table, value, preferred_element_type=jnp.float32)


def times_table(value, table):
    high, low = halves(value)
    value = jnp.concatenate([high, low, high], axis=1)
    return jnp.dot(value, table, preferred_element_type=jnp.float32)


def transform(read, write, q_ref, table_refs, field_ref, force_ref):
    wi_ref, ei_ref, ef_ref, wf_ref = table_refs
    variables = field_ref.shape[0]
    for v in range(variables):
        modes = read(v)
        stacked = jnp.concatenate([modes[:, :NB], modes[:, NB:]], axis=0)
        turned = table_times(wi_ref[...], stacked)
        beside = jnp.concatenate([turned[:NF], turned[NF:]], axis=1)
        field_ref[v] = times_table(beside, ei_ref[...])
    pairs = [(a, b) for a in range(variables) for b in range(a + 1, variables)]
    weights = [
        [q_ref[w * variables + a, b] + q_ref[w * variables + b, a] for a, b in pairs]
        for w in range(variables)
    ]
    step = 8
    for row in range(0, NF, step):
        at = slice(row, row + step)
        values = [field_ref[v, at] for v in range(variables)]
        total = [None] * variables
        for i, (a, b) in enumerate(pairs):
            product = values[a] * values[b]
            for w in range(variables):
                term = weights[w][i] * product
                total[w] = term if total[w] is None else total[w] + term
        for w in range(variables):
            force_ref[w, at] = total[w]
    for w in range(variables):
        spread = times_table(force_ref[w], ef_ref[...])
        stacked = jnp.concatenate([spread[:, :NB], spread[:, NB:]], axis=0)
        turned = table_times(wf_ref[...], stacked)
        for part in range(2):
            write(w, part, turned[part * NF : (part + 1) * NF])


def nonlinear_body(q_ref, in_ref, *refs):
    table_refs, out_ref, work_refs = refs[:4], refs[4], refs[5:]
    devices, _, _, freqs, _ = in_ref.shape

    def read(v):
        return in_ref[:, 0, v].reshape(NF, 2 * NB)

    def write(w, part, piece):
        at = slice(part * NB, (part + 1) * NB)
        out_ref[:, 0, w, :, at] = piece.reshape(devices, freqs, NB)

    transform(read, write, q_ref, table_refs, *work_refs)


def work_shapes(variables):
    return [pltpu.VMEM((variables, NF, NB), jnp.float32)] * 2


def nonlinear_cost(points, variables):
    return pl.CostEstimate(
        flops=points * variables * 12 * NF * NB * (NF + NB) * 2,
        bytes_accessed=points * variables * NF * NB * 16,
        transcendentals=0,
    )


def nonlinear(block, coefficients, transforms):
    devices, points, variables, freqs, lanes = block.shape
    spec = pl.BlockSpec((devices, 1, variables, freqs, lanes), lambda j: (0, j, 0, 0, 0))
    return pl.pallas_call(
        nonlinear_body,
        grid=(points,),
        in_specs=[pl.BlockSpec(memory_space=pltpu.SMEM), spec] + [whole(t) for t in transforms],
        out_specs=spec,
        out_shape=pltpu.HBM(block.shape, jnp.float32),
        scratch_shapes=work_shapes(variables),
        compiler_params=params(24),
        cost_estimate=nonlinear_cost(points, variables),
        name="nonlinear",
    )(coefficients, block, *[in_hbm(table) for table in transforms])


def nonlinear_apart_body(groups, spans, place_ref, q_ref, *refs):
    in_refs, refs = refs[:spans], refs[spans:]
    table_refs, refs = refs[:4], refs[4:]
    out_refs, refs = refs[:groups], refs[groups:]
    rows_ref, work_refs = refs[0], refs[1:]
    devices, _, freqs, _ = rows_ref.shape
    for j in range(groups):
        for i in range(spans):
            rows_ref[partner(place_ref, j, i, spans)] = in_refs[i][j]

    def read(v):
        return rows_ref[:, v].reshape(NF, 2 * NB)

    def write(w, part, piece):
        at = slice(part * NB, (part + 1) * NB)
        rows_ref[:, w, :, at] = piece.reshape(devices, freqs, NB)

    transform(read, write, q_ref, table_refs, *work_refs)
    for j in range(groups):
        for i in range(spans):
            out_refs[j][i] = rows_ref[partner(place_ref, j, i, spans)]


def nonlinear_apart(place, blocks, coefficients, transforms):
    spans = len(blocks)
    groups, variables, freqs, lanes = blocks[0].shape
    result = jax.ShapeDtypeStruct((spans, variables, freqs, lanes), jnp.float32)
    smem = pl.BlockSpec(memory_space=pltpu.SMEM)
    return pl.pallas_call(
        functools.partial(nonlinear_apart_body, groups, spans),
        grid=(1,),
        in_specs=[smem, smem]
        + [whole(block) for block in blocks]
        + [whole(table) for table in transforms],
        out_specs=[whole(result)] * groups,
        out_shape=[result] * groups,
        scratch_shapes=[pltpu.VMEM((groups * spans, variables, freqs, lanes), jnp.float32)]
        + work_shapes(variables),
        compiler_params=params(24),
        cost_estimate=pl.CostEstimate(flops=2 * 10**11, bytes_accessed=0, transcendentals=0),
        name="nonlinear_apart",
    )(place, coefficients, *blocks, *[in_hbm(table) for table in transforms])


def total(value):
    return jnp.sum(value, axis=0, keepdims=True)


def padded(rows, multiple):
    return rows + -rows % multiple


def edge_body(width, x_ref, mask_ref, rows_ref, out_ref):
    _, variables, heights, lanes = x_ref.shape
    keep = kept_modes(mask_ref)
    squares = 0.0
    out_ref[...] = jnp.zeros(out_ref.shape, jnp.float32)
    for part in range(2):
        kept = x_ref[part].reshape(variables * heights, lanes) * keep
        squares = squares + total(kept * kept)
        out_ref[part * width : (part + 1) * width] = table_times(rows_ref[...], kept)[:width]
    out_ref[2 * width : 2 * width + 1] = squares


def edge(amplitudes, keep, rows, width):
    _, variables, heights, modes = amplitudes.shape
    length = padded(2 * width + 1, 8)
    return pl.pallas_call(
        functools.partial(edge_body, width),
        grid=(modes // NB,),
        in_specs=[
            pl.BlockSpec((2, variables, heights, NB), lambda i: (0, 0, 0, i)),
            pl.BlockSpec((NB,), lambda i: (i,)),
            whole(rows),
        ],
        out_specs=pl.BlockSpec((length, NB), lambda i: (0, i)),
        out_shape=jax.ShapeDtypeStruct((length, modes), jnp.float32),
        compiler_params=params(),
        name="edge",
    )(in_hbm(amplitudes), keep, rows)


def base_body(cuts, walls, width, x_ref, up_ref, mask_ref, turned_ref, ahead_ref, back_ref, *refs):
    edges, refs = refs[:walls], refs[walls:]
    out_refs, (sum_ref, square_ref) = refs[: len(cuts)], refs[len(cuts) :]
    _, variables, heights, lanes = x_ref.shape
    extent = variables * heights
    pushes = walls * width
    spare = back_ref.shape[1] // 3 - pushes
    keep = kept_modes(mask_ref)
    moved, sides = [], []
    sum_ref[...] = jnp.zeros(sum_ref.shape, jnp.float32)
    for part in range(2):
        kept = x_ref[part].reshape(extent, lanes) * keep
        taken = [ref[part * width : (part + 1) * width] for ref in edges]
        if spare:
            taken.append(jnp.zeros((spare, lanes), jnp.float32))
        taken = jnp.concatenate(taken, axis=0)
        moved.append(table_times(turned_ref[...], kept) - table_times(back_ref[...], taken))
        grid = moved[part].reshape(variables, heights, lanes)
        for cut, out_ref in zip(cuts, out_refs):
            out_ref[part] = grid[:, cut]
        sides.append(up_ref[part].reshape(extent, lanes) * keep)
        added = table_times(ahead_ref[...], sides[part])
        sum_ref[part * pushes : (part + 1) * pushes] = added[:pushes]
    row = 2 * pushes
    sum_ref[row : row + 1] = total(moved[0] * sides[0] + moved[1] * sides[1])
    sum_ref[row + 1 : row + 2] = total(moved[0] * sides[1] - moved[1] * sides[0])
    squares = sum(ref[2 * width : 2 * width + 1] for ref in edges)
    square_ref[...] = jnp.broadcast_to(squares, square_ref.shape)


def base(amplitudes, upstream, keep, turned, ahead, back, edges, width, cuts):
    _, variables, heights, modes = amplitudes.shape
    walls = len(edges)
    lengths = [cut.stop - cut.start for cut in cuts]
    shapes = [(2, variables, rows, modes) for rows in lengths]
    sums = padded(2 * walls * width + 2, 8)
    spec = pl.BlockSpec((2, variables, heights, NB), lambda i: (0, 0, 0, i))

    def rows_spec(rows):
        return pl.BlockSpec((rows, NB), lambda i: (0, i))

    return pl.pallas_call(
        functools.partial(base_body, cuts, walls, width),
        grid=(modes // NB,),
        in_specs=[spec] * 2
        + [pl.BlockSpec((NB,), lambda i: (i,)), whole(turned), whole(ahead), whole(back)]
        + [rows_spec(part.shape[0]) for part in edges],
        out_specs=[
            pl.BlockSpec((2, variables, rows, NB), lambda i: (0, 0, 0, i)) for rows in lengths
        ]
        + [rows_spec(sums), rows_spec(8)],
        out_shape=[pltpu.HBM(shapes[0], jnp.float32)]
        + [jax.ShapeDtypeStruct(shape, jnp.float32) for shape in shapes[1:]]
        + [jax.ShapeDtypeStruct((rows, modes), jnp.float32) for rows in (sums, 8)],
        compiler_params=params(24),
        name="base",
    )(in_hbm(amplitudes), in_hbm(upstream), keep, turned, ahead, back, *edges)


def absorb_rows(width, read, mask_ref, ahead_ref, adj_ref, before_ref, out_ref, sum_ref, *send_refs):
    _, variables, rows, lanes = out_ref.shape
    pushes = ahead_ref.shape[1]
    keep = kept_modes(mask_ref)

    @pl.when(pl.program_id(0) == 0)
    def _():
        sum_ref[...] = before_ref[...]

    for v in range(variables):
        for part in range(2):
            out_ref[part, v] = read(v, part).reshape(rows, lanes) * keep
    sides = [out_ref[part].reshape(variables * rows, lanes) for part in range(2)]
    for part in range(2):
        sum_ref[part * pushes : (part + 1) * pushes] += jnp.dot(
            ahead_ref[0], sides[part], precision=SPLIT, preferred_element_type=jnp.float32
        )
    real, imag = (adj_ref[part].reshape(variables * rows, lanes) for part in range(2))
    at = 2 * pushes
    sum_ref[at : at + 1] += total(real * sides[0] + imag * sides[1])
    sum_ref[at + 1 : at + 2] += total(real * sides[1] - imag * sides[0])

    if send_refs:

        @pl.when(pl.program_id(0) == pl.num_programs(0) - 1)
        def _():
            for d, send_ref in enumerate(send_refs, 1):
                pieces = []
                for part in range(2):
                    at = part * pushes + d * width
                    pieces.append(sum_ref[at : at + width])
                pieces.append(sum_ref[2 * pushes : 2 * pushes + 2])
                pack_rows(send_ref, jnp.concatenate(pieces, axis=0))


def folded(rows, modes):
    return rows == 12 and modes % 256 == 0 and modes <= 8 * NB


def travelling(rows, modes):
    if folded(rows, modes):
        return jax.ShapeDtypeStruct((rows - 4, modes + modes // 2), jnp.float32)
    return jax.ShapeDtypeStruct((padded(rows, 8), modes), jnp.float32)


def pack_rows(out_ref, value):
    rows, modes = value.shape
    if folded(rows, modes):
        half = modes // 2
        out_ref[:, :modes] = value[: rows - 4]
        out_ref[:4, modes:] = value[rows - 4 :, :half]
        out_ref[4:8, modes:] = value[rows - 4 :, half:]
        return
    out_ref[:rows] = value
    if out_ref.shape[0] > rows:
        out_ref[rows:] = jnp.zeros((out_ref.shape[0] - rows, modes), jnp.float32)


def absorb_body(width, in_ref, *refs):
    def read(v, part):
        return in_ref[:, v, :, part * NB : (part + 1) * NB]

    absorb_rows(width, read, *refs)


def absorb_apart_body(width, spans, place_ref, *refs):
    in_refs, refs, rows_ref = refs[:spans], refs[spans:-1], refs[-1]
    for i, in_ref in enumerate(in_refs):
        for j in range(in_ref.shape[0]):
            rows_ref[partner(place_ref, j, i, spans)] = in_ref[j]

    def read(v, part):
        return rows_ref[:, v, :, part * NB : (part + 1) * NB]

    absorb_rows(width, read, *refs)


def absorb(place, blocks, keep, ahead, adjoint_modes, before, width, sends):
    blocks = list(blocks)
    apart = place is not None
    _, variables, rows, modes = adjoint_modes.shape
    steps, pushes, depth = ahead.shape
    step = rows // steps
    grid_spec = pl.BlockSpec((2, variables, step, modes), lambda r: (0, 0, r, 0))
    _, _, freqs, lanes = blocks[0].shape
    sent = travelling(2 * width + 2, modes)
    operands = blocks + [keep, ahead, adjoint_modes if apart else in_hbm(adjoint_modes), before]
    in_specs = [
        whole(block)
        if apart
        else pl.BlockSpec((step, variables, freqs, lanes), lambda r: (r, 0, 0, 0))
        for block in blocks
    ] + [
        pl.BlockSpec((modes,), lambda r: (0,)),
        pl.BlockSpec((1, pushes, depth), lambda r: (r, 0, 0)),
        grid_spec,
        whole(before),
    ]
    body, scratch = functools.partial(absorb_body, width), []
    if apart:
        operands = [place] + operands
        in_specs = [pl.BlockSpec(memory_space=pltpu.SMEM)] + in_specs
        body = functools.partial(absorb_apart_body, width, len(blocks))
        scratch = [pltpu.VMEM((rows, variables, freqs, lanes), jnp.float32)]
    return pl.pallas_call(
        body,
        grid=(steps,),
        in_specs=in_specs,
        out_specs=[grid_spec, whole(before)] + [whole(sent)] * sends,
        out_shape=[
            jax.ShapeDtypeStruct((2, variables, rows, modes), jnp.float32),
            jax.ShapeDtypeStruct(before.shape, jnp.float32),
        ]
        + [sent] * sends,
        scratch_shapes=scratch,
        compiler_params=params(24),
        name="absorb_apart" if apart else "absorb",
    )(*operands)


def solve_body(side_ref, up_ref, mask_ref, inverse_ref, out_ref):
    _, variables, heights, lanes = out_ref.shape
    keep = kept_modes(mask_ref)
    spare = heights - side_ref.shape[2]
    for part in range(2):
        forced = side_ref[part]
        if spare:
            none = jnp.zeros((variables, spare, lanes), jnp.float32)
            forced = jnp.concatenate([forced, none], axis=1)
        side = (forced + up_ref[part] * keep).reshape(variables * heights, lanes)
        out_ref[part] = table_times(inverse_ref[...], side).reshape(variables, heights, lanes)


def solve(side, upstream, keep, inverse):
    _, variables, heights, modes = upstream.shape
    lanes = min(4 * NB, modes)
    spec = pl.BlockSpec((2, variables, heights, lanes), lambda i: (0, 0, 0, i))
    return pl.pallas_call(
        solve_body,
        grid=(modes // lanes,),
        in_specs=[
            pl.BlockSpec((2, variables, side.shape[2], lanes), lambda i: (0, 0, 0, i)),
            spec,
            pl.BlockSpec((lanes,), lambda i: (i,)),
            whole(inverse),
        ],
        out_specs=spec,
        out_shape=jax.ShapeDtypeStruct(upstream.shape, jnp.float32),
        compiler_params=params(32),
        name="solve",
    )(side, in_hbm(upstream), keep, inverse)


def solve_more_body(side_ref, before_ref, inverse_ref, out_ref):
    _, variables, heights, lanes = out_ref.shape
    for part in range(2):
        moved = table_times(inverse_ref[...], side_ref[part].reshape(-1, lanes))
        out_ref[part] = before_ref[part] + moved.reshape(variables, heights, lanes)


def solve_more(side, before, inverse):
    _, variables, rows, modes = side.shape
    lanes = min(4 * NB, modes)
    spec = pl.BlockSpec(before.shape[:3] + (lanes,), lambda i: (0, 0, 0, i))
    return pl.pallas_call(
        solve_more_body,
        grid=(modes // lanes,),
        in_specs=[
            pl.BlockSpec((2, variables, rows, lanes), lambda i: (0, 0, 0, i)),
            spec,
            whole(inverse),
        ],
        out_specs=spec,
        out_shape=jax.ShapeDtypeStruct(before.shape, jnp.float32),
        compiler_params=params(32),
        name="solve_more",
    )(side, before, inverse)


def finish_body(walls, width, fold, solved_ref, sum_ref, square_ref, *refs):
    each = 2 if fold else 1
    other_refs, (columns_ref, out_ref, shift_ref) = refs[: each * (walls - 1)], refs[-3:]
    _, variables, heights, lanes = out_ref.shape
    spare = columns_ref.shape[1] // 3 - width
    pushes = walls * width
    others = [ref[...] for ref in other_refs]
    if fold:
        first = pl.program_id(0) == 0
        others = [
            jnp.concatenate([rows, jnp.where(first, rest[:4], rest[4:8])], axis=0)
            for rows, rest in zip(others[::2], others[1::2])
        ]
    for part in range(2):
        push = sum_ref[part * pushes : part * pushes + width]
        for other in others:
            push = push + other[part * width : (part + 1) * width]
        if spare:
            push = jnp.concatenate([push, jnp.zeros((spare, lanes), jnp.float32)], axis=0)
        moved = table_times(columns_ref[...], push)
        out_ref[part] = solved_ref[part] - moved.reshape(variables, heights, lanes)
    both = sum_ref[2 * pushes : 2 * pushes + 2]
    for other in others:
        both = both + other[2 * width : 2 * width + 2]
    squares = square_ref[:1]
    weight = squares + epsilon
    shift_ref[0:1] = both[1:2] / weight
    shift_ref[1:2] = (squares - both[0:1]) / weight


def finish(solved, sums, squares, others, columns, width):
    _, variables, heights, modes = solved.shape
    fold = folded(2 * width + 2, modes)
    lanes = modes // 2 if fold else min(4 * NB, modes)

    def rows_spec(rows):
        return pl.BlockSpec((rows, lanes), lambda i: (0, i))

    spec = pl.BlockSpec((2, variables, heights, lanes), lambda i: (0, 0, 0, i))
    operands, in_specs = [solved, sums, squares], [spec]
    in_specs += [rows_spec(part.shape[0]) for part in (sums, squares)]
    for part in others:
        operands.append(part)
        in_specs.append(rows_spec(part.shape[0]))
        if fold:
            operands.append(part)
            in_specs.append(pl.BlockSpec((8, lanes), lambda i: (0, 2)))
    return pl.pallas_call(
        functools.partial(finish_body, len(others) + 1, width, fold),
        grid=(modes // lanes,),
        in_specs=in_specs + [whole(columns)],
        out_specs=[spec, pl.BlockSpec((2, lanes), lambda i: (0, i))],
        out_shape=[
            jax.ShapeDtypeStruct(solved.shape, jnp.float32),
            jax.ShapeDtypeStruct((2, modes), jnp.float32),
        ],
        compiler_params=params(32),
        name="finish",
    )(*operands, columns)


def around(block, axis):
    count = lax.axis_size(axis)
    return [block] + [
        lax.ppermute(block, axis, [(i, (i + d) % count) for i in range(count)])
        for d in range(1, count)
    ]


def hand_back(blocks, axis):
    count = lax.axis_size(axis)
    return [
        lax.ppermute(block, axis, [(i, (i - d) % count) for i in range(count)])
        for d, block in enumerate(blocks, 1)
    ]


PACKED_ROWS = 16


def pack_body(*refs):
    in_refs, out_ref = refs[:-1], refs[-1]
    out_ref[...] = jnp.zeros(out_ref.shape, jnp.float32)
    for i, ref in enumerate(in_refs):
        rows, columns = ref.shape[1:]
        out_ref[i, :rows, :columns] = ref[0]


def pack(parts):
    return pl.pallas_call(
        pack_body,
        out_shape=jax.ShapeDtypeStruct((len(parts), PACKED_ROWS, 128), jnp.float32),
        name="pack",
    )(*parts)


def upper_bits(value):
    return value.astype(jnp.bfloat16).astype(jnp.float32)


def split_columns(matrix):
    high = upper_bits(matrix)
    return jnp.concatenate([high, high, matrix - high], axis=1).astype(jnp.bfloat16)


def push_width(walls, variables):
    return variables if walls == 2 else 2 * variables


def constants_body(cuts, variables, walls, place_ref, inverse_ref, *refs):
    packed, refs = refs[:walls], refs[walls:]
    turned_ref, split_ref, last_ref, column_ref, edge_ref, ahead_ref, back_ref = refs[:7]
    row_refs, (all_ref, step_ref) = refs[7 : 7 + len(cuts)], refs[7 + len(cuts) :]
    extent = inverse_ref.shape[0]
    heights = extent // variables
    ends = 2 * variables
    width = push_width(walls, variables)
    matrix = inverse_ref[...]
    turned = matrix.T
    turned_ref[...] = split_columns(turned)
    split_ref[...] = split_columns(matrix)
    cut = cuts[-1]
    last = [matrix[:, v * heights : (v + 1) * heights][:, cut] for v in range(variables)]
    last_ref[...] = split_columns(jnp.concatenate(last, axis=1))

    def dot(a, b):
        return jnp.dot(a, b, precision=FULL, preferred_element_type=jnp.float32)

    def ends_of(value):
        low = [value[v * heights : v * heights + 1] for v in range(variables)]
        high = [value[(v + 1) * heights - 1 : (v + 1) * heights] for v in range(variables)]
        return jnp.concatenate(low, axis=0), jnp.concatenate(high, axis=0)

    def extended(value, rows):
        spare = rows - value.shape[0]
        if not spare:
            return value
        return jnp.concatenate([value, jnp.zeros((spare, value.shape[1]), jnp.float32)], axis=0)

    size = walls * PACKED_ROWS
    for d in range(walls):
        all_ref[(place_ref[0] - d + walls) % walls] = packed[d][...]

    def small(j, kind):
        return all_ref[j, kind][:, :PACKED_ROWS]

    row = lax.broadcasted_iota(jnp.int32, (PACKED_ROWS, size), 0)
    column = lax.broadcasted_iota(jnp.int32, (PACKED_ROWS, size), 1)
    units = []
    for j in range(walls):
        d = (place_ref[0] - j + walls) % walls
        hit = (column == d * ends + row) & (row < ends)
        units.append(jnp.where(hit, 1.0, 0.0))
    ahead = [units[0]]
    for j in range(1, walls):
        ahead.append(units[j] - dot(small(j, 2), ahead[j - 1]))
    interface = [None] * walls
    interface[-1] = dot(small(walls - 1, 4), ahead[-1])
    for j in range(walls - 2, -1, -1):
        interface[j] = dot(small(j, 4), ahead[j] - dot(small(j, 3), interface[j + 1]))
    none = jnp.zeros((variables, size), jnp.float32)
    for j in range(walls):
        under, over = none, none
        if j > 0:
            lower = extended(interface[j - 1][variables:], PACKED_ROWS)
            under = dot(small(j, 0), lower)[:variables]
        if j < walls - 1:
            over = dot(small(j, 1), interface[j + 1])[:variables]
        push = under + over if walls == 2 else jnp.concatenate([under, over], axis=0)
        step_ref[(place_ref[0] - j + walls) % walls] = extended(push, PACKED_ROWS)

    low, high = ends_of(matrix)
    bounds = extended(jnp.concatenate([low, high], axis=0), PACKED_ROWS)
    steps = [step_ref[d][:width, :PACKED_ROWS] for d in range(walls)]
    steps = [jnp.where(column[:width, :PACKED_ROWS] < ends, step, 0.0) for step in steps]
    pushes = dot(jnp.concatenate(steps, axis=0), bounds)
    for cut, row_ref in zip(cuts, row_refs):
        step = row_step(cut.stop - cut.start)
        for r in range(row_ref.shape[0]):
            at = cut.start + r * step
            pieces = [pushes[:, v * heights + at : v * heights + at + step] for v in range(variables)]
            row_ref[r] = jnp.concatenate(pieces, axis=1)
    pushes = extended(pushes, ahead_ref.shape[0])
    ahead_ref[...] = split_columns(pushes)
    back_ref[...] = split_columns(pushes.T)
    low, high = ends_of(turned)
    edge = jnp.concatenate([low, high], axis=0)
    if walls == 2:
        edge = jnp.where(place_ref[0] == 0, high, low)
    edge = extended(edge, edge_ref.shape[0])
    edge_ref[...] = split_columns(edge)
    column_ref[...] = split_columns(edge.T)


def constants(place, inverse, packed, cuts, variables):
    walls = len(packed)
    extent = inverse.shape[0]
    width = push_width(walls, variables)
    lengths = [cut.stop - cut.start for cut in cuts]
    size = walls * PACKED_ROWS
    pushes, edge_rows = padded(walls * width, 16), padded(width, 16)

    def split_shape(rows, columns):
        return jax.ShapeDtypeStruct((rows, 3 * columns), jnp.bfloat16)

    return pl.pallas_call(
        functools.partial(constants_body, cuts, variables, walls),
        in_specs=[pl.BlockSpec(memory_space=pltpu.SMEM)]
        + [pl.BlockSpec(memory_space=pltpu.VMEM)] * (1 + walls),
        out_shape=[
            split_shape(extent, extent),
            split_shape(extent, extent),
            split_shape(extent, variables * lengths[-1]),
            split_shape(extent, edge_rows),
            split_shape(edge_rows, extent),
            split_shape(pushes, extent),
            split_shape(extent, pushes),
        ]
        + [
            jax.ShapeDtypeStruct(
                (n // row_step(n), walls * width, variables * row_step(n)), jnp.float32
            )
            for n in lengths
        ],
        scratch_shapes=[
            pltpu.VMEM((walls,) + packed[0].shape, jnp.float32),
            pltpu.VMEM((walls, PACKED_ROWS, size), jnp.float32),
        ],
        compiler_params=params(),
        name="constants",
    )(place, inverse, *packed)


def local(
    amplitudes,
    upstream,
    harmonic_mask,
    quadratic_coefficients,
    slab_inverse,
    lower_coupling,
    upper_coupling,
    reduced_lower,
    reduced_upper,
    reduced_pivot,
):
    _, variables, heights, modes = amplitudes.shape
    axes = ("freq", "span")
    groups, spans = lax.axis_size("freq"), lax.axis_size("span")
    devices = groups * spans
    points = heights // devices
    apart = points > 1 and groups & (groups - 1) == 0 and spans & (spans - 1) == 0
    edge_at = heights - devices if apart else heights
    cuts = [slice(0, edge_at)] + ([slice(edge_at, heights)] if apart else [])
    keep = harmonic_mask
    place = jnp.stack([lax.axis_index("freq"), lax.axis_index("span")]).astype(jnp.int32)
    wall = lax.axis_index("wall").reshape(1).astype(jnp.int32)
    transforms = tables()
    coefficients = quadratic_coefficients.reshape(variables * variables, variables)

    def exchange(block):
        return lax.all_to_all(block, axes, split_axis=0, concat_axis=0, tiled=True)

    def swap(blocks, axis):
        count = len(blocks)
        return [blocks[0]] + [
            lax.ppermute(blocks[i], axis, [(at, at ^ i) for at in range(count)])
            for i in range(1, count)
        ]

    def regroup(blocks):
        return [jnp.stack([block[j] for block in blocks]) for j in range(blocks[0].shape[0])]

    main = prepare(amplitudes, keep, cuts[0])
    if apart:
        main, amplitudes = lax.optimization_barrier((main, amplitudes))
        sent = prepare_apart(place, amplitudes, keep, cuts[1], groups, spans)
        arrived = regroup(swap(sent, "freq"))
        moved = swap(arrived, "span")
        moved[1], held = lax.optimization_barrier((moved[1], amplitudes))
    main = exchange(main)

    inverse = slab_inverse[0]
    parts = (lower_coupling, upper_coupling, reduced_lower, reduced_upper, reduced_pivot)
    packed = around(pack(parts), "wall")
    turned, split, last, edge_columns, edge_rows, ahead, back, *rows = constants(
        wall, inverse, packed, cuts, variables
    )
    walls = len(packed)
    width = push_width(walls, variables)
    edges = edge(held if apart else amplitudes, keep, edge_rows, width)
    edges = around(edges, "wall")
    *adjoint_modes, sums, squares = base(
        amplitudes, upstream, keep, turned, ahead, back, edges, width, cuts
    )
    size = edge_at // devices
    shape = main.shape
    main = nonlinear(main.reshape((devices, size) + shape[1:]), coefficients, transforms)
    main = main.reshape(shape)
    main = exchange(main)
    if apart:
        half = spans // 2
        sums, arrived[half] = lax.optimization_barrier((sums, arrived[half]))
        moved[half] = swap(arrived, "span")[half]
        arrived = moved
        forced = nonlinear_apart(place, arrived, coefficients, transforms)
        returned = regroup(swap(forced, "freq"))
        returned = swap(returned, "span")

    sends = walls - 1
    side, sums, *sent = absorb(
        None, [main], keep, rows[0], adjoint_modes[0], sums, width, 0 if apart else sends
    )
    solved = solve(side, upstream, keep, split)
    if apart:
        solved, sums = lax.optimization_barrier((solved, sums))
        side, sums, *sent = absorb(
            place, returned, keep, rows[1], adjoint_modes[1], sums, width, sends
        )
    others = hand_back(sent, "wall")
    if apart:
        solved = solve_more(side, solved, last)
    new_amplitudes, wavenumber_shift = finish(solved, sums, squares, others, edge_columns, width)
    return (new_amplitudes, wavenumber_shift)


def solution(mesh):
    placed = (
        P(None, None, "wall", ("freq", "span")),
        P(None, None, "wall", ("freq", "span")),
        P(("freq", "span")),
        P(),
        P("wall", None, None),
        P("wall", None, None),
        P("wall", None, None),
        P("wall", None, None),
        P("wall", None, None),
        P("wall", None, None),
    )
    return jax.shard_map(
        local,
        mesh=mesh,
        in_specs=placed,
        out_specs=(P(None, None, "wall", ("freq", "span")), P(None, ("freq", "span"))),
        check_vma=False,
    )
```

```python
import functools
import math

import jax
import jax.numpy as jnp
import ml_dtypes
import numpy as np
from jax import lax
from jax.experimental import pallas as pl
from jax.experimental.pallas import tpu as pltpu
from jax.sharding import PartitionSpec as P

NF = 128
NB = 256

epsilon = 1e-06

SPLIT = lax.Precision.HIGH
FULL = lax.Precision.HIGHEST


def tables():
    def turns(length):
        counter = np.arange(length)
        angles = (counter[:, None] * counter[None, :] % length) * (2.0 * math.pi / length)
        return np.cos(angles), np.sin(angles)

    cos_time, sin_time = turns(NF)
    cos_span, sin_span = turns(NB)
    scale = 1.0 / math.sqrt(NF * NB)
    out = (
        (np.block([[cos_time, -sin_time], [sin_time, cos_time]]), 1),
        (np.concatenate([cos_span, -sin_span], 0) * scale, 0),
        (np.concatenate([cos_span, -sin_span], 1) * scale, 0),
        (np.block([[cos_time, sin_time], [-sin_time, cos_time]]), 1),
    )

    def split(table, axis):
        high = table.astype(ml_dtypes.bfloat16)
        low = (table - high.astype(np.float64)).astype(ml_dtypes.bfloat16)
        return jnp.asarray(np.concatenate([high, high, low], axis))

    return [split(table, axis) for table, axis in out]


def params(megabytes=16):
    return pltpu.CompilerParams(vmem_limit_bytes=megabytes * 1024 * 1024)


def whole(array):
    zeros = (0,) * len(array.shape)
    return pl.BlockSpec(array.shape, lambda *_: zeros)


def in_hbm(array):
    return pltpu.with_memory_space_constraint(array, pltpu.HBM)


def kept_modes(mask_ref):
    return mask_ref[...].astype(jnp.float32).reshape(1, -1)


def row_step(rows):
    return rows // 2 if rows % 16 == 0 and rows > 16 else rows


def prepare_body(x_ref, mask_ref, out_ref):
    keep = kept_modes(mask_ref)
    rows, variables, freqs, _ = out_ref.shape
    for v in range(variables):
        for part in range(2):
            kept = x_ref[part, v] * keep
            out_ref[:, v, :, part * NB : (part + 1) * NB] = kept.reshape(rows, freqs, NB)


def prepare(amplitudes, keep, cut):
    _, variables, _, modes = amplitudes.shape
    freqs = modes // NB
    rows = cut.stop - cut.start
    step = row_step(rows)
    at = cut.start // step
    return pl.pallas_call(
        prepare_body,
        grid=(rows // step,),
        in_specs=[
            pl.BlockSpec((2, variables, step, modes), lambda r: (0, 0, at + r, 0)),
            pl.BlockSpec((modes,), lambda r: (0,)),
        ],
        out_specs=pl.BlockSpec((step, variables, freqs, 2 * NB), lambda r: (r, 0, 0, 0)),
        out_shape=pltpu.HBM((rows, variables, freqs, 2 * NB), jnp.float32),
        compiler_params=params(24),
        name="prepare",
    )(in_hbm(amplitudes), in_hbm(keep))


def partner(place_ref, j, i, spans):
    return (place_ref[0] ^ j) * spans + (place_ref[1] ^ i)


def prepare_apart_body(place_ref, x_ref, mask_ref, *refs):
    out_refs, rows_ref = refs[:-1], refs[-1]
    keep = kept_modes(mask_ref)
    rows, freqs, _ = rows_ref.shape
    spans = out_refs[0].shape[0]
    for part in range(2):
        kept = x_ref[part, 0] * keep
        rows_ref[:, :, part * NB : (part + 1) * NB] = kept.reshape(rows, freqs, NB)
    for j, out_ref in enumerate(out_refs):
        for i in range(spans):
            out_ref[i, 0] = rows_ref[partner(place_ref, j, i, spans)]


def prepare_apart(place, amplitudes, keep, cut, groups, spans):
    _, variables, _, modes = amplitudes.shape
    freqs = modes // NB
    rows = cut.stop - cut.start
    at = cut.start // rows
    return pl.pallas_call(
        prepare_apart_body,
        grid=(variables,),
        in_specs=[
            pl.BlockSpec(memory_space=pltpu.SMEM),
            pl.BlockSpec((2, 1, rows, modes), lambda v: (0, v, at, 0)),
            pl.BlockSpec((modes,), lambda v: (0,)),
        ],
        out_specs=[pl.BlockSpec((spans, 1, freqs, 2 * NB), lambda v: (0, v, 0, 0))] * groups,
        out_shape=[jax.ShapeDtypeStruct((spans, variables, freqs, 2 * NB), jnp.float32)] * groups,
        scratch_shapes=[pltpu.VMEM((rows, freqs, 2 * NB), jnp.float32)],
        compiler_params=params(),
        name="prepare_apart",
    )(place, in_hbm(amplitudes), keep)


def halves(value):
    high = value.astype(jnp.bfloat16)
    return high, (value - high.astype(jnp.float32)).astype(jnp.bfloat16)


def table_times(table, value):
    high, low = halves(value)
    value = jnp.concatenate([high, low, high], axis=0)
    return jnp.dot(table, value, preferred_element_type=jnp.float32)


def times_table(value, table):
    high, low = halves(value)
    value = jnp.concatenate([high, low, high], axis=1)
    return jnp.dot(value, table, preferred_element_type=jnp.float32)


def transform(read, write, q_ref, table_refs, field_ref, force_ref):
    wi_ref, ei_ref, ef_ref, wf_ref = table_refs
    variables = field_ref.shape[0]
    for v in range(variables):
        modes = read(v)
        stacked = jnp.concatenate([modes[:, :NB], modes[:, NB:]], axis=0)
        turned = table_times(wi_ref[...], stacked)
        beside = jnp.concatenate([turned[:NF], turned[NF:]], axis=1)
        field_ref[v] = times_table(beside, ei_ref[...])
    pairs = [(a, b) for a in range(variables) for b in range(a + 1, variables)]
    weights = [
        [q_ref[w * variables + a, b] + q_ref[w * variables + b, a] for a, b in pairs]
        for w in range(variables)
    ]
    step = 8
    for row in range(0, NF, step):
        at = slice(row, row + step)
        values = [field_ref[v, at] for v in range(variables)]
        total = [None] * variables
        for i, (a, b) in enumerate(pairs):
            product = values[a] * values[b]
            for w in range(variables):
                term = weights[w][i] * product
                total[w] = term if total[w] is None else total[w] + term
        for w in range(variables):
            force_ref[w, at] = total[w]
    for w in range(variables):
        spread = times_table(force_ref[w], ef_ref[...])
        stacked = jnp.concatenate([spread[:, :NB], spread[:, NB:]], axis=0)
        turned = table_times(wf_ref[...], stacked)
        for part in range(2):
            write(w, part, turned[part * NF : (part + 1) * NF])


def nonlinear_body(q_ref, in_ref, *refs):
    table_refs, out_ref, work_refs = refs[:4], refs[4], refs[5:]
    devices, _, _, freqs, _ = in_ref.shape

    def read(v):
        return in_ref[:, 0, v].reshape(NF, 2 * NB)

    def write(w, part, piece):
        at = slice(part * NB, (part + 1) * NB)
        out_ref[:, 0, w, :, at] = piece.reshape(devices, freqs, NB)

    transform(read, write, q_ref, table_refs, *work_refs)


def work_shapes(variables):
    return [pltpu.VMEM((variables, NF, NB), jnp.float32)] * 2


def nonlinear_cost(points, variables):
    return pl.CostEstimate(
        flops=points * variables * 12 * NF * NB * (NF + NB) * 2,
        bytes_accessed=points * variables * NF * NB * 16,
        transcendentals=0,
    )


def nonlinear(block, coefficients, transforms):
    devices, points, variables, freqs, lanes = block.shape
    spec = pl.BlockSpec((devices, 1, variables, freqs, lanes), lambda j: (0, j, 0, 0, 0))
    return pl.pallas_call(
        nonlinear_body,
        grid=(points,),
        in_specs=[pl.BlockSpec(memory_space=pltpu.SMEM), spec] + [whole(t) for t in transforms],
        out_specs=spec,
        out_shape=pltpu.HBM(block.shape, jnp.float32),
        scratch_shapes=work_shapes(variables),
        compiler_params=params(24),
        cost_estimate=nonlinear_cost(points, variables),
        name="nonlinear",
    )(coefficients, block, *[in_hbm(table) for table in transforms])


def nonlinear_apart_body(groups, spans, place_ref, q_ref, *refs):
    in_refs, refs = refs[:spans], refs[spans:]
    table_refs, refs = refs[:4], refs[4:]
    out_refs, refs = refs[:groups], refs[groups:]
    rows_ref, work_refs = refs[0], refs[1:]
    devices, _, freqs, _ = rows_ref.shape
    for j in range(groups):
        for i in range(spans):
            rows_ref[partner(place_ref, j, i, spans)] = in_refs[i][j]

    def read(v):
        return rows_ref[:, v].reshape(NF, 2 * NB)

    def write(w, part, piece):
        at = slice(part * NB, (part + 1) * NB)
        rows_ref[:, w, :, at] = piece.reshape(devices, freqs, NB)

    transform(read, write, q_ref, table_refs, *work_refs)
    for j in range(groups):
        for i in range(spans):
            out_refs[j][i] = rows_ref[partner(place_ref, j, i, spans)]


def nonlinear_apart(place, blocks, coefficients, transforms):
    spans = len(blocks)
    groups, variables, freqs, lanes = blocks[0].shape
    result = jax.ShapeDtypeStruct((spans, variables, freqs, lanes), jnp.float32)
    smem = pl.BlockSpec(memory_space=pltpu.SMEM)
    return pl.pallas_call(
        functools.partial(nonlinear_apart_body, groups, spans),
        grid=(1,),
        in_specs=[smem, smem]
        + [whole(block) for block in blocks]
        + [whole(table) for table in transforms],
        out_specs=[whole(result)] * groups,
        out_shape=[result] * groups,
        scratch_shapes=[pltpu.VMEM((groups * spans, variables, freqs, lanes), jnp.float32)]
        + work_shapes(variables),
        compiler_params=params(24),
        cost_estimate=pl.CostEstimate(flops=2 * 10**11, bytes_accessed=0, transcendentals=0),
        name="nonlinear_apart",
    )(place, coefficients, *blocks, *[in_hbm(table) for table in transforms])


def total(value):
    return jnp.sum(value, axis=0, keepdims=True)


def padded(rows, multiple):
    return rows + -rows % multiple


def edge_body(width, x_ref, mask_ref, rows_ref, out_ref):
    _, variables, heights, lanes = x_ref.shape
    keep = kept_modes(mask_ref)
    squares = 0.0
    out_ref[...] = jnp.zeros(out_ref.shape, jnp.float32)
    for part in range(2):
        kept = x_ref[part].reshape(variables * heights, lanes) * keep
        squares = squares + total(kept * kept)
        out_ref[part * width : (part + 1) * width] = table_times(rows_ref[...], kept)[:width]
    out_ref[2 * width : 2 * width + 1] = squares


def edge(amplitudes, keep, rows, width):
    _, variables, heights, modes = amplitudes.shape
    length = padded(2 * width + 1, 8)
    return pl.pallas_call(
        functools.partial(edge_body, width),
        grid=(modes // NB,),
        in_specs=[
            pl.BlockSpec((2, variables, heights, NB), lambda i: (0, 0, 0, i)),
            pl.BlockSpec((NB,), lambda i: (i,)),
            whole(rows),
        ],
        out_specs=pl.BlockSpec((length, NB), lambda i: (0, i)),
        out_shape=jax.ShapeDtypeStruct((length, modes), jnp.float32),
        compiler_params=params(),
        name="edge",
    )(in_hbm(amplitudes), keep, rows)


def base_body(cuts, walls, width, x_ref, up_ref, mask_ref, turned_ref, ahead_ref, back_ref, *refs):
    edges, refs = refs[:walls], refs[walls:]
    out_refs, (sum_ref, square_ref) = refs[: len(cuts)], refs[len(cuts) :]
    _, variables, heights, lanes = x_ref.shape
    extent = variables * heights
    pushes = walls * width
    spare = back_ref.shape[1] // 3 - pushes
    keep = kept_modes(mask_ref)
    moved, sides = [], []
    sum_ref[...] = jnp.zeros(sum_ref.shape, jnp.float32)
    for part in range(2):
        kept = x_ref[part].reshape(extent, lanes) * keep
        taken = [ref[part * width : (part + 1) * width] for ref in edges]
        if spare:
            taken.append(jnp.zeros((spare, lanes), jnp.float32))
        taken = jnp.concatenate(taken, axis=0)
        moved.append(table_times(turned_ref[...], kept) - table_times(back_ref[...], taken))
        grid = moved[part].reshape(variables, heights, lanes)
        for cut, out_ref in zip(cuts, out_refs):
            out_ref[part] = grid[:, cut]
        sides.append(up_ref[part].reshape(extent, lanes) * keep)
        added = table_times(ahead_ref[...], sides[part])
        sum_ref[part * pushes : (part + 1) * pushes] = added[:pushes]
    row = 2 * pushes
    sum_ref[row : row + 1] = total(moved[0] * sides[0] + moved[1] * sides[1])
    sum_ref[row + 1 : row + 2] = total(moved[0] * sides[1] - moved[1] * sides[0])
    squares = sum(ref[2 * width : 2 * width + 1] for ref in edges)
    square_ref[...] = jnp.broadcast_to(squares, square_ref.shape)


def base(amplitudes, upstream, keep, turned, ahead, back, edges, width, cuts):
    _, variables, heights, modes = amplitudes.shape
    walls = len(edges)
    lengths = [cut.stop - cut.start for cut in cuts]
    shapes = [(2, variables, rows, modes) for rows in lengths]
    sums = padded(2 * walls * width + 2, 8)
    spec = pl.BlockSpec((2, variables, heights, NB), lambda i: (0, 0, 0, i))

    def rows_spec(rows):
        return pl.BlockSpec((rows, NB), lambda i: (0, i))

    return pl.pallas_call(
        functools.partial(base_body, cuts, walls, width),
        grid=(modes // NB,),
        in_specs=[spec] * 2
        + [pl.BlockSpec((NB,), lambda i: (i,)), whole(turned), whole(ahead), whole(back)]
        + [rows_spec(part.shape[0]) for part in edges],
        out_specs=[
            pl.BlockSpec((2, variables, rows, NB), lambda i: (0, 0, 0, i)) for rows in lengths
        ]
        + [rows_spec(sums), rows_spec(8)],
        out_shape=[pltpu.HBM(shapes[0], jnp.float32)]
        + [jax.ShapeDtypeStruct(shape, jnp.float32) for shape in shapes[1:]]
        + [jax.ShapeDtypeStruct((rows, modes), jnp.float32) for rows in (sums, 8)],
        compiler_params=params(24),
        name="base",
    )(in_hbm(amplitudes), in_hbm(upstream), keep, turned, ahead, back, *edges)


def absorb_rows(width, read, mask_ref, ahead_ref, adj_ref, before_ref, out_ref, sum_ref, *send_refs):
    _, variables, rows, lanes = out_ref.shape
    pushes = ahead_ref.shape[1]
    keep = kept_modes(mask_ref)

    @pl.when(pl.program_id(0) == 0)
    def _():
        sum_ref[...] = before_ref[...]

    for v in range(variables):
        for part in range(2):
            out_ref[part, v] = read(v, part).reshape(rows, lanes) * keep
    sides = [out_ref[part].reshape(variables * rows, lanes) for part in range(2)]
    for part in range(2):
        sum_ref[part * pushes : (part + 1) * pushes] += jnp.dot(
            ahead_ref[0], sides[part], precision=SPLIT, preferred_element_type=jnp.float32
        )
    real, imag = (adj_ref[part].reshape(variables * rows, lanes) for part in range(2))
    at = 2 * pushes
    sum_ref[at : at + 1] += total(real * sides[0] + imag * sides[1])
    sum_ref[at + 1 : at + 2] += total(real * sides[1] - imag * sides[0])

    if send_refs:

        @pl.when(pl.program_id(0) == pl.num_programs(0) - 1)
        def _():
            for d, send_ref in enumerate(send_refs, 1):
                pieces = []
                for part in range(2):
                    at = part * pushes + d * width
                    pieces.append(sum_ref[at : at + width])
                pieces.append(sum_ref[2 * pushes : 2 * pushes + 2])
                pack_rows(send_ref, jnp.concatenate(pieces, axis=0))


def folded(rows, modes):
    return rows == 12 and modes % 256 == 0 and modes <= 8 * NB


def travelling(rows, modes):
    if folded(rows, modes):
        return jax.ShapeDtypeStruct((rows - 4, modes + modes // 2), jnp.float32)
    return jax.ShapeDtypeStruct((padded(rows, 8), modes), jnp.float32)


def pack_rows(out_ref, value):
    rows, modes = value.shape
    if folded(rows, modes):
        half = modes // 2
        out_ref[:, :modes] = value[: rows - 4]
        out_ref[:4, modes:] = value[rows - 4 :, :half]
        out_ref[4:8, modes:] = value[rows - 4 :, half:]
        return
    out_ref[:rows] = value
    if out_ref.shape[0] > rows:
        out_ref[rows:] = jnp.zeros((out_ref.shape[0] - rows, modes), jnp.float32)


def absorb_body(width, in_ref, *refs):
    def read(v, part):
        return in_ref[:, v, :, part * NB : (part + 1) * NB]

    absorb_rows(width, read, *refs)


def absorb_apart_body(width, spans, place_ref, *refs):
    in_refs, refs, rows_ref = refs[:spans], refs[spans:-1], refs[-1]
    for i, in_ref in enumerate(in_refs):
        for j in range(in_ref.shape[0]):
            rows_ref[partner(place_ref, j, i, spans)] = in_ref[j]

    def read(v, part):
        return rows_ref[:, v, :, part * NB : (part + 1) * NB]

    absorb_rows(width, read, *refs)


def absorb(place, blocks, keep, ahead, adjoint_modes, before, width, sends):
    blocks = list(blocks)
    apart = place is not None
    _, variables, rows, modes = adjoint_modes.shape
    steps, pushes, depth = ahead.shape
    step = rows // steps
    grid_spec = pl.BlockSpec((2, variables, step, modes), lambda r: (0, 0, r, 0))
    _, _, freqs, lanes = blocks[0].shape
    sent = travelling(2 * width + 2, modes)
    operands = blocks + [keep, ahead, adjoint_modes if apart else in_hbm(adjoint_modes), before]
    in_specs = [
        whole(block)
        if apart
        else pl.BlockSpec((step, variables, freqs, lanes), lambda r: (r, 0, 0, 0))
        for block in blocks
    ] + [
        pl.BlockSpec((modes,), lambda r: (0,)),
        pl.BlockSpec((1, pushes, depth), lambda r: (r, 0, 0)),
        grid_spec,
        whole(before),
    ]
    body, scratch = functools.partial(absorb_body, width), []
    if apart:
        operands = [place] + operands
        in_specs = [pl.BlockSpec(memory_space=pltpu.SMEM)] + in_specs
        body = functools.partial(absorb_apart_body, width, len(blocks))
        scratch = [pltpu.VMEM((rows, variables, freqs, lanes), jnp.float32)]
    return pl.pallas_call(
        body,
        grid=(steps,),
        in_specs=in_specs,
        out_specs=[grid_spec, whole(before)] + [whole(sent)] * sends,
        out_shape=[
            jax.ShapeDtypeStruct((2, variables, rows, modes), jnp.float32),
            jax.ShapeDtypeStruct(before.shape, jnp.float32),
        ]
        + [sent] * sends,
        scratch_shapes=scratch,
        compiler_params=params(24),
        name="absorb_apart" if apart else "absorb",
    )(*operands)


def solve_body(side_ref, up_ref, mask_ref, inverse_ref, out_ref):
    _, variables, heights, lanes = out_ref.shape
    keep = kept_modes(mask_ref)
    spare = heights - side_ref.shape[2]
    for part in range(2):
        forced = side_ref[part]
        if spare:
            none = jnp.zeros((variables, spare, lanes), jnp.float32)
            forced = jnp.concatenate([forced, none], axis=1)
        side = (forced + up_ref[part] * keep).reshape(variables * heights, lanes)
        out_ref[part] = table_times(inverse_ref[...], side).reshape(variables, heights, lanes)


def solve(side, upstream, keep, inverse):
    _, variables, heights, modes = upstream.shape
    lanes = min(4 * NB, modes)
    spec = pl.BlockSpec((2, variables, heights, lanes), lambda i: (0, 0, 0, i))
    return pl.pallas_call(
        solve_body,
        grid=(modes // lanes,),
        in_specs=[
            pl.BlockSpec((2, variables, side.shape[2], lanes), lambda i: (0, 0, 0, i)),
            spec,
            pl.BlockSpec((lanes,), lambda i: (i,)),
            whole(inverse),
        ],
        out_specs=spec,
        out_shape=jax.ShapeDtypeStruct(upstream.shape, jnp.float32),
        compiler_params=params(32),
        name="solve",
    )(side, in_hbm(upstream), keep, inverse)


def solve_more_body(side_ref, before_ref, inverse_ref, out_ref):
    _, variables, heights, lanes = out_ref.shape
    for part in range(2):
        moved = table_times(inverse_ref[...], side_ref[part].reshape(-1, lanes))
        out_ref[part] = before_ref[part] + moved.reshape(variables, heights, lanes)


def solve_more(side, before, inverse):
    _, variables, rows, modes = side.shape
    lanes = min(4 * NB, modes)
    spec = pl.BlockSpec(before.shape[:3] + (lanes,), lambda i: (0, 0, 0, i))
    return pl.pallas_call(
        solve_more_body,
        grid=(modes // lanes,),
        in_specs=[
            pl.BlockSpec((2, variables, rows, lanes), lambda i: (0, 0, 0, i)),
            spec,
            whole(inverse),
        ],
        out_specs=spec,
        out_shape=jax.ShapeDtypeStruct(before.shape, jnp.float32),
        compiler_params=params(32),
        name="solve_more",
    )(side, before, inverse)


def finish_body(walls, width, fold, solved_ref, sum_ref, square_ref, *refs):
    each = 2 if fold else 1
    other_refs, (columns_ref, out_ref, shift_ref) = refs[: each * (walls - 1)], refs[-3:]
    _, variables, heights, lanes = out_ref.shape
    spare = columns_ref.shape[1] // 3 - width
    pushes = walls * width
    others = [ref[...] for ref in other_refs]
    if fold:
        first = pl.program_id(0) == 0
        others = [
            jnp.concatenate([rows, jnp.where(first, rest[:4], rest[4:8])], axis=0)
            for rows, rest in zip(others[::2], others[1::2])
        ]
    for part in range(2):
        push = sum_ref[part * pushes : part * pushes + width]
        for other in others:
            push = push + other[part * width : (part + 1) * width]
        if spare:
            push = jnp.concatenate([push, jnp.zeros((spare, lanes), jnp.float32)], axis=0)
        moved = table_times(columns_ref[...], push)
        out_ref[part] = solved_ref[part] - moved.reshape(variables, heights, lanes)
    both = sum_ref[2 * pushes : 2 * pushes + 2]
    for other in others:
        both = both + other[2 * width : 2 * width + 2]
    squares = square_ref[:1]
    weight = squares + epsilon
    shift_ref[0:1] = both[1:2] / weight
    shift_ref[1:2] = (squares - both[0:1]) / weight


def finish(solved, sums, squares, others, columns, width):
    _, variables, heights, modes = solved.shape
    fold = folded(2 * width + 2, modes)
    lanes = modes // 2 if fold else min(4 * NB, modes)

    def rows_spec(rows):
        return pl.BlockSpec((rows, lanes), lambda i: (0, i))

    spec = pl.BlockSpec((2, variables, heights, lanes), lambda i: (0, 0, 0, i))
    operands, in_specs = [solved, sums, squares], [spec]
    in_specs += [rows_spec(part.shape[0]) for part in (sums, squares)]
    for part in others:
        operands.append(part)
        in_specs.append(rows_spec(part.shape[0]))
        if fold:
            operands.append(part)
            in_specs.append(pl.BlockSpec((8, lanes), lambda i: (0, 2)))
    return pl.pallas_call(
        functools.partial(finish_body, len(others) + 1, width, fold),
        grid=(modes // lanes,),
        in_specs=in_specs + [whole(columns)],
        out_specs=[spec, pl.BlockSpec((2, lanes), lambda i: (0, i))],
        out_shape=[
            jax.ShapeDtypeStruct(solved.shape, jnp.float32),
            jax.ShapeDtypeStruct((2, modes), jnp.float32),
        ],
        compiler_params=params(32),
        name="finish",
    )(*operands, columns)


def around(block, axis):
    count = lax.axis_size(axis)
    return [block] + [
        lax.ppermute(block, axis, [(i, (i + d) % count) for i in range(count)])
        for d in range(1, count)
    ]


def hand_back(blocks, axis):
    count = lax.axis_size(axis)
    return [
        lax.ppermute(block, axis, [(i, (i - d) % count) for i in range(count)])
        for d, block in enumerate(blocks, 1)
    ]


PACKED_ROWS = 16


def pack_body(*refs):
    in_refs, out_ref = refs[:-1], refs[-1]
    out_ref[...] = jnp.zeros(out_ref.shape, jnp.float32)
    for i, ref in enumerate(in_refs):
        rows, columns = ref.shape[1:]
        out_ref[i, :rows, :columns] = ref[0]


def pack(parts):
    return pl.pallas_call(
        pack_body,
        out_shape=jax.ShapeDtypeStruct((len(parts), PACKED_ROWS, 128), jnp.float32),
        name="pack",
    )(*parts)


def upper_bits(value):
    return value.astype(jnp.bfloat16).astype(jnp.float32)


def split_columns(matrix):
    high = upper_bits(matrix)
    return jnp.concatenate([high, high, matrix - high], axis=1).astype(jnp.bfloat16)


def push_width(walls, variables):
    return variables if walls == 2 else 2 * variables


def constants_body(cuts, variables, walls, place_ref, inverse_ref, *refs):
    packed, refs = refs[:walls], refs[walls:]
    turned_ref, split_ref, last_ref, column_ref, edge_ref, ahead_ref, back_ref = refs[:7]
    row_refs, (all_ref, step_ref) = refs[7 : 7 + len(cuts)], refs[7 + len(cuts) :]
    extent = inverse_ref.shape[0]
    heights = extent // variables
    ends = 2 * variables
    width = push_width(walls, variables)
    matrix = inverse_ref[...]
    turned = matrix.T
    turned_ref[...] = split_columns(turned)
    split_ref[...] = split_columns(matrix)
    cut = cuts[-1]
    last = [matrix[:, v * heights : (v + 1) * heights][:, cut] for v in range(variables)]
    last_ref[...] = split_columns(jnp.concatenate(last, axis=1))

    def dot(a, b):
        return jnp.dot(a, b, precision=FULL, preferred_element_type=jnp.float32)

    def ends_of(value):
        low = [value[v * heights : v * heights + 1] for v in range(variables)]
        high = [value[(v + 1) * heights - 1 : (v + 1) * heights] for v in range(variables)]
        return jnp.concatenate(low, axis=0), jnp.concatenate(high, axis=0)

    def extended(value, rows):
        spare = rows - value.shape[0]
        if not spare:
            return value
        return jnp.concatenate([value, jnp.zeros((spare, value.shape[1]), jnp.float32)], axis=0)

    size = walls * PACKED_ROWS
    for d in range(walls):
        all_ref[(place_ref[0] - d + walls) % walls] = packed[d][...]

    def small(j, kind):
        return all_ref[j, kind][:, :PACKED_ROWS]

    row = lax.broadcasted_iota(jnp.int32, (PACKED_ROWS, size), 0)
    column = lax.broadcasted_iota(jnp.int32, (PACKED_ROWS, size), 1)
    units = []
    for j in range(walls):
        d = (place_ref[0] - j + walls) % walls
        hit = (column == d * ends + row) & (row < ends)
        units.append(jnp.where(hit, 1.0, 0.0))
    ahead = [units[0]]
    for j in range(1, walls):
        ahead.append(units[j] - dot(small(j, 2), ahead[j - 1]))
    interface = [None] * walls
    interface[-1] = dot(small(walls - 1, 4), ahead[-1])
    for j in range(walls - 2, -1, -1):
        interface[j] = dot(small(j, 4), ahead[j] - dot(small(j, 3), interface[j + 1]))
    none = jnp.zeros((variables, size), jnp.float32)
    for j in range(walls):
        under, over = none, none
        if j > 0:
            lower = extended(interface[j - 1][variables:], PACKED_ROWS)
            under = dot(small(j, 0), lower)[:variables]
        if j < walls - 1:
            over = dot(small(j, 1), interface[j + 1])[:variables]
        push = under + over if walls == 2 else jnp.concatenate([under, over], axis=0)
        step_ref[(place_ref[0] - j + walls) % walls] = extended(push, PACKED_ROWS)

    low, high = ends_of(matrix)
    bounds = extended(jnp.concatenate([low, high], axis=0), PACKED_ROWS)
    steps = [step_ref[d][:width, :PACKED_ROWS] for d in range(walls)]
    steps = [jnp.where(column[:width, :PACKED_ROWS] < ends, step, 0.0) for step in steps]
    pushes = dot(jnp.concatenate(steps, axis=0), bounds)
    for cut, row_ref in zip(cuts, row_refs):
        step = row_step(cut.stop - cut.start)
        for r in range(row_ref.shape[0]):
            at = cut.start + r * step
            pieces = [pushes[:, v * heights + at : v * heights + at + step] for v in range(variables)]
            row_ref[r] = jnp.concatenate(pieces, axis=1)
    pushes = extended(pushes, ahead_ref.shape[0])
    ahead_ref[...] = split_columns(pushes)
    back_ref[...] = split_columns(pushes.T)
    low, high = ends_of(turned)
    edge = jnp.concatenate([low, high], axis=0)
    if walls == 2:
        edge = jnp.where(place_ref[0] == 0, high, low)
    edge = extended(edge, edge_ref.shape[0])
    edge_ref[...] = split_columns(edge)
    column_ref[...] = split_columns(edge.T)


def constants(place, inverse, packed, cuts, variables):
    walls = len(packed)
    extent = inverse.shape[0]
    width = push_width(walls, variables)
    lengths = [cut.stop - cut.start for cut in cuts]
    size = walls * PACKED_ROWS
    pushes, edge_rows = padded(walls * width, 16), padded(width, 16)

    def split_shape(rows, columns):
        return jax.ShapeDtypeStruct((rows, 3 * columns), jnp.bfloat16)

    return pl.pallas_call(
        functools.partial(constants_body, cuts, variables, walls),
        in_specs=[pl.BlockSpec(memory_space=pltpu.SMEM)]
        + [pl.BlockSpec(memory_space=pltpu.VMEM)] * (1 + walls),
        out_shape=[
            split_shape(extent, extent),
            split_shape(extent, extent),
            split_shape(extent, variables * lengths[-1]),
            split_shape(extent, edge_rows),
            split_shape(edge_rows, extent),
            split_shape(pushes, extent),
            split_shape(extent, pushes),
        ]
        + [
            jax.ShapeDtypeStruct(
                (n // row_step(n), walls * width, variables * row_step(n)), jnp.float32
            )
            for n in lengths
        ],
        scratch_shapes=[
            pltpu.VMEM((walls,) + packed[0].shape, jnp.float32),
            pltpu.VMEM((walls, PACKED_ROWS, size), jnp.float32),
        ],
        compiler_params=params(),
        name="constants",
    )(place, inverse, *packed)


def local(
    amplitudes,
    upstream,
    harmonic_mask,
    quadratic_coefficients,
    slab_inverse,
    lower_coupling,
    upper_coupling,
    reduced_lower,
    reduced_upper,
    reduced_pivot,
):
    _, variables, heights, modes = amplitudes.shape
    axes = ("freq", "span")
    groups, spans = lax.axis_size("freq"), lax.axis_size("span")
    devices = groups * spans
    points = heights // devices
    apart = points > 1 and groups & (groups - 1) == 0 and spans & (spans - 1) == 0
    edge_at = heights - devices if apart else heights
    cuts = [slice(0, edge_at)] + ([slice(edge_at, heights)] if apart else [])
    keep = harmonic_mask
    place = jnp.stack([lax.axis_index("freq"), lax.axis_index("span")]).astype(jnp.int32)
    wall = lax.axis_index("wall").reshape(1).astype(jnp.int32)
    transforms = tables()
    coefficients = quadratic_coefficients.reshape(variables * variables, variables)

    def exchange(block):
        return lax.all_to_all(block, axes, split_axis=0, concat_axis=0, tiled=True)

    def swap(blocks, axis):
        count = len(blocks)
        return [blocks[0]] + [
            lax.ppermute(blocks[i], axis, [(at, at ^ i) for at in range(count)])
            for i in range(1, count)
        ]

    def regroup(blocks):
        return [jnp.stack([block[j] for block in blocks]) for j in range(blocks[0].shape[0])]

    main = prepare(amplitudes, keep, cuts[0])
    if apart:
        main, amplitudes = lax.optimization_barrier((main, amplitudes))
        sent = prepare_apart(place, amplitudes, keep, cuts[1], groups, spans)
        arrived = regroup(swap(sent, "freq"))
        moved = swap(arrived, "span")
        moved[1], held = lax.optimization_barrier((moved[1], amplitudes))
    main = exchange(main)

    inverse = slab_inverse[0]
    parts = (lower_coupling, upper_coupling, reduced_lower, reduced_upper, reduced_pivot)
    packed = around(pack(parts), "wall")
    turned, split, last, edge_columns, edge_rows, ahead, back, *rows = constants(
        wall, inverse, packed, cuts, variables
    )
    walls = len(packed)
    width = push_width(walls, variables)
    edges = edge(held if apart else amplitudes, keep, edge_rows, width)
    edges = around(edges, "wall")
    *adjoint_modes, sums, squares = base(
        amplitudes, upstream, keep, turned, ahead, back, edges, width, cuts
    )
    size = edge_at // devices
    shape = main.shape
    main = nonlinear(main.reshape((devices, size) + shape[1:]), coefficients, transforms)
    main = main.reshape(shape)
    main = exchange(main)
    if apart:
        last_one = spans - 1
        sums, arrived[last_one] = lax.optimization_barrier((sums, arrived[last_one]))
        moved[last_one] = swap(arrived, "span")[last_one]
        arrived = moved
        forced = nonlinear_apart(place, arrived, coefficients, transforms)
        returned = regroup(swap(forced, "freq"))
        returned = swap(returned, "span")

    sends = walls - 1
    side, sums, *sent = absorb(
        None, [main], keep, rows[0], adjoint_modes[0], sums, width, 0 if apart else sends
    )
    solved = solve(side, upstream, keep, split)
    if apart:
        solved, sums = lax.optimization_barrier((solved, sums))
        side, sums, *sent = absorb(
            place, returned, keep, rows[1], adjoint_modes[1], sums, width, sends
        )
    others = hand_back(sent, "wall")
    if apart:
        solved = solve_more(side, solved, last)
    new_amplitudes, wavenumber_shift = finish(solved, sums, squares, others, edge_columns, width)
    return (new_amplitudes, wavenumber_shift)


def solution(mesh):
    placed = (
        P(None, None, "wall", ("freq", "span")),
        P(None, None, "wall", ("freq", "span")),
        P(("freq", "span")),
        P(),
        P("wall", None, None),
        P("wall", None, None),
        P("wall", None, None),
        P("wall", None, None),
        P("wall", None, None),
        P("wall", None, None),
    )
    return jax.shard_map(
        local,
        mesh=mesh,
        in_specs=placed,
        out_specs=(P(None, None, "wall", ("freq", "span")), P(None, ("freq", "span"))),
        check_vma=False,
    )
```
